32 devices in a mesh: ang: 8 (over y, x, core), hgt: 4 (over z).
Axes of the slice: x: 2, y: 2, z: 4, core: 2. Of those that a mesh axis runs over, the one named last changes fastest.
Arguments:
- loads: float32 [4, 3, 256, 32, 128], P(None, None, 'ang', 'hgt'), may hold values from -6 to 6
- material: int32 [256, 32, 128], P('ang', 'hgt'), may hold values from 0 to 7
- support: int32 [256, 32, 128], P('ang', 'hgt'), may hold values 0 or 1
- modulus: float32 [8], replicated, may hold values from 0.5 to 5
- positions: int32 [4], replicated, may hold values from 0 to 255
Outputs:
- solution_field: float32 [4, 3, 256, 32, 128], P(None, None, 'ang', 'hgt')
- residual: float32 [4, 3, 256, 32, 128], P(None, None, 'ang', 'hgt')
The draws below stay inside these ranges and needn't reach their ends.
All inputs are finite; a program needn't handle non-finite values. No bound on the sum of `support` on one device may be relied on, other than what follows from the above.
Results may differ from the reference program's by a relative error of at most 0.0003.
Values sent between devices are 32-bit elements; how exact they have to be, the bound alone decides.
No kernel may reach another device: no remote copies, remote signals or barrier semaphores. Data moves between devices by JAX's collectives and lax.ppermute only.
A program may use at most 64 MiB of HBM per device.

```python
import math
import jax
import jax.numpy as jnp
from jax import lax

CASES = 4
COMPS = 3
RAD = 128
NMAT = 8
ITERS = 3
CSWEEPS = 4
ANG = 256
HGT = 32
BAND = 32


def place_ends(values, rng, least, top_value):
    extent = values.shape
    spot = [jax.random.randint(jax.random.fold_in(rng, axis), (), 0, extent[axis]) for axis in range(len(extent))]
    values = values.at[tuple(spot)].set(least)
    longest = extent.index(max(extent))
    spot[longest] = (spot[longest] + 1) % extent[longest]
    return values.at[tuple(spot)].set(top_value)


def shard_levels(stream_key, dims, split, low, top_value):
    def one(axis_at, blocks):
        draws = jax.random.uniform(jax.random.fold_in(jax.random.fold_in(stream_key, 6), axis_at), (blocks,), jnp.float32, low / len(split), top_value / len(split))
        return jnp.repeat(jnp.exp(draws), dims[axis_at] // blocks).reshape((-1,) + (1,) * (len(dims) - axis_at - 1))

    factor_of = one(*split[0])
    for cut in split[1:]:
        factor_of = factor_of * one(*cut)
    return factor_of


def normal_values(own_key, extent, spread, bound, shards=(), kind=jnp.bfloat16):
    drawn = spread * jax.random.normal(own_key, extent, jnp.float32)
    if shards:
        drawn = drawn * shard_levels(own_key, extent, shards, -0.22, 0.18)
    return jnp.clip(drawn, -bound, bound).astype(kind)


def setup_inputs(seed: int = 0) -> dict:
    arg_keys = jax.random.split(jax.random.key(seed), 6)
    loads = normal_values(arg_keys[0], (CASES, COMPS, ANG, HGT, RAD), 1.0, 6.0, ((2, 8), (3, 4)), jnp.float32)
    material = place_ends(jax.random.randint(arg_keys[1], (ANG, HGT, RAD), 0, NMAT), jax.random.fold_in(arg_keys[1], 1), 0, NMAT - 1).astype(jnp.int32)
    support = place_ends((jax.random.randint(arg_keys[2], (ANG, HGT, RAD), 0, 8) < 1).astype(jnp.int32), jax.random.fold_in(arg_keys[2], 1), 0, 1)
    modulus = jnp.clip(jnp.exp(jax.random.uniform(arg_keys[3], (NMAT,), jnp.float32, math.log(0.5), math.log(5.0))), 0.5, 5.0)
    positions = place_ends(jax.random.randint(arg_keys[4], (CASES,), 0, ANG), jax.random.fold_in(arg_keys[4], 1), 0, ANG - 1).astype(jnp.int32)
    return dict(loads=loads, material=material, support=support, modulus=modulus, positions=positions)


SIGMA = 6.5
SPRING = 20.0
OMEGA = 0.8
LOAD = 3.0

def zero_pair(v, axis):
    widths = [(0, 0)] * v.ndim
    widths[axis] = (1, 1)
    padded = jnp.pad(v, widths)
    size = v.shape[axis]
    return lax.slice_in_dim(padded, 2, size + 2, axis=axis) + lax.slice_in_dim(padded, 0, size, axis=axis)

def apply_op(u, weight, spring):
    v = weight * u
    beside = jnp.roll(v, 1, axis=2) + jnp.roll(v, -1, axis=2)
    beside = beside + zero_pair(v, 3) + zero_pair(v, 4)
    return weight * (SIGMA * v - beside) + SPRING * spring * u

def coarsen(field):
    a, h, r = field.shape
    return field.reshape(a // 2, 2, h // 2, 2, r).mean(axis=(1, 3))

def restrict(r):
    c, k, a, h, n = r.shape
    return r.reshape(c, k, a // 2, 2, h // 2, 2, n).sum(axis=(3, 5)) * 0.5

def prolong(e):
    return jnp.repeat(jnp.repeat(e, 2, axis=2), 2, axis=3) * 0.5

def reference(loads, material, support, modulus, positions):
    levels = jnp.arange(NMAT, dtype=jnp.int32)
    stiff = lax.optimization_barrier(jnp.sum(jnp.where(material[None] == levels[:, None, None, None], modulus[:, None, None, None], 0.0), axis=0))
    weight = jnp.sqrt(stiff)
    spring = support.astype(jnp.float32)
    diag = SIGMA * weight * weight + SPRING * spring
    wide_c = coarsen(weight)
    spring_c = coarsen(spring)
    diag_c = SIGMA * wide_c * wide_c + SPRING * spring_c
    angles = jnp.arange(ANG, dtype=jnp.int32)
    apart = jnp.abs(angles[None, :] - positions[:, None])
    cycle_dist = jnp.minimum(apart, ANG - apart)
    hit = jnp.where(cycle_dist < BAND, -LOAD, 0.0)
    select = jnp.where(jnp.arange(COMPS, dtype=jnp.int32) == 2, 1.0, 0.0)
    right = loads + hit[:, None, :, None, None] * select[None, :, None, None, None]

    def precondition(r):
        coarse_rhs = restrict(r)
        err = OMEGA * coarse_rhs / diag_c
        for sweep in range(CSWEEPS - 1):
            err = err + OMEGA * (coarse_rhs - apply_op(err, wide_c, spring_c)) / diag_c
        return OMEGA * r / diag + prolong(err)

    def column_sum(a, b):
        return lax.optimization_barrier(jnp.sum(a * b, axis=(2, 3, 4)))[:, :, None, None, None]
    solution_field = jnp.zeros_like(right)
    residual = right
    precond = precondition(residual)
    direction = precond
    rz_now = column_sum(residual, precond)
    for step in range(ITERS):
        image = apply_op(direction, weight, spring)
        alpha = rz_now / column_sum(direction, image)
        solution_field = solution_field + alpha * direction
        residual = residual - alpha * image
        if step + 1 < ITERS:
            precond = precondition(residual)
            rz_next = column_sum(residual, precond)
            direction = precond + rz_next / rz_now * direction
            rz_now = rz_next
    return (solution_field, residual)
```

```python
import functools

import jax
import jax.numpy as jnp
from jax import lax
from jax.experimental import pallas as pl
from jax.experimental.pallas import tpu as pltpu
from jax.sharding import PartitionSpec as P

ITERS = 3
CSWEEPS = 4


SIGMA = 6.5
SPRING = 20.0
OMEGA = 0.8
LOAD = 3.0
SHIFT = 1.0
PAD = 8


def call(kernel, out_shape, *args, smem=(), **scratch):
    vmem = pl.BlockSpec(memory_space=pltpu.VMEM)
    scalar = pl.BlockSpec(memory_space=pltpu.SMEM)
    single = not isinstance(out_shape, (list, tuple))
    return pl.pallas_call(
        kernel,
        out_shape=out_shape,
        in_specs=[scalar if i in smem else vmem for i in range(len(args))],
        out_specs=vmem if single else [vmem] * len(out_shape),
        scratch_shapes=list(scratch.values()),
        compiler_params=pltpu.CompilerParams(vmem_limit_bytes=40 * 1024 * 1024),
    )(*args)


def f32(*shape):
    return jax.ShapeDtypeStruct(shape, jnp.float32)


def radial_pair(v):
    lane = lax.broadcasted_iota(jnp.int32, v.shape, 1)
    last = v.shape[1] - 1
    inner = jnp.where(lane == 0, 0.0, pltpu.roll(v, 1, 1))
    return inner + jnp.where(lane == last, 0.0, pltpu.roll(v, last, 1))


def corner_pieces(margin, own):
    pieces = [(margin + k, margin) for k in range(own)]
    for d in range(1, margin):
        pieces += [(margin - d, margin - d), (margin + own - 1 + d, margin - d)]
    return pieces


def write_faces(c, u, q, parity_h, msg_a, msg_b, beside, coarse_rows):
    height, angles, _ = u.shape[1:]
    rows = pl.ds(coarse_rows, angles)
    top = q[height - 1] * u[c, height - 1]
    bottom = q[0] * u[c, 0]
    even = parity_h == 0
    msg_a[c, rows, :] = jnp.where(even, top, bottom)
    msg_b[c, rows, :] = jnp.where(even, bottom, top)
    for h in range(height):
        slot = h // 2 + (height // 2) * (h % 2)
        for side, a in ((0, 0), (1, angles - 1)):
            beside[c, pl.ds(side * height + slot, 1), :] = q[h, pl.ds(a, 1), :] * u[c, h, pl.ds(a, 1), :]


def restrict_column(c, u, weight, pre, pair, msg_a, msg_b):
    height, angles, _ = u.shape[1:]
    half = angles // 2
    for k in range(height // 2):
        pair[k] = weight[2 * k] * u[c, 2 * k] + weight[2 * k + 1] * u[c, 2 * k + 1]
        g = pre[k] * (pair[k, pl.ds(0, half, stride=2), :] + pair[k, pl.ds(1, half, stride=2), :])
        msg_a[c, pl.ds(k * half, half), :] = g
        msg_b[c, pl.ds(k * half, half), :] = g


def prepare(cases, comps, levels, loads, hit, material, support, modulus, parity,
            u, msg_a, msg_b, beside, delta, q, beta, weight, winv, pre, kappa, mat, sup, pair):
    columns, height, angles, radial = u.shape
    half = angles // 2
    parity_h = parity[0]
    for h in range(height):
        rows = pl.ds(h, angles, stride=height)
        level = material[rows, :]
        stiff = jnp.zeros(level.shape, jnp.float32)
        for n in range(levels):
            stiff = jnp.where(level == n, modulus[n], stiff)
        w = jnp.sqrt(stiff)
        s = support[rows, :].astype(jnp.float32)
        d = SIGMA + SPRING * s / (w * w)
        weight[h] = w
        winv[h] = 1.0 / w
        delta[h] = d
        q[h] = OMEGA / d
        sup[h] = s
    for k in range(height // 2):
        pair[k] = weight[2 * k] + weight[2 * k + 1]
        wc = 0.25 * (pair[k, pl.ds(0, half, stride=2), :] + pair[k, pl.ds(1, half, stride=2), :])
        pair[k] = sup[2 * k] + sup[2 * k + 1]
        sc = 0.25 * (pair[k, pl.ds(0, half, stride=2), :] + pair[k, pl.ds(1, half, stride=2), :])
        dc = SIGMA * wc * wc + SPRING * sc
        pre[k] = 0.5 * OMEGA * wc / dc
        kap = OMEGA * wc * wc / dc
        kappa[k] = kap
        msg_a[columns, pl.ds(k * half, half), :] = kap
        msg_b[columns, pl.ds(k * half, half), :] = kap
        inv = 0.5 / wc
        mat[pl.ds(0, half, stride=2), :] = inv
        mat[pl.ds(1, half, stride=2), :] = inv
        beta[2 * k] = mat[...] * weight[2 * k]
        beta[2 * k + 1] = mat[...] * weight[2 * k + 1]
    coarse_rows = half * (height // 2)
    even = parity_h == 0
    msg_a[columns, pl.ds(coarse_rows, angles), :] = jnp.where(even, beta[height - 1], beta[0])
    msg_b[columns, pl.ds(coarse_rows, angles), :] = jnp.where(even, beta[0], beta[height - 1])
    for h in range(height):
        slot = h // 2 + (height // 2) * (h % 2)
        for side, a in ((0, 0), (1, angles - 1)):
            beside[columns, pl.ds(side * height + slot, 1), :] = beta[h, pl.ds(a, 1), :]

    @pl.loop(0, columns)
    def _(c):
        extra = jnp.where(lax.rem(c, comps) == 2, 1.0, 0.0)
        push = hit[lax.div(c, comps)] * extra
        for h in range(height):
            u[c, h] = winv[h] * (loads[c, pl.ds(h, angles, stride=height), :] + push)
        restrict_column(c, u, weight, pre, pair, msg_a, msg_b)
        write_faces(c, u, q, parity_h, msg_a, msg_b, beside, coarse_rows)


def beside_messages(margin, own, half, parity, sent, from_a, from_b, beside, out_a, out_b):
    columns = out_a.shape[0]
    height = beside.shape[1] // 2
    pieces = corner_pieces(margin, own)

    def build(up, down, low, high):
        @pl.loop(0, columns)
        def _(c):
            at = 0
            for h, count in pieces:
                if h < margin:
                    source, k = down, own - margin + h
                elif h < margin + own:
                    source, k = sent, h - margin
                else:
                    source, k = up, h - margin - own
                low[c, pl.ds(at, count), :] = source[c, pl.ds(k * half, count), :]
                high[c, pl.ds(at, count), :] = source[c, pl.ds(k * half + half - count, count), :]
                at += count
            low[c, pl.ds(at, height), :] = beside[c, pl.ds(0, height), :]
            high[c, pl.ds(at, height), :] = beside[c, pl.ds(height, height), :]

    for ph in range(2):
        for pa in range(2):
            @pl.when((parity[0] == ph) & (parity[1] == pa))
            def _(ph=ph, pa=pa):
                up, down = (from_a, from_b) if ph == 0 else (from_b, from_a)
                high, low = (out_a, out_b) if pa == 0 else (out_b, out_a)
                build(up, down, low, high)


def assemble(c, field, margin, own, half, parity, sent, up_down, beside_ab, edge):
    from_a, from_b = up_down
    side_a, side_b = beside_ab
    ang0 = PAD + margin
    coarse_rows = own * half
    for k in range(own):
        field[margin + k, pl.ds(ang0, half), :] = sent[c, pl.ds(k * half, half), :]

    def heights(up, down):
        for k in range(margin):
            field[margin + own + k, pl.ds(ang0, half), :] = up[c, pl.ds(k * half, half), :]
            field[k, pl.ds(ang0, half), :] = down[c, pl.ds((own - margin + k) * half, half), :]
        if edge is not None:
            edge[0] = down[c, pl.ds(coarse_rows, 2 * half), :]
            edge[1] = up[c, pl.ds(coarse_rows, 2 * half), :]

    def angles(low, high):
        at = 0
        for h, count in corner_pieces(margin, own):
            field[h, pl.ds(ang0 - count, count), :] = low[c, pl.ds(at, count), :]
            field[h, pl.ds(ang0 + half, count), :] = high[c, pl.ds(at, count), :]
            at += count

    for par in range(2):
        @pl.when(parity[0] == par)
        def _(par=par):
            heights(*((from_a, from_b) if par == 0 else (from_b, from_a)))

        @pl.when(parity[1] == par)
        def _(par=par):
            angles(*((side_b, side_a) if par == 0 else (side_a, side_b)))


def apply_step(margin, own, half, first, last, dot_at, *refs):
    refs = list(refs)
    take = lambda n: [refs.pop(0) for _ in range(n)]
    u, sent, from_a, from_b, side_a, side_b, dots_in, parity = take(8)
    delta, q, beta, weight, pre = take(5)
    if first:
        sent_c, from_ac, from_bc, side_ac, side_bc = sent, from_a, from_b, side_a, side_b
        w, un = take(2)
        kx, edge_b, side_face = take(3)
    else:
        kx_in, edge_b, side_face = take(3)
        kx = kx_in
        w, un = take(2)
    if not last:
        msg_a, msg_b, beside = take(3)
    dots, = take(1)
    gx, va, vb, ex, zx, edge, pair = take(7)
    columns, height, angles, radial = u.shape
    parity_h = parity[0]
    ext = half + 2 * margin
    body = pl.ds(PAD, ext)
    coarse_rows = own * half
    face_at = sum(count for _, count in corner_pieces(margin, own))
    ends = ((PAD - 1, 2 * margin - 1), (PAD + angles, 2 * margin + angles))

    if first:
        assemble(columns, gx, margin, own, half, parity, sent, (from_a, from_b), (side_a, side_b), edge_b)
        for h in range(own + 2 * margin):
            kx[h] = gx[h, body, :]
        for par in range(2):
            @pl.when(parity[1] == par)
            def _(par=par):
                low, high = (side_b, side_a) if par == 0 else (side_a, side_b)
                side_face[0] = low[columns, pl.ds(face_at, height), :]
                side_face[1] = high[columns, pl.ds(face_at, height), :]

    @pl.loop(0, columns)
    def _(c):
        assemble(c, gx, margin, own, half, parity, sent, (from_a, from_b), (side_a, side_b), edge)
        source, target = gx, va
        for sweep in range(1, CSWEEPS):
            lo, hi = sweep, own + 2 * margin - sweep
            below, here = source[lo - 1, body, :], source[lo, body, :]
            for h in range(lo, hi):
                above = source[h + 1, body, :]
                near = below + above + source[h, pl.ds(PAD - 1, ext), :] + source[h, pl.ds(PAD + 1, ext), :]
                near = near + radial_pair(here)
                target[h, body, :] = gx[h, body, :] + (1.0 - OMEGA) * here + kx[h] * near
                below, here = here, above
            source, target = target, (vb if target is va else va)
        for h in range(own + 2):
            e = source[margin - 1 + h, body, :]
            ex[h, pl.ds(0, ext, stride=2), :] = e
            ex[h, pl.ds(1, ext, stride=2), :] = e
        inner = pl.ds(2 * margin, angles)
        line = pl.ds(PAD, angles)
        dot_uw = jnp.zeros((angles, radial), jnp.float32)
        for h in range(height):
            z = q[h] * u[c, h] + beta[h] * ex[1 + h // 2, inner, :]
            zx[h + 1, line, :] = z
            w[c, h] = z
            dot_uw = dot_uw + u[c, h] * z
        zx[0, line, :] = edge[0] + edge_b[0] * ex[0, inner, :]
        zx[height + 1, line, :] = edge[1] + edge_b[1] * ex[own + 1, inner, :]
        for par in range(2):
            @pl.when(parity[1] == par)
            def _(par=par):
                sides = (side_b, side_a) if par == 0 else (side_a, side_b)
                for s in range(2):
                    put, get = ends[s]
                    for h in range(height):
                        slot = h // 2 + (height // 2) * (h % 2)
                        zx[h + 1, pl.ds(put, 1), :] = (
                            sides[s][c, pl.ds(face_at + slot, 1), :]
                            + side_face[s, pl.ds(slot, 1), :] * ex[1 + h // 2, pl.ds(get, 1), :]
                        )
        dot_aw = jnp.zeros((angles, radial), jnp.float32)
        below, here = zx[0, line, :], zx[1, line, :]
        for h in range(height):
            above = zx[h + 2, line, :]
            near = below + above + zx[h + 1, pl.ds(PAD - 1, angles), :] + zx[h + 1, pl.ds(PAD + 1, angles), :]
            near = near + radial_pair(here)
            new = delta[h] * here - near - SHIFT * u[c, h]
            un[c, h] = new
            dot_aw = dot_aw + new * here
            below, here = here, above
        lane = lax.broadcasted_iota(jnp.int32, (1, radial), 1)
        row = dots_in[...] if False else jnp.zeros((1, radial), jnp.float32)
        row = jnp.where(lane == dot_at * columns + c, jnp.sum(dot_uw), row)
        row = jnp.where(lane == (dot_at + 1) * columns + c, jnp.sum(dot_aw), row)

        @pl.when(c == 0)
        def _():
            dots[...] = dots_in[...]

        dots[...] += jnp.broadcast_to(row, dots.shape)
        if not last:
            restrict_column(c, un, weight, pre, pair, msg_a, msg_b)
            write_faces(c, un, q, parity_h, msg_a, msg_b, beside, coarse_rows)


def krylov(mu):
    def apply(p):
        out = [SHIFT * v for v in p] + [jnp.zeros_like(mu[0])]
        for i, v in enumerate(p):
            out[i + 1] = out[i + 1] + v
        return out

    def inner(a, b):
        total = 0.0
        for m in range(len(a) + len(b) - 1):
            part = sum(a[i] * b[m - i] for i in range(len(a)) if 0 <= m - i < len(b))
            total = total + part * mu[m]
        return total

    def plus(a, b, scale):
        long = max(len(a), len(b))
        out = []
        for i in range(long):
            v = a[i] if i < len(a) else None
            s = scale * b[i] if i < len(b) else None
            out.append(v if s is None else s if v is None else v + s)
        return out

    r = [jnp.ones_like(mu[0])]
    p = r
    x = []
    rz = mu[0]
    for step in range(ITERS):
        image = apply(p)
        alpha = rz / inner(p, image)
        x = plus(x, p, alpha)
        r = plus(r, image, -alpha)
        if step + 1 < ITERS:
            new = inner(r, r)
            p = plus(r, p, new / rz)
            rz = new
    return x, r


def finish(columns, group, *refs):
    refs = list(refs)
    dots = refs.pop(0)
    us = [refs.pop(0) for _ in range(ITERS + 1)]
    ws = [refs.pop(0) for _ in range(ITERS)]
    weight, winv, x_out, r_out = refs
    height, angles, radial = us[0].shape[1:]
    total = jnp.sum(dots[...], axis=0, keepdims=True)
    mu = [total if m == 0 else pltpu.roll(total, radial - m * columns, 1) for m in range(2 * ITERS)]
    xs, rs = krylov(mu)
    lane = lax.broadcasted_iota(jnp.int32, (1, radial), 1)
    base = pl.program_id(0) * group
    for c in range(group):
        pick = lambda v: jnp.sum(jnp.where(lane == base + c, v, 0.0), axis=1, keepdims=True)
        xc = [pick(v) for v in xs]
        rc = [pick(v) for v in rs]
        for h in range(height):
            x = sum(k * w[c, h] for k, w in zip(xc, ws))
            r = sum(k * u[c, h] for k, u in zip(rc, us))
            x_out[c, pl.ds(h, angles, stride=height), :] = winv[h] * x
            r_out[c, pl.ds(h, angles, stride=height), :] = weight[h] * r


def pairs(count, odd, periodic):
    found = []
    for i in range(odd, count, 2):
        j = i + 1
        if j < count or periodic:
            found += [(i, j % count), (j % count, i)]
    return found


def body(loads, material, support, modulus, positions):
    cases, comps, angles, height, radial = loads.shape
    columns = cases * comps
    margin = CSWEEPS
    own, half = height // 2, angles // 2
    assert own >= margin and half >= margin and radial == 128
    n_ang, n_hgt = lax.axis_size("ang"), lax.axis_size("hgt")
    at_ang, at_hgt = lax.axis_index("ang"), lax.axis_index("hgt")
    parity = jnp.stack((at_hgt % 2, at_ang % 2)).astype(jnp.int32)

    total_angles = angles * n_ang
    where = at_ang * angles + lax.iota(jnp.int32, angles)
    apart = jnp.abs(where[None, :] - positions[:, None])
    cycle_dist = jnp.minimum(apart, total_angles - apart)
    hit = jnp.where(cycle_dist < angles, -LOAD, 0.0)
    hit = jnp.broadcast_to(hit[:, :, None], (cases, angles, radial))

    field = f32(columns, height, angles, radial)
    coef = f32(height, angles, radial)
    rows_h = own * half + angles
    rows_a = sum(count for _, count in corner_pieces(margin, own)) + height
    vm = lambda *s: pltpu.VMEM(s, jnp.float32)

    (u, msg_a, msg_b, beside, delta, q, beta, weight, winv, pre, _) = call(
        functools.partial(prepare, cases, comps, modulus.shape[0]),
        [field, f32(columns + 1, rows_h, radial), f32(columns + 1, rows_h, radial),
         f32(columns + 1, 2 * height, radial), coef, coef, coef, coef, coef,
         f32(own, half, radial), f32(own, half, radial)],
        loads.reshape(columns, angles * height, radial), hit,
        material.reshape(angles * height, radial), support.reshape(angles * height, radial), modulus, parity,
        smem=(4, 5),
        mat=vm(angles, radial), sup=vm(height, angles, radial), pair=vm(own, angles, radial),
    )

    us, ws = [u], []
    dots = jnp.zeros((n_ang * n_hgt, radial), jnp.float32)
    shared = None
    for step in range(ITERS):
        first, last = step == 0, step + 1 == ITERS
        from_a = lax.ppermute(msg_a, "hgt", pairs(n_hgt, 0, False))
        from_b = lax.ppermute(msg_b, "hgt", pairs(n_hgt, 1, False))
        count = msg_a.shape[0]
        out_a, out_b = call(
            functools.partial(beside_messages, margin, own, half),
            [f32(count, rows_a, radial)] * 2,
            parity, msg_a, from_a, from_b, beside, smem=(0,),
        )
        side_a = lax.ppermute(out_a, "ang", pairs(n_ang, 0, True))
        side_b = lax.ppermute(out_b, "ang", pairs(n_ang, 1, True))
        args = [us[-1], msg_a, from_a, from_b, side_a, side_b, dots, parity, delta, q, beta, weight, pre]
        outs = [field, field]
        if first:
            outs += [f32(own + 2 * margin, half + 2 * margin, radial), f32(2, angles, radial), f32(2, height, radial)]
        else:
            args += list(shared)
        if not last:
            outs += [f32(columns, rows_h, radial), f32(columns, rows_h, radial), f32(columns, 2 * height, radial)]
        outs.append(f32(n_ang * n_hgt, radial))
        ext_h = own + 2 * margin
        result = list(call(
            functools.partial(apply_step, margin, own, half, first, last, 2 * step),
            outs, *args, smem=(7,),
            gx=vm(ext_h, half + 2 * margin + 2 * PAD, radial),
            va=vm(ext_h, half + 2 * margin + 2 * PAD, radial),
            vb=vm(ext_h, half + 2 * margin + 2 * PAD, radial),
            ex=vm(own + 2, 2 * (half + 2 * margin), radial),
            zx=vm(height + 2, angles + 2 * PAD, radial),
            edge=vm(2, angles, radial),
            pair=vm(own, angles, radial),
        ))
        ws.append(result.pop(0))
        us.append(result.pop(0))
        if first:
            shared = [result.pop(0) for _ in range(3)]
        if not last:
            msg_a, msg_b, beside = [result.pop(0) for _ in range(3)]
        dots = result.pop(0)

    dots = lax.all_to_all(dots, ("ang", "hgt"), 0, 0, tiled=True)
    group = comps
    whole = pl.BlockSpec(memory_space=pltpu.VMEM)
    block = pl.BlockSpec((group, height, angles, radial), lambda i: (i, 0, 0, 0))
    out_block = pl.BlockSpec((group, angles * height, radial), lambda i: (i, 0, 0))
    x, r = pl.pallas_call(
        functools.partial(finish, columns, group),
        grid=(columns // group,),
        out_shape=[f32(columns, angles * height, radial)] * 2,
        in_specs=[whole] + [block] * (2 * ITERS + 1) + [whole] * 2,
        out_specs=[out_block] * 2,
        compiler_params=pltpu.CompilerParams(vmem_limit_bytes=40 * 1024 * 1024),
    )(dots, *us, *ws, weight, winv)
    return x.reshape(loads.shape), r.reshape(loads.shape)


def solution(mesh):
    in_specs = (
        P(None, None, "ang", "hgt", None),
        P("ang", "hgt", None),
        P("ang", "hgt", None),
        P(),
        P(),
    )
    out_specs = (P(None, None, "ang", "hgt", None), P(None, None, "ang", "hgt", None))
    return jax.shard_map(body, mesh=mesh, in_specs=in_specs, out_specs=out_specs, check_vma=False)
```

```python
import functools

import jax
import jax.numpy as jnp
from jax import lax
from jax.experimental import pallas as pl
from jax.experimental.pallas import tpu as pltpu
from jax.sharding import PartitionSpec as P

ITERS = 3
CSWEEPS = 4


SIGMA = 6.5
SPRING = 20.0
OMEGA = 0.8
LOAD = 3.0
SHIFT = 1.0
PAD = 8
LIMIT = 40 * 1024 * 1024


def f32(*shape):
    return jax.ShapeDtypeStruct(shape, jnp.float32)


def call(kernel, out_shape, *args, smem=(), hbm=(), **scratch):
    vmem = pl.BlockSpec(memory_space=pltpu.VMEM)
    scalar = pl.BlockSpec(memory_space=pltpu.SMEM)
    outside = pl.BlockSpec(memory_space=pltpu.HBM)
    return pl.pallas_call(
        kernel,
        out_shape=out_shape,
        in_specs=[scalar if i in smem else outside if i in hbm else vmem for i in range(len(args))],
        out_specs=[vmem] * len(out_shape),
        scratch_shapes=list(scratch.values()),
        compiler_params=pltpu.CompilerParams(vmem_limit_bytes=LIMIT),
    )(*args)


def even(axis):
    return lax.rem(lax.axis_index(axis), 2) == 0


def radial_pair(v):
    lane = lax.broadcasted_iota(jnp.int32, v.shape, 1)
    last = v.shape[1] - 1
    inner = jnp.where(lane == 0, 0.0, pltpu.roll(v, 1, 1))
    return inner + jnp.where(lane == last, 0.0, pltpu.roll(v, last, 1))


def corner_rows(margin):
    pieces, at = [], 0
    for side in range(2):
        for d in range(1, margin):
            pieces.append((side, d, margin - d, at))
            at += margin - d
    return pieces, at


def pair_slot(c, rows):
    if isinstance(c, int):
        return c // 2, (c % 2) * rows
    return c[0], c[1] * rows


def send_coarse(c, k, g, dims, even_a, msg, side):
    margin, own, half = dims
    msg_a, msg_b = msg
    side_a, side_b = side
    msg_a[c, pl.ds(k * half, half), :] = g
    msg_b[c, pl.ds(k * half, half), :] = g
    low, high = g[:margin], g[half - margin:]
    rows = pl.ds(k * margin, margin)
    side_a[c, rows, :] = jnp.where(even_a, high, low)
    side_b[c, rows, :] = jnp.where(even_a, low, high)


def send_faces(c, field, scale, dims, even_a, even_h, msg, side):
    margin, own, half = dims
    height, angles = 2 * own, 2 * half
    bottom, top = field(pl.ds(0, angles)), field(pl.ds((height - 1) * angles, angles))
    ends = []
    for s, a in enumerate((0, angles - 1)):
        for odd in range(2):
            ends.append(field(pl.ds(odd * angles + a, own, stride=2 * angles)))
    if scale is not None:
        full, ends_scale = scale
        bottom = full[pl.ds(0, angles), :] * bottom
        top = full[pl.ds((height - 1) * angles, angles), :] * top
        ends = [ends_scale[pl.ds(i * own, own), :] * e for i, e in enumerate(ends)]
    rows = pl.ds(own * half, angles)
    msg[0][c, rows, :] = jnp.where(even_h, top, bottom)
    msg[1][c, rows, :] = jnp.where(even_h, bottom, top)
    for odd in range(2):
        rows = pl.ds(own * margin + odd * own, own)
        low, high = ends[odd], ends[2 + odd]
        side[0][c, rows, :] = jnp.where(even_a, high, low)
        side[1][c, rows, :] = jnp.where(even_a, low, high)


def restrict_column(c, u, weight, pre, pair, dims, even_a, msg, side):
    margin, own, half = dims
    angles = 2 * half
    for k in range(own):
        one, two = pl.ds(2 * k * angles, angles), pl.ds((2 * k + 1) * angles, angles)
        pair[k] = weight[one, :] * u[c, one, :] + weight[two, :] * u[c, two, :]
    for k in range(own):
        g = pre[k] * (pair[k, pl.ds(0, half, stride=2), :] + pair[k, pl.ds(1, half, stride=2), :])
        send_coarse(c, k, g, dims, even_a, msg, side)


def prepare(cases, comps, levels, n_ang, dims, *refs):
    refs = list(refs)
    take = lambda n: [refs.pop(0) for _ in range(n)]
    loads, material, support, modulus, positions = take(5)
    u, = take(1)
    msg, side = take(2), take(2)
    delta, q, beta, weight, winv, pre, q_ends = take(7)
    sup, pair, prolonged = take(3)
    margin, own, half = dims
    columns = cases * comps
    height, angles = 2 * own, 2 * half
    radial = u.shape[-1]
    even_a, even_h = even("ang"), even("hgt")
    for h in range(height):
        rows = pl.ds(h, angles, stride=height)
        level = material[rows, :]
        stiff = jnp.zeros(level.shape, jnp.float32)
        for n in range(levels):
            stiff = jnp.where(level == n, modulus[n], stiff)
        w = jnp.sqrt(stiff)
        s = support[rows, :].astype(jnp.float32)
        d = SIGMA + SPRING * s / stiff
        line = pl.ds(h * angles, angles)
        weight[line, :] = w
        winv[line, :] = 1.0 / w
        delta[line, :] = d
        q[line, :] = OMEGA / d
        sup[line, :] = s
    for k in range(own):
        one, two = pl.ds(2 * k * angles, angles), pl.ds((2 * k + 1) * angles, angles)
        pair[2 * k] = weight[one, :] + weight[two, :]
        pair[2 * k + 1] = sup[one, :] + sup[two, :]
    for k in range(own):
        mean = lambda i: 0.25 * (pair[i, pl.ds(0, half, stride=2), :] + pair[i, pl.ds(1, half, stride=2), :])
        wc, sc = mean(2 * k), mean(2 * k + 1)
        dc = SIGMA * wc * wc + SPRING * sc
        pre[k] = 0.5 * OMEGA * wc / dc
        send_coarse(columns, k, OMEGA * wc * wc / dc, dims, even_a, msg, side)
        inv = 0.5 / wc
        prolonged[k, pl.ds(0, half, stride=2), :] = inv
        prolonged[k, pl.ds(1, half, stride=2), :] = inv
    for h in range(height):
        line = pl.ds(h * angles, angles)
        beta[line, :] = prolonged[h // 2] * weight[line, :]
    for s, a in enumerate((0, angles - 1)):
        for odd in range(2):
            q_ends[pl.ds((2 * s + odd) * own, own), :] = q[pl.ds(odd * angles + a, own, stride=2 * angles), :]
    send_faces(columns, lambda rows: beta[rows, :], None, dims, even_a, even_h, msg, side)
    where = lax.axis_index("ang") * angles + lax.broadcasted_iota(jnp.int32, (angles, radial), 0)

    @pl.loop(0, columns)
    def _(c):
        apart = jnp.abs(where - positions[lax.div(c, comps)])
        hit = jnp.minimum(apart, angles * n_ang - apart) < angles
        push = jnp.where(hit & (lax.rem(c, comps) == 2), -LOAD, 0.0)
        for h in range(height):
            line = pl.ds(h * angles, angles)
            u[c, line, :] = winv[line, :] * (loads[c, pl.ds(h, angles, stride=height), :] + push)
        restrict_column(c, u, weight, pre, pair, dims, even_a, msg, side)
        send_faces(c, lambda rows: u[c, rows, :], (q, q_ends), dims, even_a, even_h, msg, side)


def corner_messages(dims, count, side_a, side_b, out_a, out_b):
    margin, own, half = dims
    pieces, rows = corner_rows(margin)
    even_a, even_h = even("ang"), even("hgt")
    for c in range(count):
        slab, base = pair_slot(c, rows)
        for s, d, n, at in pieces:
            def piece(k):
                first = k * margin + (margin - n if s == 0 else 0)
                a, b = side_a[c, pl.ds(first, n), :], side_b[c, pl.ds(first, n), :]
                return jnp.where(even_a, b, a) if s == 0 else jnp.where(even_a, a, b)
            top, bottom = piece(own - d), piece(d - 1)
            out_a[slab, pl.ds(base + at, n), :] = jnp.where(even_h, top, bottom)
            out_b[slab, pl.ds(base + at, n), :] = jnp.where(even_h, bottom, top)


def assemble(c, slot, field, edge, dims, even_a, even_h, sent, far, side, corner):
    margin, own, half = dims
    ang0 = PAD + margin
    pick = lambda test, pair: (jnp.where(test, pair[0], pair[1]), jnp.where(test, pair[1], pair[0]))
    for k in range(own):
        field[margin + k, pl.ds(ang0, half), :] = sent[c, pl.ds(k * half, half), :]
        rows = pl.ds(k * half, half)
        up, down = pick(even_h, (far[0][c, rows, :], far[1][c, rows, :]))
        if k < margin:
            field[margin + own + k, pl.ds(ang0, half), :] = up
        if k >= own - margin:
            field[k - (own - margin), pl.ds(ang0, half), :] = down
        rows = pl.ds(k * margin, margin)
        high, low = pick(even_a, (side[0][c, rows, :], side[1][c, rows, :]))
        field[margin + k, pl.ds(ang0 - margin, margin), :] = low
        field[margin + k, pl.ds(ang0 + half, margin), :] = high
    rows = pl.ds(own * half, 2 * half)
    edge[1], edge[0] = pick(even_h, (far[0][c, rows, :], far[1][c, rows, :]))
    pieces, length = corner_rows(margin)
    slab, base = pair_slot(slot, length)
    for s, d, n, at in pieces:
        rows = pl.ds(base + at, n)
        up, down = pick(even_h, (corner[0][slab, rows, :], corner[1][slab, rows, :]))
        lane0 = ang0 - n if s == 0 else ang0 + half
        field[margin + own - 1 + d, pl.ds(lane0, n), :] = up
        field[margin - d, pl.ds(lane0, n), :] = down


def apply_step(dims, columns, first, last, dot_at, *refs):
    refs = list(refs)
    take = lambda n: [refs.pop(0) for _ in range(n)]
    u, sent = take(2)
    far, side, corner = take(2), take(2), take(2)
    dots_in, delta, q, beta, weight, pre, q_ends = take(7)
    kx, edge_b, ends_b = take(3) if not first else (None,) * 3
    w, un = take(2)
    if first:
        kx, edge_b, ends_b = take(3)
    if not last:
        msg, beside = take(2), take(2)
    dots, = take(1)
    gxs, vas, vbs, exs, zxs, edges, pairs_, sums = take(8)
    margin, own, half = dims
    height, angles = 2 * own, 2 * half
    radial = u.shape[-1]
    even_a, even_h = even("ang"), even("hgt")
    ext = half + 2 * margin
    body = pl.ds(PAD, ext)
    wide, fine = 2 * ext, angles + 2 * PAD
    face_at = own * margin

    def angular_ends(c):
        rows = pl.ds(face_at, height)
        a, b = side[0][c, rows, :], side[1][c, rows, :]
        return jnp.where(even_a, b, a), jnp.where(even_a, a, b)

    if first:
        assemble(columns, columns, gxs.at[0], edge_b, dims, even_a, even_h, sent, far, side, corner)
        for h in range(own + 2 * margin):
            kx[h] = gxs[0, h, body, :]
        ends_b[0], ends_b[1] = angular_ends(columns)

    def column(c, slot, lane):
        gx, va, vb, edge = gxs.at[lane], vas.at[lane], vbs.at[lane], edges.at[lane]
        ex, zx, pair = exs.at[lane], zxs.at[lane], pairs_.at[lane]
        assemble(c, slot, gx, edge, dims, even_a, even_h, sent, far, side, corner)
        source, target = gx, va
        for sweep in range(1, CSWEEPS):
            lo, hi = sweep, own + 2 * margin - sweep
            below, here = source[lo - 1, body, :], source[lo, body, :]
            for h in range(lo, hi):
                above = source[h + 1, body, :]
                near = below + above + source[h, pl.ds(PAD - 1, ext), :] + source[h, pl.ds(PAD + 1, ext), :]
                near = near + radial_pair(here)
                target[h, body, :] = gx[h, body, :] + (1.0 - OMEGA) * here + kx[h] * near
                below, here = here, above
            source, target = target, (vb if target is va else va)
        for h in range(own + 2):
            e = source[margin - 1 + h, body, :]
            ex[pl.ds(h * wide, ext, stride=2), :] = e
            ex[pl.ds(h * wide + 1, ext, stride=2), :] = e
        dot_uw = jnp.zeros((angles, radial), jnp.float32)
        for h in range(height):
            line = pl.ds(h * angles, angles)
            here = u[c, line, :]
            z = q[line, :] * here + beta[line, :] * ex[pl.ds((1 + h // 2) * wide + 2 * margin, angles), :]
            zx[pl.ds((h + 1) * fine + PAD, angles), :] = z
            w[c, line, :] = z
            dot_uw = dot_uw + here * z
        zx[pl.ds(PAD, angles), :] = edge[0] + edge_b[0] * ex[pl.ds(2 * margin, angles), :]
        zx[pl.ds((height + 1) * fine + PAD, angles), :] = (
            edge[1] + edge_b[1] * ex[pl.ds((own + 1) * wide + 2 * margin, angles), :]
        )
        for s, ends in enumerate(angular_ends(c)):
            put, get = ((PAD - 1, 2 * margin - 1), (PAD + angles, 2 * margin + angles))[s]
            e = ex[pl.ds(wide + get, own, stride=wide), :]
            for odd in range(2):
                rows = slice(odd * own, (odd + 1) * own)
                zx[pl.ds((1 + odd) * fine + put, own, stride=2 * fine), :] = ends[rows] + ends_b[s, rows, :] * e
        dot_aw = jnp.zeros((angles, radial), jnp.float32)
        below, here = zx[pl.ds(PAD, angles), :], zx[pl.ds(fine + PAD, angles), :]
        for h in range(height):
            line = pl.ds(h * angles, angles)
            at = (h + 1) * fine + PAD
            above = zx[pl.ds(at + fine, angles), :]
            near = below + above + zx[pl.ds(at - 1, angles), :] + zx[pl.ds(at + 1, angles), :]
            near = near + radial_pair(here)
            new = delta[line, :] * here - near - SHIFT * u[c, line, :]
            un[c, line, :] = new
            dot_aw = dot_aw + new * here
            below, here = here, above
        tile = lambda d: sum(d[i:i + 8] for i in range(0, angles, 8))
        sums[0, c] = tile(dot_uw)
        sums[1, c] = tile(dot_aw)
        if not last:
            restrict_column(c, un, weight, pre, pair, dims, even_a, msg, beside)
            send_faces(c, lambda rows: un[c, rows, :], (q, q_ends), dims, even_a, even_h, msg, beside)

    @pl.loop(0, columns // 2)
    def _(i):
        for lane in range(2):
            column(2 * i + lane, (i, lane), lane)

    if columns % 2:
        column(columns - 1, columns - 1, 0)

    lane = lax.broadcasted_iota(jnp.int32, (1, radial), 1)
    row = jnp.zeros((1, radial), jnp.float32)
    for m in range(2):
        for c in range(columns):
            total = jnp.sum(jnp.sum(sums[m, c], axis=0, keepdims=True), axis=1, keepdims=True)
            row = jnp.where(lane == (dot_at + m) * columns + c, total, row)
    dots[...] = dots_in[...] + jnp.broadcast_to(row, dots.shape)


def krylov(mu):
    def apply(p):
        out = [SHIFT * v for v in p] + [jnp.zeros_like(mu[0])]
        for i, v in enumerate(p):
            out[i + 1] = out[i + 1] + v
        return out

    def inner(a, b):
        total = 0.0
        for m in range(len(a) + len(b) - 1):
            part = sum(a[i] * b[m - i] for i in range(len(a)) if 0 <= m - i < len(b))
            total = total + part * mu[m]
        return total

    def plus(a, b, scale):
        out = []
        for i in range(max(len(a), len(b))):
            v = a[i] if i < len(a) else None
            s = scale * b[i] if i < len(b) else None
            out.append(v if s is None else s if v is None else v + s)
        return out

    r = [jnp.ones_like(mu[0])]
    p = r
    x = []
    rz = mu[0]
    for step in range(ITERS):
        image = apply(p)
        alpha = rz / inner(p, image)
        x = plus(x, p, alpha)
        r = plus(r, image, -alpha)
        if step + 1 < ITERS:
            new = inner(r, r)
            p = plus(r, p, new / rz)
            rz = new
    return x, r


def finish(columns, group, dims, *refs):
    refs = list(refs)
    dots = refs.pop(0)
    us = [refs.pop(0) for _ in range(ITERS + 1)]
    ws = [refs.pop(0) for _ in range(ITERS)]
    weight, winv, x_out, r_out = refs
    margin, own, half = dims
    height, angles = 2 * own, 2 * half
    radial = us[0].shape[-1]
    total = jnp.sum(dots[...], axis=0, keepdims=True)
    mu = [total if m == 0 else pltpu.roll(total, radial - m * columns, 1) for m in range(2 * ITERS)]
    xs, rs = krylov(mu)
    lane = lax.broadcasted_iota(jnp.int32, (1, radial), 1)
    base = pl.program_id(0) * group
    for c in range(group):
        pick = lambda v: jnp.sum(jnp.where(lane == base + c, v, 0.0), axis=1, keepdims=True)
        xc = [pick(v) for v in xs]
        rc = [pick(v) for v in rs]
        for h in range(height):
            line = pl.ds(h * angles, angles)
            x = sum(k * w[c, line, :] for k, w in zip(xc, ws))
            r = sum(k * u[c, line, :] for k, u in zip(rc, us))
            x_out[c, pl.ds(h, angles, stride=height), :] = winv[line, :] * x
            r_out[c, pl.ds(h, angles, stride=height), :] = weight[line, :] * r


def pairs(count, odd, periodic):
    found = []
    for i in range(odd, count, 2):
        j = i + 1
        if j < count or periodic:
            found += [(i, j % count), (j % count, i)]
    return found


def body(loads, material, support, modulus, positions):
    cases, comps, angles, height, radial = loads.shape
    columns = cases * comps
    margin = CSWEEPS
    own, half = height // 2, angles // 2
    dims = (margin, own, half)
    n_ang, n_hgt = lax.axis_size("ang"), lax.axis_size("hgt")
    assert own >= margin and half >= margin and angles % 8 == 0 and n_ang % 2 == 0
    assert 2 * ITERS * columns <= radial
    cells = height * angles
    field, coef = f32(columns, cells, radial), f32(cells, radial)
    rows_h, rows_a, rows_c = own * half + angles, own * margin + height, corner_rows(margin)[1]
    vm = lambda *s: pltpu.VMEM(s, jnp.float32)
    message = lambda n: [f32(n, rows_h, radial)] * 2 + [f32(n, rows_a, radial)] * 2

    out = list(call(
        functools.partial(prepare, cases, comps, modulus.shape[0], n_ang, dims),
        [field] + message(columns + 1) + [coef] * 5 + [f32(own, half, radial), f32(4 * own, radial)],
        loads.reshape(columns, cells, radial), material.reshape(cells, radial), support.reshape(cells, radial),
        modulus, positions,
        smem=(3, 4),
        sup=vm(cells, radial), pair=vm(2 * own, angles, radial), prolonged=vm(own, angles, radial),
    ))
    u, msg, side = out[0], out[1:3], out[3:5]
    delta, q, beta, weight, winv, pre, q_ends = out[5:]
    us, ws = [u], []
    dots = jnp.zeros((n_ang * n_hgt, radial), jnp.float32)
    shared = []
    for step in range(ITERS):
        first, last = step == 0, step + 1 == ITERS
        count = columns + 1 if first else columns
        slabs = (count + 1) // 2
        swap = lambda v, axis, wraps: [lax.ppermute(v[i], axis, pairs(lax.axis_size(axis), i, wraps)) for i in range(2)]
        far = swap(msg, "hgt", False)
        beside = swap(side, "ang", True)
        corner = call(
            functools.partial(corner_messages, dims, count), [f32(slabs, 2 * rows_c, radial)] * 2, *beside,
        )
        corner = swap(corner, "hgt", False)
        args = [us[-1], msg[0], *far, *beside, *corner, dots, delta, q, beta, weight, pre, q_ends, *shared]
        outs = [field, field]
        ext_h, ext_a = own + 2 * margin, half + 2 * margin
        if first:
            outs += [f32(ext_h, ext_a, radial), f32(2, angles, radial), f32(2, height, radial)]
        if not last:
            outs += message(columns)
        outs.append(f32(n_ang * n_hgt, radial))
        block = vm(2, ext_h, ext_a + 2 * PAD, radial)
        out = list(call(
            functools.partial(apply_step, dims, columns, first, last, 2 * step),
            outs, *args,
            gx=block, va=block, vb=block,
            ex=vm(2, (own + 2) * 2 * ext_a, radial),
            zx=vm(2, (height + 2) * (angles + 2 * PAD), radial),
            edge=vm(2, 2, angles, radial),
            pair=vm(2, own, angles, radial),
            sums=vm(2, columns, 8, radial),
        ))
        ws.append(out.pop(0))
        us.append(out.pop(0))
        if first:
            shared, out = out[:3], out[3:]
        if not last:
            msg, side, out = out[:2], out[2:4], out[4:]
        dots = out.pop(0)

    dots = lax.all_to_all(dots, ("ang", "hgt"), 0, 0, tiled=True)
    group = comps
    whole = pl.BlockSpec(memory_space=pltpu.VMEM)
    block = pl.BlockSpec((group, cells, radial), lambda i: (i, 0, 0))
    x, r = pl.pallas_call(
        functools.partial(finish, columns, group, dims),
        grid=(columns // group,),
        out_shape=[field] * 2,
        in_specs=[whole] + [block] * (2 * ITERS + 1) + [whole] * 2,
        out_specs=[block] * 2,
        compiler_params=pltpu.CompilerParams(vmem_limit_bytes=LIMIT),
    )(dots, *us, *ws, weight, winv)
    return x.reshape(loads.shape), r.reshape(loads.shape)


def solution(mesh):
    in_specs = (
        P(None, None, "ang", "hgt", None),
        P("ang", "hgt", None),
        P("ang", "hgt", None),
        P(),
        P(),
    )
    out_specs = (P(None, None, "ang", "hgt", None), P(None, None, "ang", "hgt", None))
    return jax.shard_map(body, mesh=mesh, in_specs=in_specs, out_specs=out_specs, check_vma=False)
```

```python
import functools

import jax
import jax.numpy as jnp
from jax import lax
from jax.experimental import pallas as pl
from jax.experimental.pallas import tpu as pltpu
from jax.sharding import PartitionSpec as P

ITERS = 3
CSWEEPS = 4


SIGMA = 6.5
SPRING = 20.0
OMEGA = 0.8
LOAD = 3.0
SHIFT = 1.0
PAD = 8
LIMIT = 40 * 1024 * 1024


def f32(*shape):
    return jax.ShapeDtypeStruct(shape, jnp.float32)


def call(kernel, out_shape, *args, hbm=(), hbm_out=False, scratch=()):
    vmem = pl.BlockSpec(memory_space=pltpu.VMEM)
    outside = pl.BlockSpec(memory_space=pltpu.HBM)
    return pl.pallas_call(
        kernel,
        out_shape=out_shape,
        in_specs=[outside if i in hbm else vmem for i in range(len(args))],
        out_specs=[outside if hbm_out else vmem] * len(out_shape),
        scratch_shapes=list(scratch),
        compiler_params=pltpu.CompilerParams(vmem_limit_bytes=LIMIT),
    )(*args)


def even(axis):
    return lax.rem(lax.axis_index(axis), 2) == 0


def radial_pair(v):
    lane = lax.broadcasted_iota(jnp.int32, v.shape, 1)
    last = v.shape[1] - 1
    inner = jnp.where(lane == 0, 0.0, pltpu.roll(v, 1, 1))
    return inner + jnp.where(lane == last, 0.0, pltpu.roll(v, last, 1))


def choose(test, one, two):
    return jnp.where(test, one, two), jnp.where(test, two, one)


def corner_rows(margin):
    pieces, at = [], 0
    for side in range(2):
        for d in range(1, margin):
            pieces.append((side, d, margin - d, at))
            at += margin - d
    return pieces, at


def send(c, coarse, bottom, top, low, high, dims, evens, out):
    margin, own, half = dims
    even_a, even_h = evens
    sent, msg_a, msg_b, side_a, side_b = out
    for k, g in enumerate(coarse):
        sent[c, pl.ds(k * half, half), :] = g
        rows = pl.ds(k * margin, margin)
        side_a[c, rows, :], side_b[c, rows, :] = choose(even_a, g[half - margin:], g[:margin])
    for d in range(1, margin):
        rows = pl.ds((d - 1) * half, half)
        msg_a[c, rows, :], msg_b[c, rows, :] = choose(even_h, coarse[own - d], coarse[d - 1])
    rows = pl.ds((margin - 1) * half, 2 * half)
    msg_a[c, rows, :], msg_b[c, rows, :] = choose(even_h, top, bottom)
    rows = pl.ds(own * margin, 2 * own)
    side_a[c, rows, :], side_b[c, rows, :] = choose(even_a, high, low)


def send_field(c, field, q, q_ends, fold, weight, pre, dims, evens, out):
    margin, own, half = dims
    angles, height = 2 * half, 2 * own
    part = lambda ref, h, p: ref[pl.ds(h * angles + p * half, half), :]
    coarse = []
    for k in range(own):
        total = sum(part(weight, h, p) * part(field, h, p) for h in (2 * k, 2 * k + 1) for p in range(2))
        coarse.append(pre[k] * total)
    faces = []
    for s, (h, far) in enumerate(((0, margin - 1), (height - 1, own - margin))):
        faces.append(jnp.concatenate([
            part(q, h, p) * part(field, h, p) + part(fold.at[s], 0, p) * coarse[far] for p in range(2)
        ]))
    ends = [q_ends[s] * field[pl.ds(a, height, stride=angles), :] for s, a in enumerate((0, angles - 1))]
    send(c, coarse, *faces, *ends, dims, evens, out)


def prepare(cases, comps, levels, n_ang, dims, *refs):
    refs = list(refs)
    take = lambda n: [refs.pop(0) for _ in range(n)]
    loads_far, material_far, support_far, modulus_far, positions_far = take(5)
    u, = take(1)
    out = take(5)
    delta, q, beta, weight, winv, pre, q_ends, fold = take(8)
    loads, material, support, modulus, positions, sems, small = take(7)
    margin, own, half = dims
    columns = cases * comps
    height, angles = 2 * own, 2 * half
    radial = u.shape[-1]
    evens = even("ang"), even("hgt")
    early = [
        pltpu.make_async_copy(far, near, small.at[i])
        for i, (far, near) in enumerate((
            (material_far, material), (support_far, support), (modulus_far, modulus), (positions_far, positions),
        ))
    ]
    for copy in early:
        copy.start()
    for c in range(columns):
        pltpu.make_async_copy(loads_far.at[c], loads.at[c], sems.at[c]).start()
    for copy in early:
        copy.wait()
    wide, stiffen = [], []
    for h in range(height):
        for p in range(2):
            rows = pl.ds(p * height + h, half, stride=2 * height)
            level = material[rows, :]
            stiff = jnp.zeros(level.shape, jnp.float32)
            for n in range(levels):
                stiff = jnp.where(level == n, modulus[n], stiff)
            w = jnp.sqrt(stiff)
            s = support[rows, :].astype(jnp.float32)
            d = SIGMA + SPRING * s / stiff
            line = pl.ds(h * angles + p * half, half)
            weight[line, :] = w
            winv[line, :] = 1.0 / w
            delta[line, :] = d
            q[line, :] = OMEGA / d
            wide.append(w)
            stiffen.append(s)
    kappa = []
    for k in range(own):
        four = slice(4 * k, 4 * k + 4)
        wc, sc = 0.25 * sum(wide[four]), 0.25 * sum(stiffen[four])
        dc = SIGMA * wc * wc + SPRING * sc
        pre[k] = 0.5 * OMEGA * wc / dc
        kappa.append(OMEGA * wc * wc / dc)
        for i in range(4 * k, 4 * k + 4):
            beta[pl.ds(i * half, half), :] = 0.5 / wc * wide[i]
    faces = [beta[pl.ds(h * angles, angles), :] for h in (0, height - 1)]
    for s in range(2):
        path = 1.0
        for d in range(margin - 1):
            path = path * kappa[d if s == 0 else own - 1 - d]
        fold[s] = faces[s] * jnp.concatenate([path, path])
    ends = []
    for s, a in enumerate((0, angles - 1)):
        rows = pl.ds(a, height, stride=angles)
        q_ends[s] = q[rows, :]
        ends.append(beta[rows, :])
    send(columns, kappa, *faces, *ends, dims, evens, out)
    where = lax.axis_index("ang") * angles + 2 * lax.broadcasted_iota(jnp.int32, (half, radial), 0)

    @pl.loop(0, columns)
    def _(c):
        pltpu.make_async_copy(loads_far.at[c], loads.at[c], sems.at[c]).wait()
        for p in range(2):
            apart = jnp.abs(where + p - positions[lax.div(c, comps)])
            hit = jnp.minimum(apart, angles * n_ang - apart) < angles
            push = jnp.where(hit & (lax.rem(c, comps) == 2), -LOAD, 0.0)
            for h in range(height):
                line = pl.ds(h * angles + p * half, half)
                rows = pl.ds(p * height + h, half, stride=2 * height)
                u[c, line, :] = winv[line, :] * (loads[c, rows, :] + push)
        send_field(c, u.at[c], q, q_ends, fold, weight, pre, dims, evens, out)


def corner_messages(dims, count, side_a, side_b, out_a, out_b):
    margin, own, half = dims
    pieces, rows = corner_rows(margin)
    even_a, even_h = even("ang"), even("hgt")
    for c in range(count):
        slab, base = c // 2, (c % 2) * rows
        for s, d, n, at in pieces:
            def piece(k):
                first = k * margin + (margin - n if s == 0 else 0)
                a, b = side_a[c, pl.ds(first, n), :], side_b[c, pl.ds(first, n), :]
                return jnp.where(even_a, b, a) if s == 0 else jnp.where(even_a, a, b)
            to = pl.ds(base + at, n)
            out_a[slab, to, :], out_b[slab, to, :] = choose(even_h, piece(own - d), piece(d - 1))


def apply_step(dims, columns, group, first, last, dot_at, *refs):
    refs = list(refs)
    take = lambda n: [refs.pop(0) for _ in range(n)]
    u, sent = take(2)
    far, side, corner = take(2), take(2), take(2)
    dots_in, delta, q, beta, weight, pre, q_ends, fold = take(8)
    kx, edge_b, ends_b = take(3) if not first else (None,) * 3
    w, un = take(2)
    if first:
        kx, edge_b, ends_b = take(3)
    if not last:
        out = take(5)
    dots, = take(1)
    gx, va, vb, zx, edge, sums = take(6)
    margin, own, half = dims
    height, angles = 2 * own, 2 * half
    radial = u.shape[-1]
    even_a, even_h = evens = even("ang"), even("hgt")
    ext_h, ext_a = own + 2 * margin, half + 2 * margin
    pitch = ext_a + 2 * PAD
    line_pitch = 3 * half
    start = PAD + margin
    coarse = lambda h, shift=0: pl.ds(h * pitch + PAD + shift, ext_a)
    inner = lambda h: pl.ds(h * pitch + start, half)
    pieces, corner_length = corner_rows(margin)

    def assemble(c, slab, base, lane, put_faces):
        field = gx.at[lane]
        for k in range(own):
            field[inner(margin + k), :] = sent[c, pl.ds(k * half, half), :]
            rows = pl.ds(k * margin, margin)
            high, low = choose(even_a, side[0][c, rows, :], side[1][c, rows, :])
            field[pl.ds((margin + k) * pitch + start - margin, margin), :] = low
            field[pl.ds((margin + k) * pitch + start + half, margin), :] = high
        for d in range(1, margin):
            rows = pl.ds((d - 1) * half, half)
            up, down = choose(even_h, far[0][c, rows, :], far[1][c, rows, :])
            field[inner(margin + own - 1 + d), :] = up
            field[inner(margin - d), :] = down
        rows = pl.ds((margin - 1) * half, angles)
        up, down = choose(even_h, far[0][c, rows, :], far[1][c, rows, :])
        put_faces(down, up)
        for s, d, n, at in pieces:
            rows = pl.ds(base + at, n)
            up, down = choose(even_h, corner[0][slab, rows, :], corner[1][slab, rows, :])
            to = start - n if s == 0 else start + half
            field[pl.ds((margin + own - 1 + d) * pitch + to, n), :] = up
            field[pl.ds((margin - d) * pitch + to, n), :] = down

    def angular_ends(c, odd):
        rows = pl.ds(own * margin + odd, own, stride=2)
        return reversed(choose(even_a, side[0][c, rows, :], side[1][c, rows, :]))

    for lane in range(group):
        for h in (0, ext_h - 1):
            gx[lane, coarse(h), :] = jnp.zeros((ext_a, radial), jnp.float32)

    if first:
        def keep(down, up):
            edge_b[0], edge_b[1] = down, up
        assemble(columns, columns // 2, (columns % 2) * corner_length, 0, keep)
        for h in range(1, ext_h - 1):
            kx[h] = gx[0, coarse(h), :]
        for odd in range(2):
            for s, end in enumerate(angular_ends(columns, odd)):
                ends_b[s, odd] = end

    def run(first_column, slab_of):
        lanes = range(group)
        at = [first_column + lane for lane in lanes]
        for lane in lanes:
            def keep(down, up, lane=lane):
                edge[lane, 0], edge[lane, 1] = down, up
            assemble(at[lane], *slab_of(lane), lane, keep)
        source, target = gx, va
        for sweep in range(1, CSWEEPS):
            lo, hi = sweep, ext_h - sweep
            below = [source[n, coarse(lo - 1), :] for n in lanes]
            here = [source[n, coarse(lo), :] for n in lanes]
            for h in range(lo, hi):
                k = kx[h]
                for n in lanes:
                    above = source[n, coarse(h + 1), :]
                    near = below[n] + above + source[n, coarse(h, -1), :] + source[n, coarse(h, 1), :]
                    near = near + radial_pair(here[n])
                    target[n, coarse(h), :] = gx[n, coarse(h), :] + (1.0 - OMEGA) * here[n] + k * near
                    below[n], here[n] = here[n], above
            source, target = target, (vb if target is va else va)
        dot_uw = [jnp.zeros((half, radial), jnp.float32) for _ in lanes]
        dot_aw = [jnp.zeros((half, radial), jnp.float32) for _ in lanes]
        place = lambda h, p, shift=0: pl.ds((h + 1) * line_pitch + 2 * p * half + shift, half)
        for k in range(own):
            e = [source[n, inner(margin + k), :] for n in lanes]
            for h in (2 * k, 2 * k + 1):
                for p in range(2):
                    line = pl.ds(h * angles + p * half, half)
                    qs, bs = q[line, :], beta[line, :]
                    for n in lanes:
                        here = u[at[n], line, :]
                        z = qs * here + bs * e[n]
                        zx[n, place(h, p), :] = z
                        w[at[n], line, :] = z
                        dot_uw[n] = dot_uw[n] + here * z
        for n in lanes:
            for s, (h, k) in enumerate(((-1, margin - 1), (height, margin + own))):
                e = source[n, inner(k), :]
                for p in range(2):
                    rows = pl.ds(p * half, half)
                    zx[n, place(h, p), :] = edge[n, s, rows, :] + edge_b[s, rows, :] * e
            for odd in range(2):
                for s, end in enumerate(angular_ends(at[n], odd)):
                    k = start - 1 if s == 0 else start + half
                    e = source[n, pl.ds(margin * pitch + k, own, stride=pitch), :]
                    put = 2 * half - 1 if s == 0 else half
                    zx[n, pl.ds((1 + odd) * line_pitch + put, own, stride=2 * line_pitch), :] = end + ends_b[s, odd] * e
        load = lambda n, h: [zx[n, place(h, p), :] for p in range(2)]
        below = [load(n, -1) for n in lanes]
        here = [load(n, 0) for n in lanes]
        for h in range(height):
            above = [load(n, h + 1) for n in lanes]
            for p in range(2):
                line = pl.ds(h * angles + p * half, half)
                d = delta[line, :]
                for n in lanes:
                    near = below[n][p] + above[n][p] + here[n][1 - p]
                    near = near + zx[n, place(h, 1 - p, 1 if p else -1), :]
                    near = near + radial_pair(here[n][p])
                    new = d * here[n][p] - near - SHIFT * u[at[n], line, :]
                    un[at[n], line, :] = new
                    dot_aw[n] = dot_aw[n] + new * here[n][p]
            below, here = here, above
        tile = lambda d: sum(d[i:i + 8] for i in range(0, half, 8))
        for n in lanes:
            sums[0, at[n]] = tile(dot_uw[n])
            sums[1, at[n]] = tile(dot_aw[n])
            if not last:
                send_field(at[n], un.at[at[n]], q, q_ends, fold, weight, pre, dims, evens, out)

    @pl.loop(0, columns // group)
    def _(i):
        slabs = group // 2
        run(group * i, lambda lane: (i * slabs + lane // 2, (lane % 2) * corner_length))

    lane = lax.broadcasted_iota(jnp.int32, (1, radial), 1)
    row = jnp.zeros((1, radial), jnp.float32)
    for m in range(2):
        for c in range(columns):
            total = jnp.sum(jnp.sum(sums[m, c], axis=0, keepdims=True), axis=1, keepdims=True)
            row = jnp.where(lane == (dot_at + m) * columns + c, total, row)
    dots[...] = dots_in[...] + jnp.broadcast_to(row, dots.shape)


def krylov(mu):
    def apply(p):
        out = [SHIFT * v for v in p] + [jnp.zeros_like(mu[0])]
        for i, v in enumerate(p):
            out[i + 1] = out[i + 1] + v
        return out

    def inner(a, b):
        total = 0.0
        for m in range(len(a) + len(b) - 1):
            part = sum(a[i] * b[m - i] for i in range(len(a)) if 0 <= m - i < len(b))
            total = total + part * mu[m]
        return total

    def plus(a, b, scale):
        out = []
        for i in range(max(len(a), len(b))):
            v = a[i] if i < len(a) else None
            s = scale * b[i] if i < len(b) else None
            out.append(v if s is None else s if v is None else v + s)
        return out

    r = [jnp.ones_like(mu[0])]
    p = r
    x = []
    rz = mu[0]
    for step in range(ITERS):
        image = apply(p)
        alpha = rz / inner(p, image)
        x = plus(x, p, alpha)
        r = plus(r, image, -alpha)
        if step + 1 < ITERS:
            new = inner(r, r)
            p = plus(r, p, new / rz)
            rz = new
    return x, r


def finish(columns, dims, *refs):
    refs = list(refs)
    dots = refs.pop(0)
    us = [refs.pop(0) for _ in range(ITERS + 1)]
    ws = [refs.pop(0) for _ in range(ITERS)]
    weight, winv, x_far, r_far, x_out, r_out, factors, sems = refs
    margin, own, half = dims
    height, angles = 2 * own, 2 * half
    radial = us[0].shape[-1]
    total = jnp.sum(dots[...], axis=0, keepdims=True)
    mu = [total if m == 0 else pltpu.roll(total, radial - m * columns, 1) for m in range(2 * ITERS)]
    xs, rs = krylov(mu)
    lane = lax.broadcasted_iota(jnp.int32, (1, radial), 1)
    for c in range(columns):
        for j, v in enumerate(xs + rs):
            one = jnp.sum(jnp.where(lane == c, v, 0.0), axis=1, keepdims=True)
            factors[c, j] = jnp.broadcast_to(one, (8, radial))

    copies = lambda c: [
        pltpu.make_async_copy(near.at[c], far.at[c], sems.at[i, c])
        for i, (near, far) in enumerate(((x_out, x_far), (r_out, r_far)))
    ]

    @pl.loop(0, columns)
    def _(c):
        full = [jnp.concatenate([factors[c, j]] * (half // 8)) for j in range(2 * ITERS + 1)]
        xc, rc = full[:ITERS], full[ITERS:]
        for h in range(height):
            for p in range(2):
                line = pl.ds(h * angles + p * half, half)
                rows = pl.ds(p * height + h, half, stride=2 * height)
                x_out[c, rows, :] = winv[line, :] * sum(k * w[c, line, :] for k, w in zip(xc, ws))
                r_out[c, rows, :] = weight[line, :] * sum(k * u[c, line, :] for k, u in zip(rc, us))
        for copy in copies(c):
            copy.start()

    @pl.loop(0, columns)
    def _(c):
        for copy in copies(c):
            copy.wait()


def pairs(count, odd, periodic):
    found = []
    for i in range(odd, count, 2):
        j = i + 1
        if j < count or periodic:
            found += [(i, j % count), (j % count, i)]
    return found


def body(loads, material, support, modulus, positions):
    cases, comps, angles, height, radial = loads.shape
    columns = cases * comps
    margin = CSWEEPS
    own, half = height // 2, angles // 2
    dims = (margin, own, half)
    n_ang, n_hgt = lax.axis_size("ang"), lax.axis_size("hgt")
    assert own >= margin and half >= margin and half % 8 == 0 and n_ang % 2 == 0
    assert 2 * ITERS * columns <= radial and columns % 2 == 0
    cells = height * angles
    field, coef = f32(columns, cells, radial), f32(cells, radial)
    rows_h, rows_a = (margin - 1) * half + angles, own * margin + height
    rows_c = corner_rows(margin)[1]
    vm = lambda *s: pltpu.VMEM(s, jnp.float32)
    message = lambda n: [f32(n, own * half, radial)] + [f32(n, rows_h, radial)] * 2 + [f32(n, rows_a, radial)] * 2

    out = list(call(
        functools.partial(prepare, cases, comps, modulus.shape[0], n_ang, dims),
        [field] + message(columns + 1) + [coef] * 5
        + [f32(own, half, radial), f32(2, height, radial), f32(2, angles, radial)],
        loads.reshape(columns, cells, radial), material.reshape(cells, radial), support.reshape(cells, radial),
        modulus, positions,
        hbm=range(5),
        scratch=[
            vm(columns, cells, radial), pltpu.VMEM((cells, radial), jnp.int32), pltpu.VMEM((cells, radial), jnp.int32),
            pltpu.SMEM(modulus.shape, jnp.float32), pltpu.SMEM(positions.shape, jnp.int32),
            pltpu.SemaphoreType.DMA((columns,)), pltpu.SemaphoreType.DMA((4,)),
        ],
    ))
    u, sent, msg, side = out[0], out[1], out[2:4], out[4:6]
    delta, q, beta, weight, winv, pre, q_ends, fold = out[6:]
    us, ws = [u], []
    dots = jnp.zeros((n_ang * n_hgt, radial), jnp.float32)
    shared = []
    group = 2
    for step in range(ITERS):
        first, last = step == 0, step + 1 == ITERS
        count = columns + 1 if first else columns
        slabs = (count + 1) // 2
        swap = lambda v, axis, wraps: [lax.ppermute(v[i], axis, pairs(lax.axis_size(axis), i, wraps)) for i in range(2)]
        far = swap(msg, "hgt", False)
        beside = swap(side, "ang", True)
        corner = call(
            functools.partial(corner_messages, dims, count), [f32(slabs, 2 * rows_c, radial)] * 2, *beside,
        )
        corner = swap(corner, "hgt", False)
        args = [us[-1], sent, *far, *beside, *corner, dots, delta, q, beta, weight, pre, q_ends, fold, *shared]
        outs = [field, field]
        ext_h, ext_a = own + 2 * margin, half + 2 * margin
        if first:
            outs += [f32(ext_h, ext_a, radial), f32(2, angles, radial), f32(2, 2, own, radial)]
        if not last:
            outs += message(columns)
        outs.append(f32(n_ang * n_hgt, radial))
        block = vm(group, ext_h * (ext_a + 2 * PAD), radial)
        out = list(call(
            functools.partial(apply_step, dims, columns, group, first, last, 2 * step),
            outs, *args,
            scratch=[
                block, block, block, vm(group, (height + 2) * 3 * half, radial),
                vm(group, 2, angles, radial), vm(2, columns, 8, radial),
            ],
        ))
        ws.append(out.pop(0))
        us.append(out.pop(0))
        if first:
            shared, out = out[:3], out[3:]
        if not last:
            sent, msg, side, out = out[0], out[1:3], out[3:5], out[5:]
        dots = out.pop(0)

    dots = lax.all_to_all(dots, ("ang", "hgt"), 0, 0, tiled=True)
    x, r = call(
        functools.partial(finish, columns, dims), [field] * 2, dots, *us, *ws, weight, winv,
        hbm_out=True,
        scratch=[
            vm(columns, cells, radial), vm(columns, cells, radial), vm(columns, 2 * ITERS + 1, 8, radial),
            pltpu.SemaphoreType.DMA((2, columns)),
        ],
    )
    return x.reshape(loads.shape), r.reshape(loads.shape)


def solution(mesh):
    in_specs = (
        P(None, None, "ang", "hgt", None),
        P("ang", "hgt", None),
        P("ang", "hgt", None),
        P(),
        P(),
    )
    out_specs = (P(None, None, "ang", "hgt", None), P(None, None, "ang", "hgt", None))
    return jax.shard_map(body, mesh=mesh, in_specs=in_specs, out_specs=out_specs, check_vma=False)
```

```python
import functools

import jax
import jax.numpy as jnp
from jax import lax
from jax.experimental import pallas as pl
from jax.experimental.pallas import tpu as pltpu
from jax.sharding import PartitionSpec as P

ITERS = 3
CSWEEPS = 4


SIGMA = 6.5
SPRING = 20.0
OMEGA = 0.8
LOAD = 3.0
SHIFT = 1.0
PAD = 8
LIMIT = 40 * 1024 * 1024


def f32(*shape):
    return jax.ShapeDtypeStruct(shape, jnp.float32)


def call(kernel, out_shape, *args, hbm=(), hbm_out=False, scratch=()):
    vmem = pl.BlockSpec(memory_space=pltpu.VMEM)
    outside = pl.BlockSpec(memory_space=pltpu.HBM)
    args = [pltpu.with_memory_space_constraint(v, pltpu.HBM) if i in hbm else v for i, v in enumerate(args)]
    return pl.pallas_call(
        kernel,
        out_shape=out_shape,
        in_specs=[outside if i in hbm else vmem for i in range(len(args))],
        out_specs=[outside if hbm_out else vmem] * len(out_shape),
        scratch_shapes=list(scratch),
        compiler_params=pltpu.CompilerParams(vmem_limit_bytes=LIMIT),
    )(*args)


def even(axis):
    return lax.rem(lax.axis_index(axis), 2) == 0


def radial_pair(v):
    lane = lax.broadcasted_iota(jnp.int32, v.shape, 1)
    last = v.shape[1] - 1
    inner = jnp.where(lane == 0, 0.0, pltpu.roll(v, 1, 1))
    return inner + jnp.where(lane == last, 0.0, pltpu.roll(v, last, 1))


def choose(test, one, two):
    return jnp.where(test, one, two), jnp.where(test, two, one)


def corner_rows(margin):
    pieces, at = [], 0
    for side in range(2):
        for d in range(1, margin):
            pieces.append((side, d, margin - d, at))
            at += margin - d
    return pieces, at


def send(c, coarse, bottom, top, low, high, dims, evens, out):
    margin, own, half = dims
    even_a, even_h = evens
    sent, msg_a, msg_b, side_a, side_b = out
    for k, g in enumerate(coarse):
        sent[c, pl.ds(k * half, half), :] = g
        rows = pl.ds(k * margin, margin)
        side_a[c, rows, :], side_b[c, rows, :] = choose(even_a, g[half - margin:], g[:margin])
    for d in range(1, margin):
        rows = pl.ds((d - 1) * half, half)
        msg_a[c, rows, :], msg_b[c, rows, :] = choose(even_h, coarse[own - d], coarse[d - 1])
    rows = pl.ds((margin - 1) * half, 2 * half)
    msg_a[c, rows, :], msg_b[c, rows, :] = choose(even_h, top, bottom)
    rows = pl.ds(own * margin, 2 * own)
    side_a[c, rows, :], side_b[c, rows, :] = choose(even_a, high, low)


def send_field(c, field, q, q_ends, fold, weight, pre, dims, evens, out):
    margin, own, half = dims
    angles, height = 2 * half, 2 * own
    part = lambda ref, h, p: ref[pl.ds(h * angles + p * half, half), :]
    coarse = []
    for k in range(own):
        total = sum(part(weight, h, p) * part(field, h, p) for h in (2 * k, 2 * k + 1) for p in range(2))
        coarse.append(pre[k] * total)
    faces = []
    for s, (h, far) in enumerate(((0, margin - 1), (height - 1, own - margin))):
        faces.append(jnp.concatenate([
            part(q, h, p) * part(field, h, p) + part(fold.at[s], 0, p) * coarse[far] for p in range(2)
        ]))
    ends = [q_ends[s] * field[pl.ds(a, height, stride=angles), :] for s, a in enumerate((0, angles - 1))]
    send(c, coarse, *faces, *ends, dims, evens, out)


def prepare(cases, comps, levels, n_ang, dims, *refs):
    refs = list(refs)
    take = lambda n: [refs.pop(0) for _ in range(n)]
    loads_far, material_far, support_far, modulus_far, positions_far = take(5)
    u, = take(1)
    out = take(5)
    delta, q, beta, weight, winv, pre, q_ends, fold = take(8)
    loads, material, support, modulus, positions, sems, small = take(7)
    margin, own, half = dims
    columns = cases * comps
    height, angles = 2 * own, 2 * half
    radial = u.shape[-1]
    evens = even("ang"), even("hgt")
    early = [
        pltpu.make_async_copy(far, near, small.at[i])
        for i, (far, near) in enumerate((
            (material_far, material), (support_far, support), (modulus_far, modulus), (positions_far, positions),
        ))
    ]
    for copy in early:
        copy.start()
    for c in range(columns):
        pltpu.make_async_copy(loads_far.at[c], loads.at[c], sems.at[c]).start()
    for copy in early:
        copy.wait()
    wide, stiffen = [], []
    for h in range(height):
        for p in range(2):
            rows = pl.ds(p * height + h, half, stride=2 * height)
            level = material[rows, :]
            stiff = jnp.zeros(level.shape, jnp.float32)
            for n in range(levels):
                stiff = jnp.where(level == n, modulus[n], stiff)
            w = jnp.sqrt(stiff)
            s = support[rows, :].astype(jnp.float32)
            d = SIGMA + SPRING * s / stiff
            line = pl.ds(h * angles + p * half, half)
            weight[line, :] = w
            winv[line, :] = 1.0 / w
            delta[line, :] = d
            q[line, :] = OMEGA / d
            wide.append(w)
            stiffen.append(s)
    kappa = []
    for k in range(own):
        four = slice(4 * k, 4 * k + 4)
        wc, sc = 0.25 * sum(wide[four]), 0.25 * sum(stiffen[four])
        dc = SIGMA * wc * wc + SPRING * sc
        pre[k] = 0.5 * OMEGA * wc / dc
        kappa.append(OMEGA * wc * wc / dc)
        for i in range(4 * k, 4 * k + 4):
            beta[pl.ds(i * half, half), :] = 0.5 / wc * wide[i]
    faces = [beta[pl.ds(h * angles, angles), :] for h in (0, height - 1)]
    for s in range(2):
        path = 1.0
        for d in range(margin - 1):
            path = path * kappa[d if s == 0 else own - 1 - d]
        fold[s] = faces[s] * jnp.concatenate([path, path])
    ends = []
    for s, a in enumerate((0, angles - 1)):
        rows = pl.ds(a, height, stride=angles)
        q_ends[s] = q[rows, :]
        ends.append(beta[rows, :])
    send(columns, kappa, *faces, *ends, dims, evens, out)
    where = lax.axis_index("ang") * angles + 2 * lax.broadcasted_iota(jnp.int32, (half, radial), 0)

    @pl.loop(0, columns)
    def _(c):
        pltpu.make_async_copy(loads_far.at[c], loads.at[c], sems.at[c]).wait()
        for p in range(2):
            apart = jnp.abs(where + p - positions[lax.div(c, comps)])
            hit = jnp.minimum(apart, angles * n_ang - apart) < angles
            push = jnp.where(hit & (lax.rem(c, comps) == 2), -LOAD, 0.0)
            for h in range(height):
                line = pl.ds(h * angles + p * half, half)
                rows = pl.ds(p * height + h, half, stride=2 * height)
                u[c, line, :] = winv[line, :] * (loads[c, rows, :] + push)
        send_field(c, u.at[c], q, q_ends, fold, weight, pre, dims, evens, out)


def corner_messages(dims, count, side_a, side_b, out_a, out_b):
    margin, own, half = dims
    pieces, rows = corner_rows(margin)
    even_a, even_h = even("ang"), even("hgt")
    for c in range(count):
        slab, base = c // 2, (c % 2) * rows
        for s, d, n, at in pieces:
            def piece(k):
                first = k * margin + (margin - n if s == 0 else 0)
                a, b = side_a[c, pl.ds(first, n), :], side_b[c, pl.ds(first, n), :]
                return jnp.where(even_a, b, a) if s == 0 else jnp.where(even_a, a, b)
            to = pl.ds(base + at, n)
            out_a[slab, to, :], out_b[slab, to, :] = choose(even_h, piece(own - d), piece(d - 1))


def apply_step(dims, columns, group, first, last, dot_at, *refs):
    refs = list(refs)
    take = lambda n: [refs.pop(0) for _ in range(n)]
    u, sent = take(2)
    far, side, corner = take(2), take(2), take(2)
    dots_in, delta, q, beta, weight, pre, q_ends, fold = take(8)
    kx, edge_b, ends_b = take(3) if not first else (None,) * 3
    w, un = take(2)
    if first:
        kx, edge_b, ends_b = take(3)
    if not last:
        out = take(5)
    dots, = take(1)
    gx, va, vb, zx, edge, sums = take(6)
    margin, own, half = dims
    height, angles = 2 * own, 2 * half
    radial = u.shape[-1]
    even_a, even_h = evens = even("ang"), even("hgt")
    ext_h, ext_a = own + 2 * margin, half + 2 * margin
    pitch = ext_a + 2 * PAD
    line_pitch = 3 * half
    start = PAD + margin
    coarse = lambda h, shift=0: pl.ds(h * pitch + PAD + shift, ext_a)
    inner = lambda h: pl.ds(h * pitch + start, half)
    pieces, corner_length = corner_rows(margin)

    def assemble(c, slab, base, lane, put_faces):
        field = gx.at[lane]
        for k in range(own):
            field[inner(margin + k), :] = sent[c, pl.ds(k * half, half), :]
            rows = pl.ds(k * margin, margin)
            high, low = choose(even_a, side[0][c, rows, :], side[1][c, rows, :])
            field[pl.ds((margin + k) * pitch + start - margin, margin), :] = low
            field[pl.ds((margin + k) * pitch + start + half, margin), :] = high
        for d in range(1, margin):
            rows = pl.ds((d - 1) * half, half)
            up, down = choose(even_h, far[0][c, rows, :], far[1][c, rows, :])
            field[inner(margin + own - 1 + d), :] = up
            field[inner(margin - d), :] = down
        rows = pl.ds((margin - 1) * half, angles)
        up, down = choose(even_h, far[0][c, rows, :], far[1][c, rows, :])
        put_faces(down, up)
        for s, d, n, at in pieces:
            rows = pl.ds(base + at, n)
            up, down = choose(even_h, corner[0][slab, rows, :], corner[1][slab, rows, :])
            to = start - n if s == 0 else start + half
            field[pl.ds((margin + own - 1 + d) * pitch + to, n), :] = up
            field[pl.ds((margin - d) * pitch + to, n), :] = down

    def angular_ends(c, odd):
        rows = pl.ds(own * margin + odd, own, stride=2)
        return reversed(choose(even_a, side[0][c, rows, :], side[1][c, rows, :]))

    for lane in range(group):
        for h in (0, ext_h - 1):
            gx[lane, coarse(h), :] = jnp.zeros((ext_a, radial), jnp.float32)

    if first:
        def keep(down, up):
            edge_b[0], edge_b[1] = down, up
        assemble(columns, columns // 2, (columns % 2) * corner_length, 0, keep)
        for h in range(1, ext_h - 1):
            kx[h] = gx[0, coarse(h), :]
        for odd in range(2):
            for s, end in enumerate(angular_ends(columns, odd)):
                ends_b[s, odd] = end

    def run(first_column, slab_of):
        lanes = range(group)
        at = [first_column + lane for lane in lanes]
        for lane in lanes:
            def keep(down, up, lane=lane):
                edge[lane, 0], edge[lane, 1] = down, up
            assemble(at[lane], *slab_of(lane), lane, keep)
        source, target = gx, va
        for sweep in range(1, CSWEEPS):
            lo, hi = sweep, ext_h - sweep
            below = [source[n, coarse(lo - 1), :] for n in lanes]
            here = [source[n, coarse(lo), :] for n in lanes]
            for h in range(lo, hi):
                k = kx[h]
                for n in lanes:
                    above = source[n, coarse(h + 1), :]
                    near = below[n] + above + source[n, coarse(h, -1), :] + source[n, coarse(h, 1), :]
                    near = near + radial_pair(here[n])
                    target[n, coarse(h), :] = gx[n, coarse(h), :] + (1.0 - OMEGA) * here[n] + k * near
                    below[n], here[n] = here[n], above
            source, target = target, (vb if target is va else va)
        dot_uw = [jnp.zeros((half, radial), jnp.float32) for _ in lanes]
        dot_aw = [jnp.zeros((half, radial), jnp.float32) for _ in lanes]
        place = lambda h, p, shift=0: pl.ds((h + 1) * line_pitch + 2 * p * half + shift, half)
        for k in range(own):
            e = [source[n, inner(margin + k), :] for n in lanes]
            for h in (2 * k, 2 * k + 1):
                for p in range(2):
                    line = pl.ds(h * angles + p * half, half)
                    qs, bs = q[line, :], beta[line, :]
                    for n in lanes:
                        here = u[at[n], line, :]
                        z = qs * here + bs * e[n]
                        zx[n, place(h, p), :] = z
                        w[at[n], line, :] = z
                        dot_uw[n] = dot_uw[n] + here * z
        for n in lanes:
            for s, (h, k) in enumerate(((-1, margin - 1), (height, margin + own))):
                e = source[n, inner(k), :]
                for p in range(2):
                    rows = pl.ds(p * half, half)
                    zx[n, place(h, p), :] = edge[n, s, rows, :] + edge_b[s, rows, :] * e
            for odd in range(2):
                for s, end in enumerate(angular_ends(at[n], odd)):
                    k = start - 1 if s == 0 else start + half
                    e = source[n, pl.ds(margin * pitch + k, own, stride=pitch), :]
                    put = 2 * half - 1 if s == 0 else half
                    zx[n, pl.ds((1 + odd) * line_pitch + put, own, stride=2 * line_pitch), :] = end + ends_b[s, odd] * e
        load = lambda n, h: [zx[n, place(h, p), :] for p in range(2)]
        below = [load(n, -1) for n in lanes]
        here = [load(n, 0) for n in lanes]
        for h in range(height):
            above = [load(n, h + 1) for n in lanes]
            for p in range(2):
                line = pl.ds(h * angles + p * half, half)
                d = delta[line, :]
                for n in lanes:
                    near = below[n][p] + above[n][p] + here[n][1 - p]
                    near = near + zx[n, place(h, 1 - p, 1 if p else -1), :]
                    near = near + radial_pair(here[n][p])
                    new = d * here[n][p] - near - SHIFT * u[at[n], line, :]
                    un[at[n], line, :] = new
                    dot_aw[n] = dot_aw[n] + new * here[n][p]
            below, here = here, above
        tile = lambda d: sum(d[i:i + 8] for i in range(0, half, 8))
        for n in lanes:
            sums[0, at[n]] = tile(dot_uw[n])
            sums[1, at[n]] = tile(dot_aw[n])
            if not last:
                send_field(at[n], un.at[at[n]], q, q_ends, fold, weight, pre, dims, evens, out)

    @pl.loop(0, columns // group)
    def _(i):
        slabs = group // 2
        run(group * i, lambda lane: (i * slabs + lane // 2, (lane % 2) * corner_length))

    lane = lax.broadcasted_iota(jnp.int32, (1, radial), 1)
    row = jnp.zeros((1, radial), jnp.float32)
    for m in range(2):
        for c in range(columns):
            total = jnp.sum(jnp.sum(sums[m, c], axis=0, keepdims=True), axis=1, keepdims=True)
            row = jnp.where(lane == (dot_at + m) * columns + c, total, row)
    dots[...] = dots_in[...] + jnp.broadcast_to(row, dots.shape)


def krylov(mu):
    def apply(p):
        out = [SHIFT * v for v in p] + [jnp.zeros_like(mu[0])]
        for i, v in enumerate(p):
            out[i + 1] = out[i + 1] + v
        return out

    def inner(a, b):
        total = 0.0
        for m in range(len(a) + len(b) - 1):
            part = sum(a[i] * b[m - i] for i in range(len(a)) if 0 <= m - i < len(b))
            total = total + part * mu[m]
        return total

    def plus(a, b, scale):
        out = []
        for i in range(max(len(a), len(b))):
            v = a[i] if i < len(a) else None
            s = scale * b[i] if i < len(b) else None
            out.append(v if s is None else s if v is None else v + s)
        return out

    r = [jnp.ones_like(mu[0])]
    p = r
    x = []
    rz = mu[0]
    for step in range(ITERS):
        image = apply(p)
        alpha = rz / inner(p, image)
        x = plus(x, p, alpha)
        r = plus(r, image, -alpha)
        if step + 1 < ITERS:
            new = inner(r, r)
            p = plus(r, p, new / rz)
            rz = new
    return x, r


def finish(columns, dims, *refs):
    refs = list(refs)
    dots = refs.pop(0)
    us = [refs.pop(0) for _ in range(ITERS + 1)]
    ws = [refs.pop(0) for _ in range(ITERS)]
    weight, winv, x_far, r_far, x_out, r_out, factors, sems = refs
    margin, own, half = dims
    height, angles = 2 * own, 2 * half
    radial = us[0].shape[-1]
    total = jnp.sum(dots[...], axis=0, keepdims=True)
    mu = [total if m == 0 else pltpu.roll(total, radial - m * columns, 1) for m in range(2 * ITERS)]
    xs, rs = krylov(mu)
    lane = lax.broadcasted_iota(jnp.int32, (1, radial), 1)
    for c in range(columns):
        for j, v in enumerate(xs + rs):
            one = jnp.sum(jnp.where(lane == c, v, 0.0), axis=1, keepdims=True)
            factors[c, j] = jnp.broadcast_to(one, (8, radial))

    copies = lambda c: [
        pltpu.make_async_copy(near.at[c], far.at[c], sems.at[i, c])
        for i, (near, far) in enumerate(((x_out, x_far), (r_out, r_far)))
    ]

    @pl.loop(0, columns)
    def _(c):
        full = [jnp.concatenate([factors[c, j]] * (half // 8)) for j in range(2 * ITERS + 1)]
        xc, rc = full[:ITERS], full[ITERS:]
        for h in range(height):
            for p in range(2):
                line = pl.ds(h * angles + p * half, half)
                rows = pl.ds(p * height + h, half, stride=2 * height)
                x_out[c, rows, :] = winv[line, :] * sum(k * w[c, line, :] for k, w in zip(xc, ws))
                r_out[c, rows, :] = weight[line, :] * sum(k * u[c, line, :] for k, u in zip(rc, us))
        for copy in copies(c):
            copy.start()

    @pl.loop(0, columns)
    def _(c):
        for copy in copies(c):
            copy.wait()


def pairs(count, odd, periodic):
    found = []
    for i in range(odd, count, 2):
        j = i + 1
        if j < count or periodic:
            found += [(i, j % count), (j % count, i)]
    return found


def body(loads, material, support, modulus, positions):
    cases, comps, angles, height, radial = loads.shape
    columns = cases * comps
    margin = CSWEEPS
    own, half = height // 2, angles // 2
    dims = (margin, own, half)
    n_ang, n_hgt = lax.axis_size("ang"), lax.axis_size("hgt")
    assert own >= margin and half >= margin and half % 8 == 0 and n_ang % 2 == 0
    assert 2 * ITERS * columns <= radial and columns % 4 == 0
    cells = height * angles
    field, coef = f32(columns, cells, radial), f32(cells, radial)
    rows_h, rows_a = (margin - 1) * half + angles, own * margin + height
    rows_c = corner_rows(margin)[1]
    vm = lambda *s: pltpu.VMEM(s, jnp.float32)
    message = lambda n: [f32(n, own * half, radial)] + [f32(n, rows_h, radial)] * 2 + [f32(n, rows_a, radial)] * 2

    out = list(call(
        functools.partial(prepare, cases, comps, modulus.shape[0], n_ang, dims),
        [field] + message(columns + 1) + [coef] * 5
        + [f32(own, half, radial), f32(2, height, radial), f32(2, angles, radial)],
        loads.reshape(columns, cells, radial), material.reshape(cells, radial), support.reshape(cells, radial),
        modulus, positions,
        hbm=range(5),
        scratch=[
            vm(columns, cells, radial), pltpu.VMEM((cells, radial), jnp.int32), pltpu.VMEM((cells, radial), jnp.int32),
            pltpu.SMEM(modulus.shape, jnp.float32), pltpu.SMEM(positions.shape, jnp.int32),
            pltpu.SemaphoreType.DMA((columns,)), pltpu.SemaphoreType.DMA((4,)),
        ],
    ))
    u, sent, msg, side = out[0], out[1], out[2:4], out[4:6]
    delta, q, beta, weight, winv, pre, q_ends, fold = out[6:]
    us, ws = [u], []
    dots = jnp.zeros((n_ang * n_hgt, radial), jnp.float32)
    shared = []
    group = 4
    for step in range(ITERS):
        first, last = step == 0, step + 1 == ITERS
        count = columns + 1 if first else columns
        slabs = (count + 1) // 2
        swap = lambda v, axis, wraps: [lax.ppermute(v[i], axis, pairs(lax.axis_size(axis), i, wraps)) for i in range(2)]
        far = swap(msg, "hgt", False)
        beside = swap(side, "ang", True)
        corner = call(
            functools.partial(corner_messages, dims, count), [f32(slabs, 2 * rows_c, radial)] * 2, *beside,
        )
        corner = swap(corner, "hgt", False)
        args = [us[-1], sent, *far, *beside, *corner, dots, delta, q, beta, weight, pre, q_ends, fold, *shared]
        outs = [field, field]
        ext_h, ext_a = own + 2 * margin, half + 2 * margin
        if first:
            outs += [f32(ext_h, ext_a, radial), f32(2, angles, radial), f32(2, 2, own, radial)]
        if not last:
            outs += message(columns)
        outs.append(f32(n_ang * n_hgt, radial))
        block = vm(group, ext_h * (ext_a + 2 * PAD), radial)
        out = list(call(
            functools.partial(apply_step, dims, columns, group, first, last, 2 * step),
            outs, *args,
            scratch=[
                block, block, block, vm(group, (height + 2) * 3 * half, radial),
                vm(group, 2, angles, radial), vm(2, columns, 8, radial),
            ],
        ))
        ws.append(out.pop(0))
        us.append(out.pop(0))
        if first:
            shared, out = out[:3], out[3:]
        if not last:
            sent, msg, side, out = out[0], out[1:3], out[3:5], out[5:]
        dots = out.pop(0)

    dots = lax.all_to_all(dots, ("ang", "hgt"), 0, 0, tiled=True)
    x, r = call(
        functools.partial(finish, columns, dims), [field] * 2, dots, *us, *ws, weight, winv,
        hbm_out=True,
        scratch=[
            vm(columns, cells, radial), vm(columns, cells, radial), vm(columns, 2 * ITERS + 1, 8, radial),
            pltpu.SemaphoreType.DMA((2, columns)),
        ],
    )
    return x.reshape(loads.shape), r.reshape(loads.shape)


def solution(mesh):
    in_specs = (
        P(None, None, "ang", "hgt", None),
        P("ang", "hgt", None),
        P("ang", "hgt", None),
        P(),
        P(),
    )
    out_specs = (P(None, None, "ang", "hgt", None), P(None, None, "ang", "hgt", None))
    return jax.shard_map(body, mesh=mesh, in_specs=in_specs, out_specs=out_specs, check_vma=False)
```

```python
import functools

import jax
import jax.numpy as jnp
from jax import lax
from jax.experimental import pallas as pl
from jax.experimental.pallas import tpu as pltpu
from jax.sharding import PartitionSpec as P

ITERS = 3
CSWEEPS = 4


SIGMA = 6.5
SPRING = 20.0
OMEGA = 0.8
LOAD = 3.0
SHIFT = 1.0
PAD = 8
GROWTH = 500.0
LIMIT = 24 * 1024 * 1024


def f32(*shape):
    return jax.ShapeDtypeStruct(shape, jnp.float32)


def call(kernel, out_shape, *args, hbm=(), hbm_out=(), scratch=()):
    vmem = pl.BlockSpec(memory_space=pltpu.VMEM)
    outside = pl.BlockSpec(memory_space=pltpu.HBM)
    args = [pltpu.with_memory_space_constraint(v, pltpu.HBM) if i in hbm else v for i, v in enumerate(args)]
    return pl.pallas_call(
        kernel,
        out_shape=out_shape,
        in_specs=[outside if i in hbm else vmem for i in range(len(args))],
        out_specs=[outside if i in hbm_out else vmem for i in range(len(out_shape))],
        scratch_shapes=list(scratch),
        compiler_params=pltpu.CompilerParams(vmem_limit_bytes=LIMIT),
    )(*args)


def even(axis):
    return lax.rem(lax.axis_index(axis), 2) == 0


def radial_pair(v):
    lane = lax.broadcasted_iota(jnp.int32, v.shape, 1)
    last = v.shape[1] - 1
    inner = jnp.where(lane == 0, 0.0, pltpu.roll(v, 1, 1))
    return inner + jnp.where(lane == last, 0.0, pltpu.roll(v, last, 1))


def choose(test, one, two):
    return jnp.where(test, one, two), jnp.where(test, two, one)


def corner_rows(margin):
    pieces, at = [], 0
    for side in range(2):
        for d in range(1, margin):
            pieces.append((side, d, margin - d, at))
            at += margin - d
    return pieces, at


def send(c, coarse, bottom, top, low, high, dims, evens, out):
    margin, own, half = dims
    even_a, even_h = evens
    sent, msg_a, msg_b, side_a, side_b = out
    for k, g in enumerate(coarse):
        sent[c, pl.ds(k * half, half), :] = g
        rows = pl.ds(k * margin, margin)
        side_a[c, rows, :], side_b[c, rows, :] = choose(even_a, g[half - margin:], g[:margin])
    for d in range(1, margin):
        rows = pl.ds((d - 1) * half, half)
        msg_a[c, rows, :], msg_b[c, rows, :] = choose(even_h, coarse[own - d], coarse[d - 1])
    rows = pl.ds((margin - 1) * half, 2 * half)
    msg_a[c, rows, :], msg_b[c, rows, :] = choose(even_h, top, bottom)
    rows = pl.ds(own * margin, 2 * own)
    side_a[c, rows, :], side_b[c, rows, :] = choose(even_a, high, low)


def send_field(c, field, q, q_ends, fold, weight, pre, dims, evens, out):
    margin, own, half = dims
    angles, height = 2 * half, 2 * own
    part = lambda ref, h, p: ref[pl.ds(h * angles + p * half, half), :]
    coarse = []
    for k in range(own):
        total = sum(part(weight, h, p) * part(field, h, p) for h in (2 * k, 2 * k + 1) for p in range(2))
        coarse.append(pre[k] * total)
    faces = []
    for s, (h, far) in enumerate(((0, margin - 1), (height - 1, own - margin))):
        faces.append(jnp.concatenate([
            part(q, h, p) * part(field, h, p) + part(fold.at[s], 0, p) * coarse[far] for p in range(2)
        ]))
    ends = [q_ends[s] * field[pl.ds(a, height, stride=angles), :] for s, a in enumerate((0, angles - 1))]
    send(c, coarse, *faces, *ends, dims, evens, out)


def prepare(cases, comps, levels, n_ang, dims, *refs):
    refs = list(refs)
    take = lambda n: [refs.pop(0) for _ in range(n)]
    loads_far, material_far, support_far, modulus_far, positions_far = take(5)
    u, = take(1)
    out = take(5)
    delta, q, beta, weight, winv, pre, q_ends, fold = take(8)
    loads, material, support, modulus, positions, sems = take(6)
    margin, own, half = dims
    columns = cases * comps
    height, angles = 2 * own, 2 * half
    radial = u.shape[-1]
    evens = even("ang"), even("hgt")
    copies = [
        pltpu.make_async_copy(far, near, sems.at[i])
        for i, (far, near) in enumerate((
            (modulus_far, modulus), (material_far, material), (support_far, support), (positions_far, positions),
        ))
    ]
    for copy in copies:
        copy.start()
    thirds = columns // 3
    fetch = lambda c, i: pltpu.make_async_copy(loads_far.at[pl.ds(c, thirds)], loads.at[pl.ds(c, thirds)], sems.at[i])
    for i in range(3):
        fetch(i * thirds, 4 + i).start()
    for copy in copies:
        copy.wait()
    wide, stiffen = [], []
    for h in range(height):
        for p in range(2):
            rows = pl.ds(p * height + h, half, stride=2 * height)
            level = material[rows, :]
            stiff = jnp.zeros(level.shape, jnp.float32)
            for n in range(levels):
                stiff = jnp.where(level == n, modulus[n], stiff)
            w = jnp.sqrt(stiff)
            s = support[rows, :].astype(jnp.float32)
            d = SIGMA + SPRING * s / stiff
            line = pl.ds(h * angles + p * half, half)
            weight[line, :] = w
            winv[line, :] = 1.0 / w
            delta[line, :] = d
            q[line, :] = OMEGA / d
            wide.append(w)
            stiffen.append(s)
    kappa = []
    for k in range(own):
        four = slice(4 * k, 4 * k + 4)
        wc, sc = 0.25 * sum(wide[four]), 0.25 * sum(stiffen[four])
        dc = SIGMA * wc * wc + SPRING * sc
        pre[k] = 0.5 * OMEGA * wc / dc
        kappa.append(OMEGA * wc * wc / dc)
        for i in range(4 * k, 4 * k + 4):
            beta[pl.ds(i * half, half), :] = 0.5 / wc * wide[i]
    faces = [beta[pl.ds(h * angles, angles), :] for h in (0, height - 1)]
    for s in range(2):
        path = 1.0
        for d in range(margin - 1):
            path = path * kappa[d if s == 0 else own - 1 - d]
        fold[s] = faces[s] * jnp.concatenate([path, path])
    ends = []
    for s, a in enumerate((0, angles - 1)):
        rows = pl.ds(a, height, stride=angles)
        q_ends[s] = q[rows, :]
        ends.append(beta[rows, :])
    send(columns, kappa, *faces, *ends, dims, evens, out)
    where = lax.axis_index("ang") * angles + 2 * lax.broadcasted_iota(jnp.int32, (half, radial), 0)

    @pl.loop(0, columns)
    def _(c):
        @pl.when(lax.rem(c, thirds) == 0)
        def _():
            fetch(c, 4 + lax.div(c, thirds)).wait()

        for p in range(2):
            apart = jnp.abs(where + p - positions[lax.div(c, comps)])
            hit = jnp.minimum(apart, angles * n_ang - apart) < angles
            push = jnp.where(hit & (lax.rem(c, comps) == 2), -LOAD, 0.0)
            for h in range(height):
                line = pl.ds(h * angles + p * half, half)
                rows = pl.ds(p * height + h, half, stride=2 * height)
                u[c, line, :] = winv[line, :] * (loads[c, rows, :] + push)
        send_field(c, u.at[c], q, q_ends, fold, weight, pre, dims, evens, out)


def corner_messages(dims, count, side_a, side_b, out_a, out_b):
    margin, own, half = dims
    pieces, rows = corner_rows(margin)
    even_a, even_h = even("ang"), even("hgt")
    for c in range(count):
        slab, base = c // 2, (c % 2) * rows
        for s, d, n, at in pieces:
            def piece(k):
                first = k * margin + (margin - n if s == 0 else 0)
                a, b = side_a[c, pl.ds(first, n), :], side_b[c, pl.ds(first, n), :]
                return jnp.where(even_a, b, a) if s == 0 else jnp.where(even_a, a, b)
            to = pl.ds(base + at, n)
            out_a[slab, to, :], out_b[slab, to, :] = choose(even_h, piece(own - d), piece(d - 1))


def apply_step(dims, columns, group, first, last, dot_at, *refs):
    refs = list(refs)
    take = lambda n: [refs.pop(0) for _ in range(n)]
    u, sent = take(2)
    far, side, corner = take(2), take(2), take(2)
    dots_in, delta, q, beta, weight, pre, q_ends, fold = take(8)
    kx, edge_b, ends_b = take(3) if not first else (None,) * 3
    w, un = take(2)
    if first:
        kx, edge_b, ends_b = take(3)
    if not last:
        out = take(5)
    dots, = take(1)
    gx, va, vb, zx, edge, sums = take(6)
    margin, own, half = dims
    height, angles = 2 * own, 2 * half
    radial = u.shape[-1]
    even_a, even_h = evens = even("ang"), even("hgt")
    ext_h, ext_a = own + 2 * margin, half + 2 * margin
    pitch = ext_a + 2 * PAD
    line_pitch = 3 * half
    start = PAD + margin
    coarse = lambda h, shift=0: pl.ds(h * pitch + PAD + shift, ext_a)
    inner = lambda h: pl.ds(h * pitch + start, half)
    pieces, corner_length = corner_rows(margin)

    def assemble(c, slab, base, lane, put_faces):
        field = gx.at[lane]
        for k in range(own):
            field[inner(margin + k), :] = sent[c, pl.ds(k * half, half), :]
            rows = pl.ds(k * margin, margin)
            high, low = choose(even_a, side[0][c, rows, :], side[1][c, rows, :])
            field[pl.ds((margin + k) * pitch + start - margin, margin), :] = low
            field[pl.ds((margin + k) * pitch + start + half, margin), :] = high
        for d in range(1, margin):
            rows = pl.ds((d - 1) * half, half)
            up, down = choose(even_h, far[0][c, rows, :], far[1][c, rows, :])
            field[inner(margin + own - 1 + d), :] = up
            field[inner(margin - d), :] = down
        rows = pl.ds((margin - 1) * half, angles)
        up, down = choose(even_h, far[0][c, rows, :], far[1][c, rows, :])
        put_faces(down, up)
        for s, d, n, at in pieces:
            rows = pl.ds(base + at, n)
            up, down = choose(even_h, corner[0][slab, rows, :], corner[1][slab, rows, :])
            to = start - n if s == 0 else start + half
            field[pl.ds((margin + own - 1 + d) * pitch + to, n), :] = up
            field[pl.ds((margin - d) * pitch + to, n), :] = down

    def angular_ends(c, odd):
        rows = pl.ds(own * margin + odd, own, stride=2)
        return reversed(choose(even_a, side[0][c, rows, :], side[1][c, rows, :]))

    for lane in range(group):
        for h in (0, ext_h - 1):
            gx[lane, coarse(h), :] = jnp.zeros((ext_a, radial), jnp.float32)

    if first:
        def keep(down, up):
            edge_b[0], edge_b[1] = down, up
        assemble(columns, columns // 2, (columns % 2) * corner_length, 0, keep)
        for h in range(1, ext_h - 1):
            kx[h] = gx[0, coarse(h), :]
        for odd in range(2):
            for s, end in enumerate(angular_ends(columns, odd)):
                ends_b[s, odd] = end

    def run(first_column, slab_of):
        lanes = range(group)
        at = [first_column + lane for lane in lanes]
        for lane in lanes:
            def keep(down, up, lane=lane):
                edge[lane, 0], edge[lane, 1] = down, up
            assemble(at[lane], *slab_of(lane), lane, keep)
        source, target = gx, va
        for sweep in range(1, CSWEEPS):
            lo, hi = sweep, ext_h - sweep
            below = [source[n, coarse(lo - 1), :] for n in lanes]
            here = [source[n, coarse(lo), :] for n in lanes]
            for h in range(lo, hi):
                k = kx[h]
                for n in lanes:
                    above = source[n, coarse(h + 1), :]
                    near = below[n] + above + source[n, coarse(h, -1), :] + source[n, coarse(h, 1), :]
                    near = near + radial_pair(here[n])
                    target[n, coarse(h), :] = gx[n, coarse(h), :] + (1.0 - OMEGA) * here[n] + k * near
                    below[n], here[n] = here[n], above
            source, target = target, (vb if target is va else va)
        dot_uw = [jnp.zeros((half, radial), jnp.float32) for _ in lanes]
        dot_aw = [jnp.zeros((half, radial), jnp.float32) for _ in lanes]
        place = lambda h, p, shift=0: pl.ds((h + 1) * line_pitch + 2 * p * half + shift, half)
        for k in range(own):
            e = [source[n, inner(margin + k), :] for n in lanes]
            for h in (2 * k, 2 * k + 1):
                for p in range(2):
                    line = pl.ds(h * angles + p * half, half)
                    qs, bs = q[line, :], beta[line, :]
                    for n in lanes:
                        here = u[at[n], line, :]
                        z = qs * here + bs * e[n]
                        zx[n, place(h, p), :] = z
                        w[at[n], line, :] = z
                        dot_uw[n] = dot_uw[n] + here * z
        for n in lanes:
            for s, (h, k) in enumerate(((-1, margin - 1), (height, margin + own))):
                e = source[n, inner(k), :]
                for p in range(2):
                    rows = pl.ds(p * half, half)
                    zx[n, place(h, p), :] = edge[n, s, rows, :] + edge_b[s, rows, :] * e
            for odd in range(2):
                for s, end in enumerate(angular_ends(at[n], odd)):
                    k = start - 1 if s == 0 else start + half
                    e = source[n, pl.ds(margin * pitch + k, own, stride=pitch), :]
                    put = 2 * half - 1 if s == 0 else half
                    zx[n, pl.ds((1 + odd) * line_pitch + put, own, stride=2 * line_pitch), :] = end + ends_b[s, odd] * e
        load = lambda n, h: [zx[n, place(h, p), :] for p in range(2)]
        below = [load(n, -1) for n in lanes]
        here = [load(n, 0) for n in lanes]
        for h in range(height):
            above = [load(n, h + 1) for n in lanes]
            for p in range(2):
                line = pl.ds(h * angles + p * half, half)
                d = delta[line, :]
                for n in lanes:
                    near = below[n][p] + above[n][p] + here[n][1 - p]
                    near = near + zx[n, place(h, 1 - p, 1 if p else -1), :]
                    near = near + radial_pair(here[n][p])
                    new = d * here[n][p] - near - SHIFT * u[at[n], line, :]
                    un[at[n], line, :] = new
                    dot_aw[n] = dot_aw[n] + new * here[n][p]
            below, here = here, above
        tile = lambda d: sum(d[i:i + 8] for i in range(0, half, 8))
        for n in lanes:
            for m, dot in enumerate((dot_uw[n], dot_aw[n])):
                sums[pl.ds(pl.multiple_of((m * columns + at[n]) * 8, 8), 8), :] = tile(dot)
            if not last:
                send_field(at[n], un.at[at[n]], q, q_ends, fold, weight, pre, dims, evens, out)

    @pl.loop(0, columns // group)
    def _(i):
        slabs = group // 2
        run(group * i, lambda lane: (i * slabs + lane // 2, (lane % 2) * corner_length))

    count = 2 * columns
    total = sum(sums[pl.ds(r, count, stride=8), :] for r in range(8))
    total = jnp.sum(total, axis=1, keepdims=True)
    lane = lax.broadcasted_iota(jnp.int32, (count, radial), 1)
    item = lax.broadcasted_iota(jnp.int32, (count, radial), 0)
    row = jnp.sum(jnp.where(lane == dot_at * columns + item, total, 0.0), axis=0, keepdims=True)
    dots[...] = dots_in[...] + jnp.broadcast_to(row, dots.shape)


def krylov(mu):
    sound = []

    def apply(p):
        out = [SHIFT * v for v in p] + [jnp.zeros_like(mu[0])]
        for i, v in enumerate(p):
            out[i + 1] = out[i + 1] + v
        return out

    def inner(a, b):
        total, size = 0.0, 0.0
        for m in range(len(a) + len(b) - 1):
            terms = [a[i] * b[m - i] for i in range(len(a)) if 0 <= m - i < len(b)]
            total = total + sum(terms) * mu[m]
            size = size + sum(jnp.abs(v) for v in terms) * jnp.abs(mu[m])
        sound.append(size <= GROWTH * jnp.abs(total))
        return total

    def plus(a, b, scale):
        out = []
        for i in range(max(len(a), len(b))):
            v = a[i] if i < len(a) else None
            s = scale * b[i] if i < len(b) else None
            out.append(v if s is None else s if v is None else v + s)
        return out

    r = [jnp.ones_like(mu[0])]
    p = r
    x = []
    rz = mu[0]
    for step in range(ITERS):
        image = apply(p)
        alpha = rz / inner(p, image)
        x = plus(x, p, alpha)
        r = plus(r, image, -alpha)
        if step + 1 < ITERS:
            new = inner(r, r)
            p = plus(r, p, new / rz)
            rz = new
    return x, r, functools.reduce(jnp.logical_and, sound)


def finish(columns, group, dims, *refs):
    refs = list(refs)
    dots = refs.pop(0)
    us = [refs.pop(0) for _ in range(ITERS + 1)]
    ws = [refs.pop(0) for _ in range(ITERS)]
    weight, winv, x_far, r_far, trouble, x_out, r_out, factors, sems = refs
    margin, own, half = dims
    height, angles = 2 * own, 2 * half
    radial = us[0].shape[-1]
    total = jnp.sum(dots[...], axis=0, keepdims=True)
    spread = factors.shape[1], radial
    lane = lax.broadcasted_iota(jnp.int32, spread, 1)
    item = lax.broadcasted_iota(jnp.int32, spread, 0)
    mu = [
        jnp.broadcast_to(jnp.sum(jnp.where(lane == m * columns + item, total, 0.0), axis=1, keepdims=True), spread)
        for m in range(2 * ITERS)
    ]
    xs, rs, sound = krylov(mu)
    trouble[...] = jnp.max(jnp.where(sound | (item >= columns), 0.0, 1.0), axis=0, keepdims=True)
    for j, v in enumerate(xs + rs):
        factors[j] = v

    copies = lambda c, n: [
        pltpu.make_async_copy(near.at[pl.ds(c, n)], far.at[pl.ds(c, n)], sems.at[i])
        for i, (near, far) in enumerate(((x_out, x_far), (r_out, r_far)))
    ]

    @pl.loop(0, columns // group)
    def _(i):
        for n in range(group):
            c = group * i + n
            full = [jnp.broadcast_to(factors[j, pl.ds(c, 1), :], (half, radial)) for j in range(2 * ITERS + 1)]
            xc, rc = full[:ITERS], full[ITERS:]
            for h in range(height):
                for p in range(2):
                    line = pl.ds(h * angles + p * half, half)
                    rows = pl.ds(p * height + h, half, stride=2 * height)
                    x_out[c, rows, :] = winv[line, :] * sum(k * w[c, line, :] for k, w in zip(xc, ws))
                    r_out[c, rows, :] = weight[line, :] * sum(k * u[c, line, :] for k, u in zip(rc, us))
        for copy in copies(group * i, group):
            copy.start()

    for copy in copies(0, columns):
        copy.wait()


def pairs(count, odd, periodic):
    found = []
    for i in range(odd, count, 2):
        j = i + 1
        if j < count or periodic:
            found += [(i, j % count), (j % count, i)]
    return found


def padded_2(block, sides, width, periodic):
    for axis, dim in sides:
        count = lax.axis_size(axis)
        forward = [(i, i + 1) for i in range(count - 1)]
        if periodic:
            forward.append((count - 1, 0))
        backward = [(target, source) for source, target in forward]
        low = lax.ppermute(
            lax.slice_in_dim(block, block.shape[dim] - width, None, axis=dim), axis, forward
        )
        high = lax.ppermute(lax.slice_in_dim(block, 0, width, axis=dim), axis, backward)
        block = jnp.concatenate([low, block, high], axis=dim)
    return block


def zero_pair(v, axis):
    widths = [(0, 0)] * v.ndim
    widths[axis] = (1, 1)
    padded = jnp.pad(v, widths)
    size = v.shape[axis]
    return lax.slice_in_dim(padded, 2, size + 2, axis=axis) + lax.slice_in_dim(
        padded, 0, size, axis=axis
    )


def fine_apply(u, weight, spring):
    v = weight * u
    beside_all = padded_2(v, (("ang", 2),), 1, True)
    above = padded_2(v, (("hgt", 3),), 1, False)
    beside = beside_all[:, :, 2:] + beside_all[:, :, :-2] + above[:, :, :, 2:] + above[:, :, :, :-2]
    beside = beside + zero_pair(v, 4)
    return weight * (SIGMA * v - beside) + SPRING * spring * u


def padded_apply(u, weight, spring):
    v = weight * u
    beside = zero_pair(v, 2) + zero_pair(v, 3) + zero_pair(v, 4)
    return weight * (SIGMA * v - beside) + SPRING * spring * u


def coarsen(field):
    a, h, r = field.shape
    return field.reshape(a // 2, 2, h // 2, 2, r).mean(axis=(1, 3))


def restrict(r):
    c, k, a, h, n = r.shape
    return r.reshape(c, k, a // 2, 2, h // 2, 2, n).sum(axis=(3, 5)) * 0.5


def prolong(e):
    return jnp.repeat(jnp.repeat(e, 2, axis=2), 2, axis=3) * 0.5


def step_by_step(loads, material, support, modulus, positions):
    cases, comps, a_dev, h_dev, radial = loads.shape
    margin = CSWEEPS - 1
    levels = lax.iota(jnp.int32, modulus.shape[0])
    stiff = jnp.sum(
        jnp.where(material[None] == levels[:, None, None, None], modulus[:, None, None, None], 0.0),
        axis=0,
    )
    weight = jnp.sqrt(stiff)
    spring = support.astype(jnp.float32)
    diag = SIGMA * weight * weight + SPRING * spring
    wide_c = coarsen(weight)
    spring_c = coarsen(spring)
    coef = jnp.stack((wide_c, spring_c))
    coef = padded_2(coef, (("ang", 1),), margin, True)
    coef = padded_2(coef, (("hgt", 2),), margin, False)
    wide_p = coef[0]
    spring_p = coef[1]
    diag_raw = SIGMA * wide_p * wide_p + SPRING * spring_p
    diag_p = jnp.where(diag_raw > 0.0, diag_raw, 1.0)
    total_angles = a_dev * lax.axis_size("ang")
    angles = lax.axis_index("ang") * a_dev + lax.iota(jnp.int32, a_dev)
    apart = jnp.abs(angles[None, :] - positions[:, None])
    cycle_dist = jnp.minimum(apart, total_angles - apart)
    hit = jnp.where(cycle_dist < a_dev, -LOAD, 0.0)
    select = jnp.where(lax.iota(jnp.int32, comps) == 2, 1.0, 0.0)
    right = loads + hit[:, None, :, None, None] * select[None, :, None, None, None]

    def precondition(r):
        coarse_rhs = restrict(r)
        wider = padded_2(coarse_rhs, (("ang", 2),), margin, True)
        wider = padded_2(wider, (("hgt", 3),), margin, False)
        err = OMEGA * wider / diag_p
        for sweep in range(CSWEEPS - 1):
            err = err + OMEGA * (wider - padded_apply(err, wide_p, spring_p)) / diag_p
        err = err[:, :, margin : err.shape[2] - margin, margin : err.shape[3] - margin]
        return OMEGA * r / diag + prolong(err)

    def projection(a, b):
        return lax.psum(jnp.sum(a * b, axis=(2, 3, 4)), ("ang", "hgt"))[:, :, None, None, None]

    solution_field = jnp.zeros_like(right)
    residual = right
    precond = precondition(residual)
    direction = precond
    rz_now = projection(residual, precond)
    for step in range(ITERS):
        image = fine_apply(direction, weight, spring)
        curve = lax.psum(jnp.sum(direction * image, axis=(2, 3, 4)), ("ang", "hgt"))
        alpha = rz_now / curve[:, :, None, None, None]
        solution_field = solution_field + alpha * direction
        residual = residual - alpha * image
        if step + 1 < ITERS:
            precond = precondition(residual)
            rz_next = projection(residual, precond)
            direction = precond + rz_next / rz_now * direction
            rz_now = rz_next
    return (solution_field, residual)


def body(loads, material, support, modulus, positions):
    cases, comps, angles, height, radial = loads.shape
    columns = cases * comps
    margin = CSWEEPS
    own, half = height // 2, angles // 2
    dims = (margin, own, half)
    n_ang, n_hgt = lax.axis_size("ang"), lax.axis_size("hgt")
    assert own >= margin and half >= margin and half % 8 == 0 and n_ang % 2 == 0
    assert 2 * ITERS * columns <= radial and columns % 12 == 0
    cells = height * angles
    field, coef = f32(columns, cells, radial), f32(cells, radial)
    rows_h, rows_a = (margin - 1) * half + angles, own * margin + height
    rows_c = corner_rows(margin)[1]
    vm = lambda *s: pltpu.VMEM(s, jnp.float32)
    message = lambda n: [f32(n, own * half, radial)] + [f32(n, rows_h, radial)] * 2 + [f32(n, rows_a, radial)] * 2

    out = list(call(
        functools.partial(prepare, cases, comps, modulus.shape[0], n_ang, dims),
        [field] + message(columns + 1) + [coef] * 5
        + [f32(own, half, radial), f32(2, height, radial), f32(2, angles, radial)],
        loads.reshape(columns, cells, radial), material.reshape(cells, radial), support.reshape(cells, radial),
        modulus, positions,
        hbm=range(5),
        scratch=[
            vm(columns, cells, radial), pltpu.VMEM((cells, radial), jnp.int32), pltpu.VMEM((cells, radial), jnp.int32),
            pltpu.SMEM(modulus.shape, jnp.float32), pltpu.SMEM(positions.shape, jnp.int32),
            pltpu.SemaphoreType.DMA((7,)),
        ],
    ))
    u, sent, msg, side = out[0], out[1], out[2:4], out[4:6]
    delta, q, beta, weight, winv, pre, q_ends, fold = out[6:]
    us, ws = [u], []
    dots = jnp.zeros((n_ang * n_hgt, radial), jnp.float32)
    shared = []
    group = 4
    for step in range(ITERS):
        first, last = step == 0, step + 1 == ITERS
        count = columns + 1 if first else columns
        slabs = (count + 1) // 2
        swap = lambda v, axis, wraps: [lax.ppermute(v[i], axis, pairs(lax.axis_size(axis), i, wraps)) for i in range(2)]
        far = swap(msg, "hgt", False)
        beside = swap(side, "ang", True)
        corner = call(
            functools.partial(corner_messages, dims, count), [f32(slabs, 2 * rows_c, radial)] * 2, *beside,
        )
        corner = swap(corner, "hgt", False)
        args = [us[-1], sent, *far, *beside, *corner, dots, delta, q, beta, weight, pre, q_ends, fold, *shared]
        outs = [field, field]
        ext_h, ext_a = own + 2 * margin, half + 2 * margin
        if first:
            outs += [f32(ext_h, ext_a, radial), f32(2, angles, radial), f32(2, 2, own, radial)]
        if not last:
            outs += message(columns)
        outs.append(f32(n_ang * n_hgt, radial))
        block = vm(group, ext_h * (ext_a + 2 * PAD), radial)
        out = list(call(
            functools.partial(apply_step, dims, columns, group, first, last, 2 * step),
            outs, *args,
            scratch=[
                block, block, block, vm(group, (height + 2) * 3 * half, radial),
                vm(group, 2, angles, radial), vm(2 * columns * 8, radial),
            ],
        ))
        ws.append(out.pop(0))
        us.append(out.pop(0))
        if first:
            shared, out = out[:3], out[3:]
        if not last:
            sent, msg, side, out = out[0], out[1:3], out[3:5], out[5:]
        dots = out.pop(0)

    dots = lax.all_to_all(dots, ("ang", "hgt"), 0, 0, tiled=True)
    x, r, trouble = call(
        functools.partial(finish, columns, 2, dims), [field] * 2 + [f32(1, radial)], dots, *us, *ws, weight, winv,
        hbm_out=(0, 1),
        scratch=[
            vm(columns, cells, radial), vm(columns, cells, radial),
            vm(2 * ITERS + 1, -(-columns // 8) * 8, radial),
            pltpu.SemaphoreType.DMA((2,)),
        ],
    )
    x, r = x.reshape(loads.shape), r.reshape(loads.shape)

    def again(state):
        given = [jnp.where(state[0], v, jnp.zeros_like(v)) for v in (loads, material, support, modulus, positions)]
        return jnp.zeros_like(state[0]), *step_by_step(*given)

    return lax.while_loop(lambda state: state[0], again, (trouble[0, 0] > 0.0, x, r))[1:]


def solution(mesh):
    in_specs = (
        P(None, None, "ang", "hgt", None),
        P("ang", "hgt", None),
        P("ang", "hgt", None),
        P(),
        P(),
    )
    out_specs = (P(None, None, "ang", "hgt", None), P(None, None, "ang", "hgt", None))
    return jax.shard_map(body, mesh=mesh, in_specs=in_specs, out_specs=out_specs, check_vma=False)
```

```python
import functools

import jax
import jax.numpy as jnp
from jax import lax
from jax.experimental import pallas as pl
from jax.experimental.pallas import tpu as pltpu
from jax.sharding import PartitionSpec as P

ITERS = 3
CSWEEPS = 4


SIGMA = 6.5
SPRING = 20.0
OMEGA = 0.8
LOAD = 3.0
SHIFT = 1.0
PAD = 8
GROWTH = 500.0
LIMIT = 24 * 1024 * 1024


def f32(*shape):
    return jax.ShapeDtypeStruct(shape, jnp.float32)


def call(kernel, out_shape, *args, hbm=(), hbm_out=(), scratch=(), cost=None):
    vmem = pl.BlockSpec(memory_space=pltpu.VMEM)
    outside = pl.BlockSpec(memory_space=pltpu.HBM)
    args = [pltpu.with_memory_space_constraint(v, pltpu.HBM) if i in hbm else v for i, v in enumerate(args)]
    return pl.pallas_call(
        kernel,
        out_shape=out_shape,
        in_specs=[outside if i in hbm else vmem for i in range(len(args))],
        out_specs=[outside if i in hbm_out else vmem for i in range(len(out_shape))],
        scratch_shapes=list(scratch),
        cost_estimate=cost,
        compiler_params=pltpu.CompilerParams(vmem_limit_bytes=LIMIT),
    )(*args)


def even(axis):
    return lax.rem(lax.axis_index(axis), 2) == 0


def radial_pair(v):
    lane = lax.broadcasted_iota(jnp.int32, v.shape, 1)
    last = v.shape[1] - 1
    inner = jnp.where(lane == 0, 0.0, pltpu.roll(v, 1, 1))
    return inner + jnp.where(lane == last, 0.0, pltpu.roll(v, last, 1))


def choose(test, one, two):
    return jnp.where(test, one, two), jnp.where(test, two, one)


def corner_rows(margin):
    pieces, at = [], 0
    for side in range(2):
        for d in range(1, margin):
            pieces.append((side, d, margin - d, at))
            at += margin - d
    return pieces, at


def send(c, coarse, bottom, top, low, high, dims, evens, out):
    margin, own, half = dims
    even_a, even_h = evens
    sent, msg_a, msg_b, side_a, side_b = out
    for k, g in enumerate(coarse):
        sent[c, pl.ds(k * half, half), :] = g
        rows = pl.ds(k * margin, margin)
        side_a[c, rows, :], side_b[c, rows, :] = choose(even_a, g[half - margin:], g[:margin])
    for d in range(1, margin):
        rows = pl.ds((d - 1) * half, half)
        msg_a[c, rows, :], msg_b[c, rows, :] = choose(even_h, coarse[own - d], coarse[d - 1])
    rows = pl.ds((margin - 1) * half, 2 * half)
    msg_a[c, rows, :], msg_b[c, rows, :] = choose(even_h, top, bottom)
    rows = pl.ds(own * margin, 2 * own)
    side_a[c, rows, :], side_b[c, rows, :] = choose(even_a, high, low)


def send_field(c, field, q, q_ends, fold, weight, pre, dims, evens, out):
    margin, own, half = dims
    angles, height = 2 * half, 2 * own
    part = lambda ref, h, p: ref[pl.ds(h * angles + p * half, half), :]
    coarse = []
    for k in range(own):
        total = sum(part(weight, h, p) * part(field, h, p) for h in (2 * k, 2 * k + 1) for p in range(2))
        coarse.append(pre[k] * total)
    faces = []
    for s, (h, far) in enumerate(((0, margin - 1), (height - 1, own - margin))):
        faces.append(jnp.concatenate([
            part(q, h, p) * part(field, h, p) + part(fold.at[s], 0, p) * coarse[far] for p in range(2)
        ]))
    ends = [q_ends[s] * field[pl.ds(a, height, stride=angles), :] for s, a in enumerate((0, angles - 1))]
    send(c, coarse, *faces, *ends, dims, evens, out)


def prepare(cases, comps, levels, n_ang, dims, *refs):
    refs = list(refs)
    take = lambda n: [refs.pop(0) for _ in range(n)]
    loads_far, material_far, support_far, modulus_far, positions_far = take(5)
    u, = take(1)
    out = take(5)
    delta, q, beta, weight, winv, pre, q_ends, fold = take(8)
    loads, material, support, modulus, positions, sems = take(6)
    margin, own, half = dims
    columns = cases * comps
    height, angles = 2 * own, 2 * half
    radial = u.shape[-1]
    evens = even("ang"), even("hgt")
    copies = [
        pltpu.make_async_copy(far, near, sems.at[i])
        for i, (far, near) in enumerate((
            (modulus_far, modulus), (material_far, material), (support_far, support), (positions_far, positions),
        ))
    ]
    for copy in copies:
        copy.start()
    thirds = columns // 3
    fetch = lambda c, i: pltpu.make_async_copy(loads_far.at[pl.ds(c, thirds)], loads.at[pl.ds(c, thirds)], sems.at[i])
    for i in range(3):
        fetch(i * thirds, 4 + i).start()
    for copy in copies:
        copy.wait()
    wide, stiffen = [], []
    for h in range(height):
        for p in range(2):
            rows = pl.ds(p * height + h, half, stride=2 * height)
            level = material[rows, :]
            stiff = jnp.zeros(level.shape, jnp.float32)
            for n in range(levels):
                stiff = jnp.where(level == n, modulus[n], stiff)
            w = jnp.sqrt(stiff)
            s = support[rows, :].astype(jnp.float32)
            d = SIGMA + SPRING * s / stiff
            line = pl.ds(h * angles + p * half, half)
            weight[line, :] = w
            winv[line, :] = 1.0 / w
            delta[line, :] = d
            q[line, :] = OMEGA / d
            wide.append(w)
            stiffen.append(s)
    kappa = []
    for k in range(own):
        four = slice(4 * k, 4 * k + 4)
        wc, sc = 0.25 * sum(wide[four]), 0.25 * sum(stiffen[four])
        dc = SIGMA * wc * wc + SPRING * sc
        pre[k] = 0.5 * OMEGA * wc / dc
        kappa.append(OMEGA * wc * wc / dc)
        for i in range(4 * k, 4 * k + 4):
            beta[pl.ds(i * half, half), :] = 0.5 / wc * wide[i]
    faces = [beta[pl.ds(h * angles, angles), :] for h in (0, height - 1)]
    for s in range(2):
        path = 1.0
        for d in range(margin - 1):
            path = path * kappa[d if s == 0 else own - 1 - d]
        fold[s] = faces[s] * jnp.concatenate([path, path])
    ends = []
    for s, a in enumerate((0, angles - 1)):
        rows = pl.ds(a, height, stride=angles)
        q_ends[s] = q[rows, :]
        ends.append(beta[rows, :])
    send(columns, kappa, *faces, *ends, dims, evens, out)
    where = lax.axis_index("ang") * angles + 2 * lax.broadcasted_iota(jnp.int32, (half, radial), 0)

    @pl.loop(0, columns)
    def _(c):
        @pl.when(lax.rem(c, thirds) == 0)
        def _():
            fetch(c, 4 + lax.div(c, thirds)).wait()

        for p in range(2):
            apart = jnp.abs(where + p - positions[lax.div(c, comps)])
            hit = jnp.minimum(apart, angles * n_ang - apart) < angles
            push = jnp.where(hit & (lax.rem(c, comps) == 2), -LOAD, 0.0)
            for h in range(height):
                line = pl.ds(h * angles + p * half, half)
                rows = pl.ds(p * height + h, half, stride=2 * height)
                u[c, line, :] = winv[line, :] * (loads[c, rows, :] + push)
        send_field(c, u.at[c], q, q_ends, fold, weight, pre, dims, evens, out)


def corner_messages(dims, count, side_a, side_b, out_a, out_b):
    margin, own, half = dims
    pieces, rows = corner_rows(margin)
    even_a, even_h = even("ang"), even("hgt")
    for c in range(count):
        slab, base = c // 2, (c % 2) * rows
        for s, d, n, at in pieces:
            def piece(k):
                first = k * margin + (margin - n if s == 0 else 0)
                a, b = side_a[c, pl.ds(first, n), :], side_b[c, pl.ds(first, n), :]
                return jnp.where(even_a, b, a) if s == 0 else jnp.where(even_a, a, b)
            to = pl.ds(base + at, n)
            out_a[slab, to, :], out_b[slab, to, :] = choose(even_h, piece(own - d), piece(d - 1))


def apply_step(dims, columns, group, first, last, dot_at, *refs):
    refs = list(refs)
    take = lambda n: [refs.pop(0) for _ in range(n)]
    u, sent = take(2)
    far, side, corner = take(2), take(2), take(2)
    if last:
        dots_in, = take(1)
    delta, q, beta, weight, pre, q_ends, fold = take(7)
    kx, edge_b, ends_b = take(3) if not first else (None,) * 3
    w, un = take(2)
    if first:
        kx, edge_b, ends_b = take(3)
    if not last:
        out = take(5)
    if last:
        dots, = take(1)
    gx, va, vb, zx, edge, sums = take(6)
    margin, own, half = dims
    height, angles = 2 * own, 2 * half
    radial = u.shape[-1]
    even_a, even_h = evens = even("ang"), even("hgt")
    ext_h, ext_a = own + 2 * margin, half + 2 * margin
    pitch = ext_a + 2 * PAD
    line_pitch = 3 * half
    start = PAD + margin
    coarse = lambda h, shift=0: pl.ds(h * pitch + PAD + shift, ext_a)
    inner = lambda h: pl.ds(h * pitch + start, half)
    pieces, corner_length = corner_rows(margin)

    def assemble(c, slab, base, lane, put_faces):
        field = gx.at[lane]
        for k in range(own):
            field[inner(margin + k), :] = sent[c, pl.ds(k * half, half), :]
            rows = pl.ds(k * margin, margin)
            high, low = choose(even_a, side[0][c, rows, :], side[1][c, rows, :])
            field[pl.ds((margin + k) * pitch + start - margin, margin), :] = low
            field[pl.ds((margin + k) * pitch + start + half, margin), :] = high
        for d in range(1, margin):
            rows = pl.ds((d - 1) * half, half)
            up, down = choose(even_h, far[0][c, rows, :], far[1][c, rows, :])
            field[inner(margin + own - 1 + d), :] = up
            field[inner(margin - d), :] = down
        rows = pl.ds((margin - 1) * half, angles)
        up, down = choose(even_h, far[0][c, rows, :], far[1][c, rows, :])
        put_faces(down, up)
        for s, d, n, at in pieces:
            rows = pl.ds(base + at, n)
            up, down = choose(even_h, corner[0][slab, rows, :], corner[1][slab, rows, :])
            to = start - n if s == 0 else start + half
            field[pl.ds((margin + own - 1 + d) * pitch + to, n), :] = up
            field[pl.ds((margin - d) * pitch + to, n), :] = down

    def angular_ends(c, odd):
        rows = pl.ds(own * margin + odd, own, stride=2)
        return reversed(choose(even_a, side[0][c, rows, :], side[1][c, rows, :]))

    for lane in range(group):
        for h in (0, ext_h - 1):
            gx[lane, coarse(h), :] = jnp.zeros((ext_a, radial), jnp.float32)

    if first:
        def keep(down, up):
            edge_b[0], edge_b[1] = down, up
        assemble(columns, columns // 2, (columns % 2) * corner_length, 0, keep)
        for h in range(1, ext_h - 1):
            kx[h] = gx[0, coarse(h), :]
        for odd in range(2):
            for s, end in enumerate(angular_ends(columns, odd)):
                ends_b[s, odd] = end

    def run(first_column, slab_of):
        lanes = range(group)
        at = [first_column + lane for lane in lanes]
        for lane in lanes:
            def keep(down, up, lane=lane):
                edge[lane, 0], edge[lane, 1] = down, up
            assemble(at[lane], *slab_of(lane), lane, keep)
        source, target = gx, va
        for sweep in range(1, CSWEEPS):
            lo, hi = sweep, ext_h - sweep
            below = [source[n, coarse(lo - 1), :] for n in lanes]
            here = [source[n, coarse(lo), :] for n in lanes]
            for h in range(lo, hi):
                k = kx[h]
                for n in lanes:
                    above = source[n, coarse(h + 1), :]
                    near = below[n] + above + source[n, coarse(h, -1), :] + source[n, coarse(h, 1), :]
                    near = near + radial_pair(here[n])
                    target[n, coarse(h), :] = gx[n, coarse(h), :] + (1.0 - OMEGA) * here[n] + k * near
                    below[n], here[n] = here[n], above
            source, target = target, (vb if target is va else va)
        dot_uw = [jnp.zeros((half, radial), jnp.float32) for _ in lanes]
        dot_aw = [jnp.zeros((half, radial), jnp.float32) for _ in lanes]
        place = lambda h, p, shift=0: pl.ds((h + 1) * line_pitch + 2 * p * half + shift, half)
        for k in range(own):
            e = [source[n, inner(margin + k), :] for n in lanes]
            for h in (2 * k, 2 * k + 1):
                for p in range(2):
                    line = pl.ds(h * angles + p * half, half)
                    qs, bs = q[line, :], beta[line, :]
                    for n in lanes:
                        here = u[at[n], line, :]
                        z = qs * here + bs * e[n]
                        zx[n, place(h, p), :] = z
                        w[at[n], line, :] = z
                        if last:
                            dot_uw[n] = dot_uw[n] + here * z
        for n in lanes:
            for s, (h, k) in enumerate(((-1, margin - 1), (height, margin + own))):
                e = source[n, inner(k), :]
                for p in range(2):
                    rows = pl.ds(p * half, half)
                    zx[n, place(h, p), :] = edge[n, s, rows, :] + edge_b[s, rows, :] * e
            for odd in range(2):
                for s, end in enumerate(angular_ends(at[n], odd)):
                    k = start - 1 if s == 0 else start + half
                    e = source[n, pl.ds(margin * pitch + k, own, stride=pitch), :]
                    put = 2 * half - 1 if s == 0 else half
                    zx[n, pl.ds((1 + odd) * line_pitch + put, own, stride=2 * line_pitch), :] = end + ends_b[s, odd] * e
        load = lambda n, h: [zx[n, place(h, p), :] for p in range(2)]
        below = [load(n, -1) for n in lanes]
        here = [load(n, 0) for n in lanes]
        for h in range(height):
            above = [load(n, h + 1) for n in lanes]
            for p in range(2):
                line = pl.ds(h * angles + p * half, half)
                d = delta[line, :]
                for n in lanes:
                    near = below[n][p] + above[n][p] + here[n][1 - p]
                    near = near + zx[n, place(h, 1 - p, 1 if p else -1), :]
                    near = near + radial_pair(here[n][p])
                    new = d * here[n][p] - near - SHIFT * u[at[n], line, :]
                    un[at[n], line, :] = new
                    if last:
                        dot_aw[n] = dot_aw[n] + new * here[n][p]
            below, here = here, above
        for n in lanes:
            if last:
                for m, dot in enumerate((dot_uw[n], dot_aw[n])):
                    put_sum(sums, m * columns + at[n], dot)
            else:
                send_field(at[n], un.at[at[n]], q, q_ends, fold, weight, pre, dims, evens, out)

    @pl.loop(0, columns // group)
    def _(i):
        slabs = group // 2
        run(group * i, lambda lane: (i * slabs + lane // 2, (lane % 2) * corner_length))

    if last:
        add_sums(sums, dots_in, dots, dot_at * columns)


def put_sum(sums, at, products):
    tile = sum(products[i:i + 8] for i in range(0, products.shape[0], 8))
    sums[pl.ds(pl.multiple_of(at * 8, 8), 8), :] = tile


def add_sums(sums, dots_in, dots, first):
    count, radial = sums.shape[0] // 8, sums.shape[1]
    total = sum(sums[pl.ds(r, count, stride=8), :] for r in range(8))
    total = jnp.sum(total, axis=1, keepdims=True)
    lane = lax.broadcasted_iota(jnp.int32, (count, radial), 1)
    item = lax.broadcasted_iota(jnp.int32, (count, radial), 0)
    row = jnp.sum(jnp.where(lane == first + item, total, 0.0), axis=0, keepdims=True)
    dots[...] = dots_in[...] + jnp.broadcast_to(row, dots.shape)


def two_sums(columns, dot_at, u, w, un, dots_in, dots, sums):
    rows = 32

    @pl.loop(0, columns)
    def _(c):
        uw, aw = 0.0, 0.0
        for r in range(0, u.shape[1], rows):
            line = pl.ds(r, rows)
            z = w[c, line, :]
            uw, aw = uw + u[c, line, :] * z, aw + un[c, line, :] * z
        put_sum(sums, c, uw)
        put_sum(sums, columns + c, aw)

    add_sums(sums, dots_in, dots, dot_at * columns)


def krylov(mu):
    sound = []

    def apply(p):
        out = [SHIFT * v for v in p] + [jnp.zeros_like(mu[0])]
        for i, v in enumerate(p):
            out[i + 1] = out[i + 1] + v
        return out

    def inner(a, b):
        total, size = 0.0, 0.0
        for m in range(len(a) + len(b) - 1):
            terms = [a[i] * b[m - i] for i in range(len(a)) if 0 <= m - i < len(b)]
            total = total + sum(terms) * mu[m]
            size = size + sum(jnp.abs(v) for v in terms) * jnp.abs(mu[m])
        sound.append(size <= GROWTH * jnp.abs(total))
        return total

    def plus(a, b, scale):
        out = []
        for i in range(max(len(a), len(b))):
            v = a[i] if i < len(a) else None
            s = scale * b[i] if i < len(b) else None
            out.append(v if s is None else s if v is None else v + s)
        return out

    r = [jnp.ones_like(mu[0])]
    p = r
    x = []
    rz = mu[0]
    for step in range(ITERS):
        image = apply(p)
        alpha = rz / inner(p, image)
        x = plus(x, p, alpha)
        r = plus(r, image, -alpha)
        if step + 1 < ITERS:
            new = inner(r, r)
            p = plus(r, p, new / rz)
            rz = new
    return x, r, functools.reduce(jnp.logical_and, sound)


def finish(columns, group, dims, *refs):
    refs = list(refs)
    dots = refs.pop(0)
    us = [refs.pop(0) for _ in range(ITERS + 1)]
    ws = [refs.pop(0) for _ in range(ITERS)]
    weight, winv, x_far, r_far, trouble, x_out, r_out, factors, sems = refs
    margin, own, half = dims
    height, angles = 2 * own, 2 * half
    radial = us[0].shape[-1]
    total = jnp.sum(dots[...], axis=0, keepdims=True)
    spread = factors.shape[1], radial
    lane = lax.broadcasted_iota(jnp.int32, spread, 1)
    item = lax.broadcasted_iota(jnp.int32, spread, 0)
    mu = [
        jnp.broadcast_to(jnp.sum(jnp.where(lane == m * columns + item, total, 0.0), axis=1, keepdims=True), spread)
        for m in range(2 * ITERS)
    ]
    xs, rs, sound = krylov(mu)
    trouble[...] = jnp.max(jnp.where(sound | (item >= columns), 0.0, 1.0), axis=0, keepdims=True)
    for j, v in enumerate(xs + rs):
        factors[j] = v

    copies = lambda c, n: [
        pltpu.make_async_copy(near.at[pl.ds(c, n)], far.at[pl.ds(c, n)], sems.at[i])
        for i, (near, far) in enumerate(((x_out, x_far), (r_out, r_far)))
    ]

    @pl.loop(0, columns // group)
    def _(i):
        for n in range(group):
            c = group * i + n
            full = [jnp.broadcast_to(factors[j, pl.ds(c, 1), :], (half, radial)) for j in range(2 * ITERS + 1)]
            xc, rc = full[:ITERS], full[ITERS:]
            for h in range(height):
                for p in range(2):
                    line = pl.ds(h * angles + p * half, half)
                    rows = pl.ds(p * height + h, half, stride=2 * height)
                    x_out[c, rows, :] = winv[line, :] * sum(k * w[c, line, :] for k, w in zip(xc, ws))
                    r_out[c, rows, :] = weight[line, :] * sum(k * u[c, line, :] for k, u in zip(rc, us))
        for copy in copies(group * i, group):
            copy.start()

    for copy in copies(0, columns):
        copy.wait()


def pairs(count, odd, periodic):
    found = []
    for i in range(odd, count, 2):
        j = i + 1
        if j < count or periodic:
            found += [(i, j % count), (j % count, i)]
    return found


def padded_2(block, sides, width, periodic):
    for axis, dim in sides:
        count = lax.axis_size(axis)
        forward = [(i, i + 1) for i in range(count - 1)]
        if periodic:
            forward.append((count - 1, 0))
        backward = [(target, source) for source, target in forward]
        low = lax.ppermute(
            lax.slice_in_dim(block, block.shape[dim] - width, None, axis=dim), axis, forward
        )
        high = lax.ppermute(lax.slice_in_dim(block, 0, width, axis=dim), axis, backward)
        block = jnp.concatenate([low, block, high], axis=dim)
    return block


def zero_pair(v, axis):
    widths = [(0, 0)] * v.ndim
    widths[axis] = (1, 1)
    padded = jnp.pad(v, widths)
    size = v.shape[axis]
    return lax.slice_in_dim(padded, 2, size + 2, axis=axis) + lax.slice_in_dim(
        padded, 0, size, axis=axis
    )


def fine_apply(u, weight, spring):
    v = weight * u
    beside_all = padded_2(v, (("ang", 2),), 1, True)
    above = padded_2(v, (("hgt", 3),), 1, False)
    beside = beside_all[:, :, 2:] + beside_all[:, :, :-2] + above[:, :, :, 2:] + above[:, :, :, :-2]
    beside = beside + zero_pair(v, 4)
    return weight * (SIGMA * v - beside) + SPRING * spring * u


def padded_apply(u, weight, spring):
    v = weight * u
    beside = zero_pair(v, 2) + zero_pair(v, 3) + zero_pair(v, 4)
    return weight * (SIGMA * v - beside) + SPRING * spring * u


def coarsen(field):
    a, h, r = field.shape
    return field.reshape(a // 2, 2, h // 2, 2, r).mean(axis=(1, 3))


def restrict(r):
    c, k, a, h, n = r.shape
    return r.reshape(c, k, a // 2, 2, h // 2, 2, n).sum(axis=(3, 5)) * 0.5


def prolong(e):
    return jnp.repeat(jnp.repeat(e, 2, axis=2), 2, axis=3) * 0.5


def step_by_step(loads, material, support, modulus, positions):
    cases, comps, a_dev, h_dev, radial = loads.shape
    margin = CSWEEPS - 1
    levels = lax.iota(jnp.int32, modulus.shape[0])
    stiff = jnp.sum(
        jnp.where(material[None] == levels[:, None, None, None], modulus[:, None, None, None], 0.0),
        axis=0,
    )
    weight = jnp.sqrt(stiff)
    spring = support.astype(jnp.float32)
    diag = SIGMA * weight * weight + SPRING * spring
    wide_c = coarsen(weight)
    spring_c = coarsen(spring)
    coef = jnp.stack((wide_c, spring_c))
    coef = padded_2(coef, (("ang", 1),), margin, True)
    coef = padded_2(coef, (("hgt", 2),), margin, False)
    wide_p = coef[0]
    spring_p = coef[1]
    diag_raw = SIGMA * wide_p * wide_p + SPRING * spring_p
    diag_p = jnp.where(diag_raw > 0.0, diag_raw, 1.0)
    total_angles = a_dev * lax.axis_size("ang")
    angles = lax.axis_index("ang") * a_dev + lax.iota(jnp.int32, a_dev)
    apart = jnp.abs(angles[None, :] - positions[:, None])
    cycle_dist = jnp.minimum(apart, total_angles - apart)
    hit = jnp.where(cycle_dist < a_dev, -LOAD, 0.0)
    select = jnp.where(lax.iota(jnp.int32, comps) == 2, 1.0, 0.0)
    right = loads + hit[:, None, :, None, None] * select[None, :, None, None, None]

    def precondition(r):
        coarse_rhs = restrict(r)
        wider = padded_2(coarse_rhs, (("ang", 2),), margin, True)
        wider = padded_2(wider, (("hgt", 3),), margin, False)
        err = OMEGA * wider / diag_p
        for sweep in range(CSWEEPS - 1):
            err = err + OMEGA * (wider - padded_apply(err, wide_p, spring_p)) / diag_p
        err = err[:, :, margin : err.shape[2] - margin, margin : err.shape[3] - margin]
        return OMEGA * r / diag + prolong(err)

    def projection(a, b):
        return lax.psum(jnp.sum(a * b, axis=(2, 3, 4)), ("ang", "hgt"))[:, :, None, None, None]

    solution_field = jnp.zeros_like(right)
    residual = right
    precond = precondition(residual)
    direction = precond
    rz_now = projection(residual, precond)
    for step in range(ITERS):
        image = fine_apply(direction, weight, spring)
        curve = lax.psum(jnp.sum(direction * image, axis=(2, 3, 4)), ("ang", "hgt"))
        alpha = rz_now / curve[:, :, None, None, None]
        solution_field = solution_field + alpha * direction
        residual = residual - alpha * image
        if step + 1 < ITERS:
            precond = precondition(residual)
            rz_next = projection(residual, precond)
            direction = precond + rz_next / rz_now * direction
            rz_now = rz_next
    return (solution_field, residual)


def body(loads, material, support, modulus, positions):
    cases, comps, angles, height, radial = loads.shape
    columns = cases * comps
    margin = CSWEEPS
    own, half = height // 2, angles // 2
    dims = (margin, own, half)
    n_ang, n_hgt = lax.axis_size("ang"), lax.axis_size("hgt")
    assert own >= margin and half >= margin and half % 8 == 0 and n_ang % 2 == 0
    assert 2 * ITERS * columns <= radial and columns % 12 == 0
    cells = height * angles
    field, coef = f32(columns, cells, radial), f32(cells, radial)
    rows_h, rows_a = (margin - 1) * half + angles, own * margin + height
    rows_c = corner_rows(margin)[1]
    vm = lambda *s: pltpu.VMEM(s, jnp.float32)
    message = lambda n: [f32(n, own * half, radial)] + [f32(n, rows_h, radial)] * 2 + [f32(n, rows_a, radial)] * 2

    out = list(call(
        functools.partial(prepare, cases, comps, modulus.shape[0], n_ang, dims),
        [field] + message(columns + 1) + [coef] * 5
        + [f32(own, half, radial), f32(2, height, radial), f32(2, angles, radial)],
        loads.reshape(columns, cells, radial), material.reshape(cells, radial), support.reshape(cells, radial),
        modulus, positions,
        hbm=range(5),
        scratch=[
            vm(columns, cells, radial), pltpu.VMEM((cells, radial), jnp.int32), pltpu.VMEM((cells, radial), jnp.int32),
            pltpu.SMEM(modulus.shape, jnp.float32), pltpu.SMEM(positions.shape, jnp.int32),
            pltpu.SemaphoreType.DMA((7,)),
        ],
    ))
    u, sent, msg, side = out[0], out[1], out[2:4], out[4:6]
    delta, q, beta, weight, winv, pre, q_ends, fold = out[6:]
    us, ws = [u], []
    dots = jnp.zeros((n_ang * n_hgt, radial), jnp.float32)
    shared = []
    group = 4
    for step in range(ITERS):
        first, last = step == 0, step + 1 == ITERS
        count = columns + 1 if first else columns
        slabs = (count + 1) // 2
        swap = lambda v, axis, wraps: [lax.ppermute(v[i], axis, pairs(lax.axis_size(axis), i, wraps)) for i in range(2)]
        far = swap(msg, "hgt", False)
        beside = swap(side, "ang", True)
        corner = call(
            functools.partial(corner_messages, dims, count), [f32(slabs, 2 * rows_c, radial)] * 2, *beside,
        )
        corner = swap(corner, "hgt", False)
        args = [us[-1], sent, *far, *beside, *corner, *([dots] if last else []), delta, q, beta, weight, pre, q_ends, fold, *shared]
        outs = [field, field]
        ext_h, ext_a = own + 2 * margin, half + 2 * margin
        if first:
            outs += [f32(ext_h, ext_a, radial), f32(2, angles, radial), f32(2, 2, own, radial)]
        if not last:
            outs += message(columns)
        else:
            outs.append(f32(n_ang * n_hgt, radial))
        block = vm(group, ext_h * (ext_a + 2 * PAD), radial)
        out = list(call(
            functools.partial(apply_step, dims, columns, group, first, last, 2 * step),
            outs, *args,
            scratch=[
                block, block, block, vm(group, (height + 2) * 3 * half, radial),
                vm(group, 2, angles, radial), vm(2 * columns * 8, radial),
            ],
        ))
        ws.append(out.pop(0))
        us.append(out.pop(0))
        if first:
            shared, out = out[:3], out[3:]
        if not last:
            sent, msg, side, out = out[0], out[1:3], out[3:5], out[5:]
        if last:
            dots = out.pop(0)
        else:
            dots, = call(
                functools.partial(two_sums, columns, 2 * step), [f32(n_ang * n_hgt, radial)],
                us[-2], ws[-1], us[-1], dots,
                scratch=[vm(2 * columns * 8, radial)],
                cost=None,
            )

    dots = lax.all_to_all(dots, ("ang", "hgt"), 0, 0, tiled=True)
    x, r, trouble = call(
        functools.partial(finish, columns, 2, dims), [field] * 2 + [f32(1, radial)], dots, *us, *ws, weight, winv,
        hbm_out=(0, 1),
        scratch=[
            vm(columns, cells, radial), vm(columns, cells, radial),
            vm(2 * ITERS + 1, -(-columns // 8) * 8, radial),
            pltpu.SemaphoreType.DMA((2,)),
        ],
    )
    x, r = x.reshape(loads.shape), r.reshape(loads.shape)

    def again(state):
        given = [jnp.where(state[0], v, jnp.zeros_like(v)) for v in (loads, material, support, modulus, positions)]
        return jnp.zeros_like(state[0]), *step_by_step(*given)

    return lax.while_loop(lambda state: state[0], again, (trouble[0, 0] > 0.0, x, r))[1:]


def solution(mesh):
    in_specs = (
        P(None, None, "ang", "hgt", None),
        P("ang", "hgt", None),
        P("ang", "hgt", None),
        P(),
        P(),
    )
    out_specs = (P(None, None, "ang", "hgt", None), P(None, None, "ang", "hgt", None))
    return jax.shard_map(body, mesh=mesh, in_specs=in_specs, out_specs=out_specs, check_vma=False)
```

```python
import functools

import jax
import jax.numpy as jnp
from jax import lax
from jax.experimental import pallas as pl
from jax.experimental.pallas import tpu as pltpu
from jax.sharding import PartitionSpec as P

ITERS = 3
CSWEEPS = 4


SIGMA = 6.5
SPRING = 20.0
OMEGA = 0.8
LOAD = 3.0
SHIFT = 1.0
PAD = 8
GROWTH = 500.0
LIMIT = 24 * 1024 * 1024


def f32(*shape):
    return jax.ShapeDtypeStruct(shape, jnp.float32)


def call(kernel, out_shape, *args, hbm=(), hbm_out=(), scratch=(), cost=None):
    vmem = pl.BlockSpec(memory_space=pltpu.VMEM)
    outside = pl.BlockSpec(memory_space=pltpu.HBM)
    args = [pltpu.with_memory_space_constraint(v, pltpu.HBM) if i in hbm else v for i, v in enumerate(args)]
    return pl.pallas_call(
        kernel,
        out_shape=out_shape,
        in_specs=[outside if i in hbm else vmem for i in range(len(args))],
        out_specs=[outside if i in hbm_out else vmem for i in range(len(out_shape))],
        scratch_shapes=list(scratch),
        cost_estimate=cost,
        compiler_params=pltpu.CompilerParams(vmem_limit_bytes=LIMIT),
    )(*args)


def even(axis):
    return lax.rem(lax.axis_index(axis), 2) == 0


def radial_pair(v):
    lane = lax.broadcasted_iota(jnp.int32, v.shape, 1)
    last = v.shape[1] - 1
    inner = jnp.where(lane == 0, 0.0, pltpu.roll(v, 1, 1))
    return inner + jnp.where(lane == last, 0.0, pltpu.roll(v, last, 1))


def choose(test, one, two):
    return jnp.where(test, one, two), jnp.where(test, two, one)


def corner_rows(margin):
    pieces, at = [], 0
    for side in range(2):
        for d in range(1, margin):
            pieces.append((side, d, margin - d, at))
            at += margin - d
    return pieces, at


def send(c, coarse, bottom, top, low, high, dims, evens, out):
    margin, own, half = dims
    even_a, even_h = evens
    sent, msg_a, msg_b, side_a, side_b = out
    for k, g in enumerate(coarse):
        sent[c, pl.ds(k * half, half), :] = g
        rows = pl.ds(k * margin, margin)
        side_a[c, rows, :], side_b[c, rows, :] = choose(even_a, g[half - margin:], g[:margin])
    for d in range(1, margin):
        rows = pl.ds((d - 1) * half, half)
        msg_a[c, rows, :], msg_b[c, rows, :] = choose(even_h, coarse[own - d], coarse[d - 1])
    rows = pl.ds((margin - 1) * half, 2 * half)
    msg_a[c, rows, :], msg_b[c, rows, :] = choose(even_h, top, bottom)
    rows = pl.ds(own * margin, 2 * own)
    side_a[c, rows, :], side_b[c, rows, :] = choose(even_a, high, low)


def send_field(c, field, q, q_ends, fold, weight, pre, dims, evens, out):
    margin, own, half = dims
    angles, height = 2 * half, 2 * own
    part = lambda ref, h, p: ref[pl.ds(h * angles + p * half, half), :]
    coarse = []
    for k in range(own):
        total = sum(part(weight, h, p) * part(field, h, p) for h in (2 * k, 2 * k + 1) for p in range(2))
        coarse.append(pre[k] * total)
    faces = []
    for s, (h, far) in enumerate(((0, margin - 1), (height - 1, own - margin))):
        faces.append(jnp.concatenate([
            part(q, h, p) * part(field, h, p) + part(fold.at[s], 0, p) * coarse[far] for p in range(2)
        ]))
    ends = [q_ends[s] * field[pl.ds(a, height, stride=angles), :] for s, a in enumerate((0, angles - 1))]
    send(c, coarse, *faces, *ends, dims, evens, out)


def prepare(cases, comps, levels, n_ang, dims, *refs):
    refs = list(refs)
    take = lambda n: [refs.pop(0) for _ in range(n)]
    loads_far, material_far, support_far, modulus_far, positions_far = take(5)
    u, = take(1)
    out = take(5)
    delta, q, beta, weight, winv, pre, q_ends, fold = take(8)
    loads, material, support, modulus, positions, sems = take(6)
    margin, own, half = dims
    columns = cases * comps
    height, angles = 2 * own, 2 * half
    radial = u.shape[-1]
    evens = even("ang"), even("hgt")
    copies = [
        pltpu.make_async_copy(far, near, sems.at[i])
        for i, (far, near) in enumerate((
            (modulus_far, modulus), (material_far, material), (support_far, support), (positions_far, positions),
        ))
    ]
    for copy in copies:
        copy.start()
    thirds = columns // 3
    fetch = lambda c, i: pltpu.make_async_copy(loads_far.at[pl.ds(c, thirds)], loads.at[pl.ds(c, thirds)], sems.at[i])
    for i in range(3):
        fetch(i * thirds, 4 + i).start()
    for copy in copies:
        copy.wait()
    wide, stiffen = [], []
    for h in range(height):
        for p in range(2):
            rows = pl.ds(p * height + h, half, stride=2 * height)
            level = material[rows, :]
            stiff = jnp.zeros(level.shape, jnp.float32)
            for n in range(levels):
                stiff = jnp.where(level == n, modulus[n], stiff)
            w = jnp.sqrt(stiff)
            s = support[rows, :].astype(jnp.float32)
            d = SIGMA + SPRING * s / stiff
            line = pl.ds(h * angles + p * half, half)
            weight[line, :] = w
            winv[line, :] = 1.0 / w
            delta[line, :] = d
            q[line, :] = OMEGA / d
            wide.append(w)
            stiffen.append(s)
    kappa = []
    for k in range(own):
        four = slice(4 * k, 4 * k + 4)
        wc, sc = 0.25 * sum(wide[four]), 0.25 * sum(stiffen[four])
        dc = SIGMA * wc * wc + SPRING * sc
        pre[k] = 0.5 * OMEGA * wc / dc
        kappa.append(OMEGA * wc * wc / dc)
        for i in range(4 * k, 4 * k + 4):
            beta[pl.ds(i * half, half), :] = 0.5 / wc * wide[i]
    faces = [beta[pl.ds(h * angles, angles), :] for h in (0, height - 1)]
    for s in range(2):
        path = 1.0
        for d in range(margin - 1):
            path = path * kappa[d if s == 0 else own - 1 - d]
        fold[s] = faces[s] * jnp.concatenate([path, path])
    ends = []
    for s, a in enumerate((0, angles - 1)):
        rows = pl.ds(a, height, stride=angles)
        q_ends[s] = q[rows, :]
        ends.append(beta[rows, :])
    send(columns, kappa, *faces, *ends, dims, evens, out)
    where = lax.axis_index("ang") * angles + 2 * lax.broadcasted_iota(jnp.int32, (half, radial), 0)

    @pl.loop(0, columns)
    def _(c):
        @pl.when(lax.rem(c, thirds) == 0)
        def _():
            fetch(c, 4 + lax.div(c, thirds)).wait()

        for p in range(2):
            apart = jnp.abs(where + p - positions[lax.div(c, comps)])
            hit = jnp.minimum(apart, angles * n_ang - apart) < angles
            push = jnp.where(hit & (lax.rem(c, comps) == 2), -LOAD, 0.0)
            for h in range(height):
                line = pl.ds(h * angles + p * half, half)
                rows = pl.ds(p * height + h, half, stride=2 * height)
                u[c, line, :] = winv[line, :] * (loads[c, rows, :] + push)
        send_field(c, u.at[c], q, q_ends, fold, weight, pre, dims, evens, out)


def corner_messages(dims, count, side_b, side_a, out_a, out_b):
    margin, own, half = dims
    pieces, rows = corner_rows(margin)
    even_a, even_h = even("ang"), even("hgt")
    for c in range(count):
        slab, base = c // 2, (c % 2) * rows
        for s, d, n, at in pieces:
            def piece(k):
                first = k * margin + (margin - n if s == 0 else 0)
                a, b = side_a[c, pl.ds(first, n), :], side_b[c, pl.ds(first, n), :]
                return jnp.where(even_a, b, a) if s == 0 else jnp.where(even_a, a, b)
            to = pl.ds(base + at, n)
            out_a[slab, to, :], out_b[slab, to, :] = choose(even_h, piece(own - d), piece(d - 1))


def apply_step(dims, columns, group, first, last, dot_at, *refs):
    refs = list(refs)
    take = lambda n: [refs.pop(0) for _ in range(n)]
    u, sent = take(2)
    far, side, corner = take(2), take(2)[::-1], take(2)
    if last:
        dots_in, = take(1)
    delta, q, beta, weight, pre, q_ends, fold = take(7)
    kx, edge_b, ends_b = take(3) if not first else (None,) * 3
    w, un = take(2)
    if first:
        kx, edge_b, ends_b = take(3)
    if not last:
        out = take(5)
    if last:
        dots, = take(1)
    gx, va, vb, zx, edge, sums = take(6)
    margin, own, half = dims
    height, angles = 2 * own, 2 * half
    radial = u.shape[-1]
    even_a, even_h = evens = even("ang"), even("hgt")
    ext_h, ext_a = own + 2 * margin, half + 2 * margin
    pitch = ext_a + 2 * PAD
    line_pitch = 3 * half
    start = PAD + margin
    coarse = lambda h, shift=0: pl.ds(h * pitch + PAD + shift, ext_a)
    inner = lambda h: pl.ds(h * pitch + start, half)
    pieces, corner_length = corner_rows(margin)

    def assemble(c, slab, base, lane, put_faces):
        field = gx.at[lane]
        for k in range(own):
            field[inner(margin + k), :] = sent[c, pl.ds(k * half, half), :]
            rows = pl.ds(k * margin, margin)
            high, low = choose(even_a, side[0][c, rows, :], side[1][c, rows, :])
            field[pl.ds((margin + k) * pitch + start - margin, margin), :] = low
            field[pl.ds((margin + k) * pitch + start + half, margin), :] = high
        for d in range(1, margin):
            rows = pl.ds((d - 1) * half, half)
            up, down = choose(even_h, far[0][c, rows, :], far[1][c, rows, :])
            field[inner(margin + own - 1 + d), :] = up
            field[inner(margin - d), :] = down
        rows = pl.ds((margin - 1) * half, angles)
        up, down = choose(even_h, far[0][c, rows, :], far[1][c, rows, :])
        put_faces(down, up)
        for s, d, n, at in pieces:
            rows = pl.ds(base + at, n)
            up, down = choose(even_h, corner[0][slab, rows, :], corner[1][slab, rows, :])
            to = start - n if s == 0 else start + half
            field[pl.ds((margin + own - 1 + d) * pitch + to, n), :] = up
            field[pl.ds((margin - d) * pitch + to, n), :] = down

    def angular_ends(c, odd):
        rows = pl.ds(own * margin + odd, own, stride=2)
        return reversed(choose(even_a, side[0][c, rows, :], side[1][c, rows, :]))

    for lane in range(group):
        for h in (0, ext_h - 1):
            gx[lane, coarse(h), :] = jnp.zeros((ext_a, radial), jnp.float32)

    if first:
        def keep(down, up):
            edge_b[0], edge_b[1] = down, up
        assemble(columns, columns // 2, (columns % 2) * corner_length, 0, keep)
        for h in range(1, ext_h - 1):
            kx[h] = gx[0, coarse(h), :]
        for odd in range(2):
            for s, end in enumerate(angular_ends(columns, odd)):
                ends_b[s, odd] = end

    def run(first_column, slab_of):
        lanes = range(group)
        at = [first_column + lane for lane in lanes]
        for lane in lanes:
            def keep(down, up, lane=lane):
                edge[lane, 0], edge[lane, 1] = down, up
            assemble(at[lane], *slab_of(lane), lane, keep)
        source, target = gx, va
        for sweep in range(1, CSWEEPS):
            lo, hi = sweep, ext_h - sweep
            below = [source[n, coarse(lo - 1), :] for n in lanes]
            here = [source[n, coarse(lo), :] for n in lanes]
            for h in range(lo, hi):
                k = kx[h]
                for n in lanes:
                    above = source[n, coarse(h + 1), :]
                    near = below[n] + above + source[n, coarse(h, -1), :] + source[n, coarse(h, 1), :]
                    near = near + radial_pair(here[n])
                    target[n, coarse(h), :] = gx[n, coarse(h), :] + (1.0 - OMEGA) * here[n] + k * near
                    below[n], here[n] = here[n], above
            source, target = target, (vb if target is va else va)
        dot_uw = [jnp.zeros((half, radial), jnp.float32) for _ in lanes]
        dot_aw = [jnp.zeros((half, radial), jnp.float32) for _ in lanes]
        place = lambda h, p, shift=0: pl.ds((h + 1) * line_pitch + 2 * p * half + shift, half)
        for k in range(own):
            e = [source[n, inner(margin + k), :] for n in lanes]
            for h in (2 * k, 2 * k + 1):
                for p in range(2):
                    line = pl.ds(h * angles + p * half, half)
                    qs, bs = q[line, :], beta[line, :]
                    for n in lanes:
                        here = u[at[n], line, :]
                        z = qs * here + bs * e[n]
                        zx[n, place(h, p), :] = z
                        w[at[n], line, :] = z
                        if last:
                            dot_uw[n] = dot_uw[n] + here * z
        for n in lanes:
            for s, (h, k) in enumerate(((-1, margin - 1), (height, margin + own))):
                e = source[n, inner(k), :]
                for p in range(2):
                    rows = pl.ds(p * half, half)
                    zx[n, place(h, p), :] = edge[n, s, rows, :] + edge_b[s, rows, :] * e
            for odd in range(2):
                for s, end in enumerate(angular_ends(at[n], odd)):
                    k = start - 1 if s == 0 else start + half
                    e = source[n, pl.ds(margin * pitch + k, own, stride=pitch), :]
                    put = 2 * half - 1 if s == 0 else half
                    zx[n, pl.ds((1 + odd) * line_pitch + put, own, stride=2 * line_pitch), :] = end + ends_b[s, odd] * e
        load = lambda n, h: [zx[n, place(h, p), :] for p in range(2)]
        below = [load(n, -1) for n in lanes]
        here = [load(n, 0) for n in lanes]
        for h in range(height):
            above = [load(n, h + 1) for n in lanes]
            for p in range(2):
                line = pl.ds(h * angles + p * half, half)
                d = delta[line, :]
                for n in lanes:
                    near = below[n][p] + above[n][p] + here[n][1 - p]
                    near = near + zx[n, place(h, 1 - p, 1 if p else -1), :]
                    near = near + radial_pair(here[n][p])
                    new = d * here[n][p] - near - SHIFT * u[at[n], line, :]
                    un[at[n], line, :] = new
                    if last:
                        dot_aw[n] = dot_aw[n] + new * here[n][p]
            below, here = here, above
        for n in lanes:
            if last:
                for m, dot in enumerate((dot_uw[n], dot_aw[n])):
                    put_sum(sums, m * columns + at[n], dot)
            else:
                send_field(at[n], un.at[at[n]], q, q_ends, fold, weight, pre, dims, evens, out)

    @pl.loop(0, columns // group)
    def _(i):
        slabs = group // 2
        run(group * i, lambda lane: (i * slabs + lane // 2, (lane % 2) * corner_length))

    if last:
        add_sums(sums, dots_in, dots, dot_at * columns)


def put_sum(sums, at, products):
    tile = sum(products[i:i + 8] for i in range(0, products.shape[0], 8))
    sums[pl.ds(pl.multiple_of(at * 8, 8), 8), :] = tile


def add_sums(sums, dots_in, dots, first):
    count, radial = sums.shape[0] // 8, sums.shape[1]
    total = sum(sums[pl.ds(r, count, stride=8), :] for r in range(8))
    total = jnp.sum(total, axis=1, keepdims=True)
    lane = lax.broadcasted_iota(jnp.int32, (count, radial), 1)
    item = lax.broadcasted_iota(jnp.int32, (count, radial), 0)
    row = jnp.sum(jnp.where(lane == first + item, total, 0.0), axis=0, keepdims=True)
    dots[...] = dots_in[...] + jnp.broadcast_to(row, dots.shape)


def two_sums(columns, dot_at, u, w, un, dots_in, dots, sums):
    rows = 32

    @pl.loop(0, columns)
    def _(c):
        uw, aw = 0.0, 0.0
        for r in range(0, u.shape[1], rows):
            line = pl.ds(r, rows)
            z = w[c, line, :]
            uw, aw = uw + u[c, line, :] * z, aw + un[c, line, :] * z
        put_sum(sums, c, uw)
        put_sum(sums, columns + c, aw)

    add_sums(sums, dots_in, dots, dot_at * columns)


def krylov(mu):
    sound = []

    def apply(p):
        out = [SHIFT * v for v in p] + [jnp.zeros_like(mu[0])]
        for i, v in enumerate(p):
            out[i + 1] = out[i + 1] + v
        return out

    def inner(a, b):
        total, size = 0.0, 0.0
        for m in range(len(a) + len(b) - 1):
            terms = [a[i] * b[m - i] for i in range(len(a)) if 0 <= m - i < len(b)]
            total = total + sum(terms) * mu[m]
            size = size + sum(jnp.abs(v) for v in terms) * jnp.abs(mu[m])
        sound.append(size <= GROWTH * jnp.abs(total))
        return total

    def plus(a, b, scale):
        out = []
        for i in range(max(len(a), len(b))):
            v = a[i] if i < len(a) else None
            s = scale * b[i] if i < len(b) else None
            out.append(v if s is None else s if v is None else v + s)
        return out

    r = [jnp.ones_like(mu[0])]
    p = r
    x = []
    rz = mu[0]
    for step in range(ITERS):
        image = apply(p)
        alpha = rz / inner(p, image)
        x = plus(x, p, alpha)
        r = plus(r, image, -alpha)
        if step + 1 < ITERS:
            new = inner(r, r)
            p = plus(r, p, new / rz)
            rz = new
    return x, r, functools.reduce(jnp.logical_and, sound)


def finish(columns, group, dims, *refs):
    refs = list(refs)
    dots = refs.pop(0)
    us = [refs.pop(0) for _ in range(ITERS + 1)]
    ws = [refs.pop(0) for _ in range(ITERS)]
    weight, winv, x_far, r_far, trouble, x_out, r_out, factors, sems = refs
    margin, own, half = dims
    height, angles = 2 * own, 2 * half
    radial = us[0].shape[-1]
    total = jnp.sum(dots[...], axis=0, keepdims=True)
    spread = factors.shape[1], radial
    lane = lax.broadcasted_iota(jnp.int32, spread, 1)
    item = lax.broadcasted_iota(jnp.int32, spread, 0)
    mu = [
        jnp.broadcast_to(jnp.sum(jnp.where(lane == m * columns + item, total, 0.0), axis=1, keepdims=True), spread)
        for m in range(2 * ITERS)
    ]
    xs, rs, sound = krylov(mu)
    trouble[...] = jnp.max(jnp.where(sound | (item >= columns), 0.0, 1.0), axis=0, keepdims=True)
    for j, v in enumerate(xs + rs):
        factors[j] = v

    copies = lambda c, n: [
        pltpu.make_async_copy(near.at[pl.ds(c, n)], far.at[pl.ds(c, n)], sems.at[i])
        for i, (near, far) in enumerate(((x_out, x_far), (r_out, r_far)))
    ]

    @pl.loop(0, columns // group)
    def _(i):
        for n in range(group):
            c = group * i + n
            full = [jnp.broadcast_to(factors[j, pl.ds(c, 1), :], (half, radial)) for j in range(2 * ITERS + 1)]
            xc, rc = full[:ITERS], full[ITERS:]
            for h in range(height):
                for p in range(2):
                    line = pl.ds(h * angles + p * half, half)
                    rows = pl.ds(p * height + h, half, stride=2 * height)
                    x_out[c, rows, :] = winv[line, :] * sum(k * w[c, line, :] for k, w in zip(xc, ws))
                    r_out[c, rows, :] = weight[line, :] * sum(k * u[c, line, :] for k, u in zip(rc, us))
        for copy in copies(group * i, group):
            copy.start()

    for copy in copies(0, columns):
        copy.wait()


def pairs(count, odd, periodic):
    found = []
    for i in range(odd, count, 2):
        j = i + 1
        if j < count or periodic:
            found += [(i, j % count), (j % count, i)]
    return found


def padded_2(block, sides, width, periodic):
    for axis, dim in sides:
        count = lax.axis_size(axis)
        forward = [(i, i + 1) for i in range(count - 1)]
        if periodic:
            forward.append((count - 1, 0))
        backward = [(target, source) for source, target in forward]
        low = lax.ppermute(
            lax.slice_in_dim(block, block.shape[dim] - width, None, axis=dim), axis, forward
        )
        high = lax.ppermute(lax.slice_in_dim(block, 0, width, axis=dim), axis, backward)
        block = jnp.concatenate([low, block, high], axis=dim)
    return block


def zero_pair(v, axis):
    widths = [(0, 0)] * v.ndim
    widths[axis] = (1, 1)
    padded = jnp.pad(v, widths)
    size = v.shape[axis]
    return lax.slice_in_dim(padded, 2, size + 2, axis=axis) + lax.slice_in_dim(
        padded, 0, size, axis=axis
    )


def fine_apply(u, weight, spring):
    v = weight * u
    beside_all = padded_2(v, (("ang", 2),), 1, True)
    above = padded_2(v, (("hgt", 3),), 1, False)
    beside = beside_all[:, :, 2:] + beside_all[:, :, :-2] + above[:, :, :, 2:] + above[:, :, :, :-2]
    beside = beside + zero_pair(v, 4)
    return weight * (SIGMA * v - beside) + SPRING * spring * u


def padded_apply(u, weight, spring):
    v = weight * u
    beside = zero_pair(v, 2) + zero_pair(v, 3) + zero_pair(v, 4)
    return weight * (SIGMA * v - beside) + SPRING * spring * u


def coarsen(field):
    a, h, r = field.shape
    return field.reshape(a // 2, 2, h // 2, 2, r).mean(axis=(1, 3))


def restrict(r):
    c, k, a, h, n = r.shape
    return r.reshape(c, k, a // 2, 2, h // 2, 2, n).sum(axis=(3, 5)) * 0.5


def prolong(e):
    return jnp.repeat(jnp.repeat(e, 2, axis=2), 2, axis=3) * 0.5


def step_by_step(loads, material, support, modulus, positions):
    cases, comps, a_dev, h_dev, radial = loads.shape
    margin = CSWEEPS - 1
    levels = lax.iota(jnp.int32, modulus.shape[0])
    stiff = jnp.sum(
        jnp.where(material[None] == levels[:, None, None, None], modulus[:, None, None, None], 0.0),
        axis=0,
    )
    weight = jnp.sqrt(stiff)
    spring = support.astype(jnp.float32)
    diag = SIGMA * weight * weight + SPRING * spring
    wide_c = coarsen(weight)
    spring_c = coarsen(spring)
    coef = jnp.stack((wide_c, spring_c))
    coef = padded_2(coef, (("ang", 1),), margin, True)
    coef = padded_2(coef, (("hgt", 2),), margin, False)
    wide_p = coef[0]
    spring_p = coef[1]
    diag_raw = SIGMA * wide_p * wide_p + SPRING * spring_p
    diag_p = jnp.where(diag_raw > 0.0, diag_raw, 1.0)
    total_angles = a_dev * lax.axis_size("ang")
    angles = lax.axis_index("ang") * a_dev + lax.iota(jnp.int32, a_dev)
    apart = jnp.abs(angles[None, :] - positions[:, None])
    cycle_dist = jnp.minimum(apart, total_angles - apart)
    hit = jnp.where(cycle_dist < a_dev, -LOAD, 0.0)
    select = jnp.where(lax.iota(jnp.int32, comps) == 2, 1.0, 0.0)
    right = loads + hit[:, None, :, None, None] * select[None, :, None, None, None]

    def precondition(r):
        coarse_rhs = restrict(r)
        wider = padded_2(coarse_rhs, (("ang", 2),), margin, True)
        wider = padded_2(wider, (("hgt", 3),), margin, False)
        err = OMEGA * wider / diag_p
        for sweep in range(CSWEEPS - 1):
            err = err + OMEGA * (wider - padded_apply(err, wide_p, spring_p)) / diag_p
        err = err[:, :, margin : err.shape[2] - margin, margin : err.shape[3] - margin]
        return OMEGA * r / diag + prolong(err)

    def projection(a, b):
        return lax.psum(jnp.sum(a * b, axis=(2, 3, 4)), ("ang", "hgt"))[:, :, None, None, None]

    solution_field = jnp.zeros_like(right)
    residual = right
    precond = precondition(residual)
    direction = precond
    rz_now = projection(residual, precond)
    for step in range(ITERS):
        image = fine_apply(direction, weight, spring)
        curve = lax.psum(jnp.sum(direction * image, axis=(2, 3, 4)), ("ang", "hgt"))
        alpha = rz_now / curve[:, :, None, None, None]
        solution_field = solution_field + alpha * direction
        residual = residual - alpha * image
        if step + 1 < ITERS:
            precond = precondition(residual)
            rz_next = projection(residual, precond)
            direction = precond + rz_next / rz_now * direction
            rz_now = rz_next
    return (solution_field, residual)


def swap(messages, axis, periodic, first=0):
    got = [None, None]
    for i in (first, 1 - first):
        got[i] = lax.ppermute(messages[i], axis, pairs(lax.axis_size(axis), i, periodic))
    return got


def body(loads, material, support, modulus, positions):
    cases, comps, angles, height, radial = loads.shape
    columns = cases * comps
    margin = CSWEEPS
    group = 6
    own, half = height // 2, angles // 2
    dims = (margin, own, half)
    n_ang, n_hgt = lax.axis_size("ang"), lax.axis_size("hgt")
    assert own >= margin and half >= margin and half % 8 == 0 and n_ang % 2 == 0
    assert 2 * ITERS * columns <= radial and columns % group == 0 and columns % 3 == 0
    cells = height * angles
    field, coef = f32(columns, cells, radial), f32(cells, radial)
    rows_h, rows_a = (margin - 1) * half + angles, own * margin + height
    rows_c = corner_rows(margin)[1]
    vm = lambda *s: pltpu.VMEM(s, jnp.float32)
    message = lambda n: [f32(n, own * half, radial)] + [f32(n, rows_h, radial)] * 2 + [f32(n, rows_a, radial)] * 2

    out = list(call(
        functools.partial(prepare, cases, comps, modulus.shape[0], n_ang, dims),
        [field] + message(columns + 1) + [coef] * 5
        + [f32(own, half, radial), f32(2, height, radial), f32(2, angles, radial)],
        loads.reshape(columns, cells, radial), material.reshape(cells, radial), support.reshape(cells, radial),
        modulus, positions,
        hbm=range(5),
        scratch=[
            vm(columns, cells, radial), pltpu.VMEM((cells, radial), jnp.int32), pltpu.VMEM((cells, radial), jnp.int32),
            pltpu.SMEM(modulus.shape, jnp.float32), pltpu.SMEM(positions.shape, jnp.int32),
            pltpu.SemaphoreType.DMA((7,)),
        ],
    ))
    u, sent, msg, side = out[0], out[1], out[2:4], out[4:6]
    delta, q, beta, weight, winv, pre, q_ends, fold = out[6:]
    us, ws = [u], []
    dots = jnp.zeros((n_ang * n_hgt, radial), jnp.float32)
    shared = []
    for step in range(ITERS):
        first, last = step == 0, step + 1 == ITERS
        count = columns + 1 if first else columns
        slabs = (count + 1) // 2
        far = swap(msg, "hgt", False)
        beside = swap(side, "ang", True, first=1)
        corner = call(
            functools.partial(corner_messages, dims, count), [f32(slabs, 2 * rows_c, radial)] * 2, *beside[::-1],
        )
        corner = swap(corner, "hgt", False)
        args = [us[-1], sent, *far, *beside[::-1], *corner, *([dots] if last else []), delta, q, beta, weight, pre, q_ends, fold, *shared]
        outs = [field, field]
        ext_h, ext_a = own + 2 * margin, half + 2 * margin
        if first:
            outs += [f32(ext_h, ext_a, radial), f32(2, angles, radial), f32(2, 2, own, radial)]
        if not last:
            outs += message(columns)
        else:
            outs.append(f32(n_ang * n_hgt, radial))
        block = vm(group, ext_h * (ext_a + 2 * PAD), radial)
        out = list(call(
            functools.partial(apply_step, dims, columns, group, first, last, 2 * step),
            outs, *args,
            scratch=[
                block, block, block, vm(group, (height + 2) * 3 * half, radial),
                vm(group, 2, angles, radial), vm(2 * columns * 8, radial),
            ],
        ))
        ws.append(out.pop(0))
        us.append(out.pop(0))
        if first:
            shared, out = out[:3], out[3:]
        if not last:
            sent, msg, side, out = out[0], out[1:3], out[3:5], out[5:]
        if last:
            dots = out.pop(0)
        else:
            dots, = call(
                functools.partial(two_sums, columns, 2 * step), [f32(n_ang * n_hgt, radial)],
                us[-2], ws[-1], us[-1], dots,
                scratch=[vm(2 * columns * 8, radial)],
                cost=None,
            )

    dots = lax.all_to_all(dots, ("ang", "hgt"), 0, 0, tiled=True)
    x, r, trouble = call(
        functools.partial(finish, columns, 2, dims), [field] * 2 + [f32(1, radial)], dots, *us, *ws, weight, winv,
        hbm_out=(0, 1),
        scratch=[
            vm(columns, cells, radial), vm(columns, cells, radial),
            vm(2 * ITERS + 1, -(-columns // 8) * 8, radial),
            pltpu.SemaphoreType.DMA((2,)),
        ],
    )
    x, r = x.reshape(loads.shape), r.reshape(loads.shape)

    def again(state):
        given = [jnp.where(state[0], v, jnp.zeros_like(v)) for v in (loads, material, support, modulus, positions)]
        return jnp.zeros_like(state[0]), *step_by_step(*given)

    return lax.while_loop(lambda state: state[0], again, (trouble[0, 0] > 0.0, x, r))[1:]


def solution(mesh):
    in_specs = (
        P(None, None, "ang", "hgt", None),
        P("ang", "hgt", None),
        P("ang", "hgt", None),
        P(),
        P(),
    )
    out_specs = (P(None, None, "ang", "hgt", None), P(None, None, "ang", "hgt", None))
    return jax.shard_map(body, mesh=mesh, in_specs=in_specs, out_specs=out_specs, check_vma=False)
```

```python
import functools

import jax
import jax.numpy as jnp
from jax import lax
from jax.experimental import pallas as pl
from jax.experimental.pallas import tpu as pltpu
from jax.sharding import PartitionSpec as P

ITERS = 3
CSWEEPS = 4


SIGMA = 6.5
SPRING = 20.0
OMEGA = 0.8
LOAD = 3.0
SHIFT = 1.0
PAD = 8
GROWTH = 500.0
LIMIT = 24 * 1024 * 1024


def f32(*shape):
    return jax.ShapeDtypeStruct(shape, jnp.float32)


def call(kernel, out_shape, *args, hbm=(), hbm_out=(), scratch=(), cost=None):
    vmem = pl.BlockSpec(memory_space=pltpu.VMEM)
    outside = pl.BlockSpec(memory_space=pltpu.HBM)
    args = [pltpu.with_memory_space_constraint(v, pltpu.HBM) if i in hbm else v for i, v in enumerate(args)]
    return pl.pallas_call(
        kernel,
        out_shape=out_shape,
        in_specs=[outside if i in hbm else vmem for i in range(len(args))],
        out_specs=[outside if i in hbm_out else vmem for i in range(len(out_shape))],
        scratch_shapes=list(scratch),
        cost_estimate=cost,
        compiler_params=pltpu.CompilerParams(vmem_limit_bytes=LIMIT),
    )(*args)


def even(axis):
    return lax.rem(lax.axis_index(axis), 2) == 0


def radial_pair(v):
    lane = lax.broadcasted_iota(jnp.int32, v.shape, 1)
    last = v.shape[1] - 1
    inner = jnp.where(lane == 0, 0.0, pltpu.roll(v, 1, 1))
    return inner + jnp.where(lane == last, 0.0, pltpu.roll(v, last, 1))


def choose(test, one, two):
    return jnp.where(test, one, two), jnp.where(test, two, one)


def corner_rows(margin):
    pieces, at = [], 0
    for side in range(2):
        for d in range(1, margin):
            pieces.append((side, d, margin - d, at))
            at += margin - d
    return pieces, at


def slot_of(c, rows):
    slab, second = (c // 2, c % 2) if isinstance(c, int) else c
    return slab, second * rows


def side_rows(dims):
    margin, own, _ = dims
    return own * (margin - 1) + 2 * own


def ends_of(ref, odd, side, dims):
    _, own, half = dims
    return ref[pl.ds((2 * odd + side) * half + side * (half - 1), own, stride=4 * half), :]


def column_of(ref, distance, side, dims):
    _, own, half = dims
    return ref[pl.ds(distance if side == 0 else half - 1 - distance, own, stride=half), :]


def send(c, slot, coarse, spare, bottom, top, ends, dims, evens, out):
    margin, own, half = dims
    even_a, even_h = evens
    sent, msg_a, msg_b, side_a, side_b = out
    slab, base = slot_of(slot, side_rows(dims))
    for k, g in enumerate(coarse):
        sent[c, pl.ds(k * half, half), :] = g
    for d in range(1, margin):
        rows = pl.ds((d - 1) * half, half)
        msg_a[c, rows, :], msg_b[c, rows, :] = choose(even_h, coarse[own - d], coarse[d - 1])
        low, high = (column_of(spare, d - 1, s, dims) for s in range(2))
        rows = pl.ds(base + (d - 1) * own, own)
        side_a[slab, rows, :], side_b[slab, rows, :] = choose(even_a, high, low)
    rows = pl.ds((margin - 1) * half, 2 * half)
    msg_a[c, rows, :], msg_b[c, rows, :] = choose(even_h, top, bottom)
    for odd in range(2):
        rows = pl.ds(base + (margin - 1 + odd) * own, own)
        side_a[slab, rows, :], side_b[slab, rows, :] = choose(even_a, ends[1][odd], ends[0][odd])


def send_field(c, slot, field, spare, scales, dims, evens, out):
    q, q_ends, fold, fold_ends, weight, pre = scales
    margin, own, half = dims
    angles, height = 2 * half, 2 * own
    part = lambda ref, h, p: ref[pl.ds(h * angles + p * half, half), :]
    coarse = []
    for k in range(own):
        total = sum(part(weight, h, p) * part(field, h, p) for h in (2 * k, 2 * k + 1) for p in range(2))
        coarse.append(pre[k] * total)
        spare[pl.ds(k * half, half), :] = coarse[k]
    faces = []
    for s, (h, far) in enumerate(((0, margin - 1), (height - 1, own - margin))):
        faces.append(jnp.concatenate([
            part(q, h, p) * part(field, h, p) + part(fold.at[s], 0, p) * coarse[far] for p in range(2)
        ]))
    ends = []
    for s in range(2):
        far = column_of(spare, margin - 1, s, dims)
        ends.append([q_ends[s, odd] * ends_of(field, odd, s, dims) + fold_ends[s, odd] * far for odd in range(2)])
    send(c, slot, coarse, spare, *faces, ends, dims, evens, out)


def prepare(cases, comps, levels, n_ang, dims, *refs):
    refs = list(refs)
    take = lambda n: [refs.pop(0) for _ in range(n)]
    loads_far, material_far, support_far, modulus_far, positions_far = take(5)
    u, = take(1)
    out = take(5)
    delta, q, beta, weight, winv, pre, q_ends, fold, fold_ends = take(9)
    loads, material, support, modulus, positions, sems, spare = take(7)
    margin, own, half = dims
    columns = cases * comps
    height, angles = 2 * own, 2 * half
    radial = u.shape[-1]
    evens = even("ang"), even("hgt")
    copies = [
        pltpu.make_async_copy(far, near, sems.at[i])
        for i, (far, near) in enumerate((
            (modulus_far, modulus), (material_far, material), (support_far, support), (positions_far, positions),
        ))
    ]
    for copy in copies:
        copy.start()
    thirds = columns // 3
    fetch = lambda c, i: pltpu.make_async_copy(loads_far.at[pl.ds(c, thirds)], loads.at[pl.ds(c, thirds)], sems.at[i])
    for i in range(3):
        fetch(i * thirds, 4 + i).start()
    for copy in copies:
        copy.wait()
    wide, stiffen = [], []
    for h in range(height):
        for p in range(2):
            rows = pl.ds(p * height + h, half, stride=2 * height)
            level = material[rows, :]
            stiff = jnp.zeros(level.shape, jnp.float32)
            for n in range(levels):
                stiff = jnp.where(level == n, modulus[n], stiff)
            w = jnp.sqrt(stiff)
            s = support[rows, :].astype(jnp.float32)
            d = SIGMA + SPRING * s / stiff
            line = pl.ds(h * angles + p * half, half)
            weight[line, :] = w
            winv[line, :] = 1.0 / w
            delta[line, :] = d
            q[line, :] = OMEGA / d
            wide.append(w)
            stiffen.append(s)
    kappa = []
    for k in range(own):
        four = slice(4 * k, 4 * k + 4)
        wc, sc = 0.25 * sum(wide[four]), 0.25 * sum(stiffen[four])
        dc = SIGMA * wc * wc + SPRING * sc
        pre[k] = 0.5 * OMEGA * wc / dc
        kappa.append(OMEGA * wc * wc / dc)
        for i in range(4 * k, 4 * k + 4):
            beta[pl.ds(i * half, half), :] = 0.5 / wc * wide[i]
    faces = [beta[pl.ds(h * angles, angles), :] for h in (0, height - 1)]
    for s in range(2):
        path = 1.0
        for d in range(margin - 1):
            path = path * kappa[d if s == 0 else own - 1 - d]
        fold[s] = faces[s] * jnp.concatenate([path, path])
    for k in range(own):
        spare[0, pl.ds(k * half, half), :] = kappa[k]
    ends = []
    for s in range(2):
        path = 1.0
        for d in range(margin - 1):
            path = path * column_of(spare.at[0], d, s, dims)
        ends.append([ends_of(beta, odd, s, dims) for odd in range(2)])
        for odd in range(2):
            q_ends[s, odd] = ends_of(q, odd, s, dims)
            fold_ends[s, odd] = path * ends[s][odd]
    send(columns, columns, kappa, spare.at[0], *faces, ends, dims, evens, out)
    scales = q, q_ends, fold, fold_ends, weight, pre
    where = lax.axis_index("ang") * angles + 2 * lax.broadcasted_iota(jnp.int32, (half, radial), 0)

    @pl.loop(0, columns // 2)
    def _(i):
        @pl.when(lax.rem(2 * i, thirds) == 0)
        def _():
            fetch(2 * i, 4 + lax.div(2 * i, thirds)).wait()

        for second in range(2):
            c = 2 * i + second
            for p in range(2):
                apart = jnp.abs(where + p - positions[lax.div(c, comps)])
                hit = jnp.minimum(apart, angles * n_ang - apart) < angles
                push = jnp.where(hit & (lax.rem(c, comps) == 2), -LOAD, 0.0)
                for h in range(height):
                    line = pl.ds(h * angles + p * half, half)
                    rows = pl.ds(p * height + h, half, stride=2 * height)
                    u[c, line, :] = winv[line, :] * (loads[c, rows, :] + push)
            send_field(c, (i, second), u.at[c], spare.at[second], scales, dims, evens, out)


def corner_messages(dims, count, side_b, side_a, out_a, out_b):
    margin, own, half = dims
    pieces, rows = corner_rows(margin)
    even_a, even_h = even("ang"), even("hgt")
    for c in range(count):
        slab, of_side = slot_of(c, side_rows(dims))
        _, of_corner = slot_of(c, rows)
        for s, d, n, at in pieces:
            for j in range(n):
                def cell(k):
                    get = pl.ds(of_side + j * own + k, 1)
                    a, b = side_a[slab, get, :], side_b[slab, get, :]
                    return jnp.where(even_a, b, a) if s == 0 else jnp.where(even_a, a, b)
                to = pl.ds(of_corner + at + (n - 1 - j if s == 0 else j), 1)
                out_a[slab, to, :], out_b[slab, to, :] = choose(even_h, cell(own - d), cell(d - 1))


def apply_step(dims, columns, group, first, last, dot_at, *refs):
    refs = list(refs)
    take = lambda n: [refs.pop(0) for _ in range(n)]
    u, sent = take(2)
    far, side, corner = take(2), take(2)[::-1], take(2)
    if last:
        dots_in, = take(1)
    delta, q, beta, weight, pre, q_ends, fold, fold_ends = take(8)
    kx, edge_b, ends_b = take(3) if not first else (None,) * 3
    w, un = take(2)
    if first:
        kx, edge_b, ends_b = take(3)
    if not last:
        out = take(5)
    if last:
        dots, = take(1)
    gx, va, vb, zx, edge, sums, spare = take(7)
    margin, own, half = dims
    height, angles = 2 * own, 2 * half
    radial = u.shape[-1]
    even_a, even_h = evens = even("ang"), even("hgt")
    ext_h, ext_a = own + 2 * margin, half + 2 * margin
    pitch = ext_a + 2 * PAD
    line_pitch = 3 * half
    start = PAD + margin
    coarse = lambda h, shift=0: pl.ds(h * pitch + PAD + shift, ext_a)
    inner = lambda h: pl.ds(h * pitch + start, half)
    pieces, corner_length = corner_rows(margin)

    def assemble(c, slot, lane, put_faces):
        field = gx.at[lane]
        slab, side_at = slot_of(slot, side_rows(dims))
        _, base = slot_of(slot, corner_length)
        for k in range(own):
            field[inner(margin + k), :] = sent[c, pl.ds(k * half, half), :]
        for d in range(1, margin):
            rows = pl.ds((d - 1) * half, half)
            up, down = choose(even_h, far[0][c, rows, :], far[1][c, rows, :])
            field[inner(margin + own - 1 + d), :] = up
            field[inner(margin - d), :] = down
            rows = pl.ds(side_at + (d - 1) * own, own)
            high, low = choose(even_a, side[0][slab, rows, :], side[1][slab, rows, :])
            field[pl.ds(margin * pitch + start - d, own, stride=pitch), :] = low
            field[pl.ds(margin * pitch + start + half + d - 1, own, stride=pitch), :] = high
        rows = pl.ds((margin - 1) * half, angles)
        up, down = choose(even_h, far[0][c, rows, :], far[1][c, rows, :])
        put_faces(down, up)
        for s, d, n, at in pieces:
            rows = pl.ds(base + at, n)
            up, down = choose(even_h, corner[0][slab, rows, :], corner[1][slab, rows, :])
            to = start - n if s == 0 else start + half
            field[pl.ds((margin + own - 1 + d) * pitch + to, n), :] = up
            field[pl.ds((margin - d) * pitch + to, n), :] = down

    def angular_ends(slot, odd):
        slab, side_at = slot_of(slot, side_rows(dims))
        rows = pl.ds(side_at + (margin - 1 + odd) * own, own)
        return reversed(choose(even_a, side[0][slab, rows, :], side[1][slab, rows, :]))

    for lane in range(group):
        for h in (0, ext_h - 1):
            gx[lane, coarse(h), :] = jnp.zeros((ext_a, radial), jnp.float32)
        for end in (start - margin, start + half + margin - 1):
            gx[lane, pl.ds(end, ext_h, stride=pitch), :] = jnp.zeros((ext_h, radial), jnp.float32)

    if first:
        def keep(down, up):
            edge_b[0], edge_b[1] = down, up
        assemble(columns, columns, 0, keep)
        for h in range(1, ext_h - 1):
            kx[h] = gx[0, coarse(h), :]
        for odd in range(2):
            for s, end in enumerate(angular_ends(columns, odd)):
                ends_b[s, odd] = end

    def run(first_column, slots):
        lanes = range(group)
        at = [first_column + lane for lane in lanes]
        for lane in lanes:
            def keep(down, up, lane=lane):
                edge[lane, 0], edge[lane, 1] = down, up
            assemble(at[lane], slots[lane], lane, keep)
        source, target = gx, va
        for sweep in range(1, CSWEEPS):
            lo, hi = sweep, ext_h - sweep
            below = [source[n, coarse(lo - 1), :] for n in lanes]
            here = [source[n, coarse(lo), :] for n in lanes]
            for h in range(lo, hi):
                k = kx[h]
                for n in lanes:
                    above = source[n, coarse(h + 1), :]
                    near = below[n] + above + source[n, coarse(h, -1), :] + source[n, coarse(h, 1), :]
                    near = near + radial_pair(here[n])
                    target[n, coarse(h), :] = gx[n, coarse(h), :] + (1.0 - OMEGA) * here[n] + k * near
                    below[n], here[n] = here[n], above
            source, target = target, (vb if target is va else va)
        dot_uw = [jnp.zeros((half, radial), jnp.float32) for _ in lanes]
        dot_aw = [jnp.zeros((half, radial), jnp.float32) for _ in lanes]
        place = lambda h, p, shift=0: pl.ds((h + 1) * line_pitch + 2 * p * half + shift, half)
        for k in range(own):
            e = [source[n, inner(margin + k), :] for n in lanes]
            for h in (2 * k, 2 * k + 1):
                for p in range(2):
                    line = pl.ds(h * angles + p * half, half)
                    qs, bs = q[line, :], beta[line, :]
                    for n in lanes:
                        here = u[at[n], line, :]
                        z = qs * here + bs * e[n]
                        zx[n, place(h, p), :] = z
                        w[at[n], line, :] = z
                        if last:
                            dot_uw[n] = dot_uw[n] + here * z
        for n in lanes:
            for s, (h, k) in enumerate(((-1, margin - 1), (height, margin + own))):
                e = source[n, inner(k), :]
                for p in range(2):
                    rows = pl.ds(p * half, half)
                    zx[n, place(h, p), :] = edge[n, s, rows, :] + edge_b[s, rows, :] * e
            for odd in range(2):
                for s, end in enumerate(angular_ends(slots[n], odd)):
                    k = start - 1 if s == 0 else start + half
                    e = source[n, pl.ds(margin * pitch + k, own, stride=pitch), :]
                    put = 2 * half - 1 if s == 0 else half
                    zx[n, pl.ds((1 + odd) * line_pitch + put, own, stride=2 * line_pitch), :] = end + ends_b[s, odd] * e
        load = lambda n, h: [zx[n, place(h, p), :] for p in range(2)]
        below = [load(n, -1) for n in lanes]
        here = [load(n, 0) for n in lanes]
        for h in range(height):
            above = [load(n, h + 1) for n in lanes]
            for p in range(2):
                line = pl.ds(h * angles + p * half, half)
                d = delta[line, :]
                for n in lanes:
                    near = below[n][p] + above[n][p] + here[n][1 - p]
                    near = near + zx[n, place(h, 1 - p, 1 if p else -1), :]
                    near = near + radial_pair(here[n][p])
                    new = d * here[n][p] - near - SHIFT * u[at[n], line, :]
                    un[at[n], line, :] = new
                    if last:
                        dot_aw[n] = dot_aw[n] + new * here[n][p]
            below, here = here, above
        for n in lanes:
            if last:
                for m, dot in enumerate((dot_uw[n], dot_aw[n])):
                    put_sum(sums, m * columns + at[n], dot)
            else:
                scales = q, q_ends, fold, fold_ends, weight, pre
                send_field(at[n], slots[n], un.at[at[n]], spare.at[n], scales, dims, evens, out)

    @pl.loop(0, columns // group)
    def _(i):
        slabs = group // 2
        run(group * i, [(i * slabs + lane // 2, lane % 2) for lane in range(group)])

    if last:
        add_sums(sums, dots_in, dots, dot_at * columns)


def put_sum(sums, at, products):
    tile = sum(products[i:i + 8] for i in range(0, products.shape[0], 8))
    sums[pl.ds(pl.multiple_of(at * 8, 8), 8), :] = tile


def add_sums(sums, dots_in, dots, first):
    count, radial = sums.shape[0] // 8, sums.shape[1]
    total = sum(sums[pl.ds(r, count, stride=8), :] for r in range(8))
    total = jnp.sum(total, axis=1, keepdims=True)
    lane = lax.broadcasted_iota(jnp.int32, (count, radial), 1)
    item = lax.broadcasted_iota(jnp.int32, (count, radial), 0)
    row = jnp.sum(jnp.where(lane == first + item, total, 0.0), axis=0, keepdims=True)
    dots[...] = dots_in[...] + jnp.broadcast_to(row, dots.shape)


def two_sums(columns, dot_at, u, w, un, dots_in, dots, sums):
    rows = 32

    @pl.loop(0, columns)
    def _(c):
        uw, aw = 0.0, 0.0
        for r in range(0, u.shape[1], rows):
            line = pl.ds(r, rows)
            z = w[c, line, :]
            uw, aw = uw + u[c, line, :] * z, aw + un[c, line, :] * z
        put_sum(sums, c, uw)
        put_sum(sums, columns + c, aw)

    add_sums(sums, dots_in, dots, dot_at * columns)


def krylov(mu):
    sound = []

    def apply(p):
        out = [SHIFT * v for v in p] + [jnp.zeros_like(mu[0])]
        for i, v in enumerate(p):
            out[i + 1] = out[i + 1] + v
        return out

    def inner(a, b):
        total, size = 0.0, 0.0
        for m in range(len(a) + len(b) - 1):
            terms = [a[i] * b[m - i] for i in range(len(a)) if 0 <= m - i < len(b)]
            total = total + sum(terms) * mu[m]
            size = size + sum(jnp.abs(v) for v in terms) * jnp.abs(mu[m])
        sound.append(size <= GROWTH * jnp.abs(total))
        return total

    def plus(a, b, scale):
        out = []
        for i in range(max(len(a), len(b))):
            v = a[i] if i < len(a) else None
            s = scale * b[i] if i < len(b) else None
            out.append(v if s is None else s if v is None else v + s)
        return out

    r = [jnp.ones_like(mu[0])]
    p = r
    x = []
    rz = mu[0]
    for step in range(ITERS):
        image = apply(p)
        alpha = rz / inner(p, image)
        x = plus(x, p, alpha)
        r = plus(r, image, -alpha)
        if step + 1 < ITERS:
            new = inner(r, r)
            p = plus(r, p, new / rz)
            rz = new
    return x, r, functools.reduce(jnp.logical_and, sound)


def finish(columns, group, dims, *refs):
    refs = list(refs)
    dots = refs.pop(0)
    us = [refs.pop(0) for _ in range(ITERS + 1)]
    ws = [refs.pop(0) for _ in range(ITERS)]
    weight, winv, x_far, r_far, trouble, x_out, r_out, factors, sems = refs
    margin, own, half = dims
    height, angles = 2 * own, 2 * half
    radial = us[0].shape[-1]
    total = jnp.sum(dots[...], axis=0, keepdims=True)
    spread = factors.shape[1], radial
    lane = lax.broadcasted_iota(jnp.int32, spread, 1)
    item = lax.broadcasted_iota(jnp.int32, spread, 0)
    mu = [
        jnp.broadcast_to(jnp.sum(jnp.where(lane == m * columns + item, total, 0.0), axis=1, keepdims=True), spread)
        for m in range(2 * ITERS)
    ]
    xs, rs, sound = krylov(mu)
    trouble[...] = jnp.max(jnp.where(sound | (item >= columns), 0.0, 1.0), axis=0, keepdims=True)
    for j, v in enumerate(xs + rs):
        factors[j] = v

    copies = lambda c, n: [
        pltpu.make_async_copy(near.at[pl.ds(c, n)], far.at[pl.ds(c, n)], sems.at[i])
        for i, (near, far) in enumerate(((x_out, x_far), (r_out, r_far)))
    ]

    @pl.loop(0, columns // group)
    def _(i):
        for n in range(group):
            c = group * i + n
            full = [jnp.broadcast_to(factors[j, pl.ds(c, 1), :], (half, radial)) for j in range(2 * ITERS + 1)]
            xc, rc = full[:ITERS], full[ITERS:]
            for h in range(height):
                for p in range(2):
                    line = pl.ds(h * angles + p * half, half)
                    rows = pl.ds(p * height + h, half, stride=2 * height)
                    x_out[c, rows, :] = winv[line, :] * sum(k * w[c, line, :] for k, w in zip(xc, ws))
                    r_out[c, rows, :] = weight[line, :] * sum(k * u[c, line, :] for k, u in zip(rc, us))
        for copy in copies(group * i, group):
            copy.start()

    for copy in copies(0, columns):
        copy.wait()


def pairs(count, odd, periodic):
    found = []
    for i in range(odd, count, 2):
        j = i + 1
        if j < count or periodic:
            found += [(i, j % count), (j % count, i)]
    return found


def padded_2(block, sides, width, periodic):
    for axis, dim in sides:
        count = lax.axis_size(axis)
        forward = [(i, i + 1) for i in range(count - 1)]
        if periodic:
            forward.append((count - 1, 0))
        backward = [(target, source) for source, target in forward]
        low = lax.ppermute(
            lax.slice_in_dim(block, block.shape[dim] - width, None, axis=dim), axis, forward
        )
        high = lax.ppermute(lax.slice_in_dim(block, 0, width, axis=dim), axis, backward)
        block = jnp.concatenate([low, block, high], axis=dim)
    return block


def zero_pair(v, axis):
    widths = [(0, 0)] * v.ndim
    widths[axis] = (1, 1)
    padded = jnp.pad(v, widths)
    size = v.shape[axis]
    return lax.slice_in_dim(padded, 2, size + 2, axis=axis) + lax.slice_in_dim(
        padded, 0, size, axis=axis
    )


def fine_apply(u, weight, spring):
    v = weight * u
    beside_all = padded_2(v, (("ang", 2),), 1, True)
    above = padded_2(v, (("hgt", 3),), 1, False)
    beside = beside_all[:, :, 2:] + beside_all[:, :, :-2] + above[:, :, :, 2:] + above[:, :, :, :-2]
    beside = beside + zero_pair(v, 4)
    return weight * (SIGMA * v - beside) + SPRING * spring * u


def padded_apply(u, weight, spring):
    v = weight * u
    beside = zero_pair(v, 2) + zero_pair(v, 3) + zero_pair(v, 4)
    return weight * (SIGMA * v - beside) + SPRING * spring * u


def coarsen(field):
    a, h, r = field.shape
    return field.reshape(a // 2, 2, h // 2, 2, r).mean(axis=(1, 3))


def restrict(r):
    c, k, a, h, n = r.shape
    return r.reshape(c, k, a // 2, 2, h // 2, 2, n).sum(axis=(3, 5)) * 0.5


def prolong(e):
    return jnp.repeat(jnp.repeat(e, 2, axis=2), 2, axis=3) * 0.5


def step_by_step(loads, material, support, modulus, positions):
    cases, comps, a_dev, h_dev, radial = loads.shape
    margin = CSWEEPS - 1
    levels = lax.iota(jnp.int32, modulus.shape[0])
    stiff = jnp.sum(
        jnp.where(material[None] == levels[:, None, None, None], modulus[:, None, None, None], 0.0),
        axis=0,
    )
    weight = jnp.sqrt(stiff)
    spring = support.astype(jnp.float32)
    diag = SIGMA * weight * weight + SPRING * spring
    wide_c = coarsen(weight)
    spring_c = coarsen(spring)
    coef = jnp.stack((wide_c, spring_c))
    coef = padded_2(coef, (("ang", 1),), margin, True)
    coef = padded_2(coef, (("hgt", 2),), margin, False)
    wide_p = coef[0]
    spring_p = coef[1]
    diag_raw = SIGMA * wide_p * wide_p + SPRING * spring_p
    diag_p = jnp.where(diag_raw > 0.0, diag_raw, 1.0)
    total_angles = a_dev * lax.axis_size("ang")
    angles = lax.axis_index("ang") * a_dev + lax.iota(jnp.int32, a_dev)
    apart = jnp.abs(angles[None, :] - positions[:, None])
    cycle_dist = jnp.minimum(apart, total_angles - apart)
    hit = jnp.where(cycle_dist < a_dev, -LOAD, 0.0)
    select = jnp.where(lax.iota(jnp.int32, comps) == 2, 1.0, 0.0)
    right = loads + hit[:, None, :, None, None] * select[None, :, None, None, None]

    def precondition(r):
        coarse_rhs = restrict(r)
        wider = padded_2(coarse_rhs, (("ang", 2),), margin, True)
        wider = padded_2(wider, (("hgt", 3),), margin, False)
        err = OMEGA * wider / diag_p
        for sweep in range(CSWEEPS - 1):
            err = err + OMEGA * (wider - padded_apply(err, wide_p, spring_p)) / diag_p
        err = err[:, :, margin : err.shape[2] - margin, margin : err.shape[3] - margin]
        return OMEGA * r / diag + prolong(err)

    def projection(a, b):
        return lax.psum(jnp.sum(a * b, axis=(2, 3, 4)), ("ang", "hgt"))[:, :, None, None, None]

    solution_field = jnp.zeros_like(right)
    residual = right
    precond = precondition(residual)
    direction = precond
    rz_now = projection(residual, precond)
    for step in range(ITERS):
        image = fine_apply(direction, weight, spring)
        curve = lax.psum(jnp.sum(direction * image, axis=(2, 3, 4)), ("ang", "hgt"))
        alpha = rz_now / curve[:, :, None, None, None]
        solution_field = solution_field + alpha * direction
        residual = residual - alpha * image
        if step + 1 < ITERS:
            precond = precondition(residual)
            rz_next = projection(residual, precond)
            direction = precond + rz_next / rz_now * direction
            rz_now = rz_next
    return (solution_field, residual)


def swap(messages, axis, periodic, first=0):
    got = [None, None]
    for i in (first, 1 - first):
        got[i] = lax.ppermute(messages[i], axis, pairs(lax.axis_size(axis), i, periodic))
    return got


def body(loads, material, support, modulus, positions):
    cases, comps, angles, height, radial = loads.shape
    columns = cases * comps
    margin = CSWEEPS
    group = 6
    own, half = height // 2, angles // 2
    dims = (margin, own, half)
    n_ang, n_hgt = lax.axis_size("ang"), lax.axis_size("hgt")
    assert own >= margin and half >= margin and half % 8 == 0 and n_ang % 2 == 0
    assert 2 * ITERS * columns <= radial and columns % group == 0 and columns % 3 == 0 and group % 2 == 0
    assert (columns // 3) % 2 == 0
    cells = height * angles
    field, coef = f32(columns, cells, radial), f32(cells, radial)
    rows_h, rows_a = (margin - 1) * half + angles, 2 * side_rows(dims)
    rows_c = corner_rows(margin)[1]
    vm = lambda *s: pltpu.VMEM(s, jnp.float32)
    message = lambda n: (
        [f32(n, own * half, radial)] + [f32(n, rows_h, radial)] * 2 + [f32((n + 1) // 2, rows_a, radial)] * 2
    )
    ends = f32(2, 2, own, radial)

    out = list(call(
        functools.partial(prepare, cases, comps, modulus.shape[0], n_ang, dims),
        [field] + message(columns + 1) + [coef] * 5
        + [f32(own, half, radial), ends, f32(2, angles, radial), ends],
        loads.reshape(columns, cells, radial), material.reshape(cells, radial), support.reshape(cells, radial),
        modulus, positions,
        hbm=range(5),
        scratch=[
            vm(columns, cells, radial), pltpu.VMEM((cells, radial), jnp.int32), pltpu.VMEM((cells, radial), jnp.int32),
            pltpu.SMEM(modulus.shape, jnp.float32), pltpu.SMEM(positions.shape, jnp.int32),
            pltpu.SemaphoreType.DMA((7,)), vm(2, own * half, radial),
        ],
    ))
    u, sent, msg, side = out[0], out[1], out[2:4], out[4:6]
    delta, q, beta, weight, winv, pre, q_ends, fold, fold_ends = out[6:]
    us, ws = [u], []
    dots = jnp.zeros((n_ang * n_hgt, radial), jnp.float32)
    shared = []
    for step in range(ITERS):
        first, last = step == 0, step + 1 == ITERS
        count = columns + 1 if first else columns
        slabs = (count + 1) // 2
        far = swap(msg, "hgt", False)
        beside = swap(side, "ang", True, first=1)
        corner = call(
            functools.partial(corner_messages, dims, count), [f32(slabs, 2 * rows_c, radial)] * 2, *beside[::-1],
        )
        corner = swap(corner, "hgt", False)
        args = [us[-1], sent, *far, *beside[::-1], *corner, *([dots] if last else []), delta, q, beta, weight, pre, q_ends, fold, fold_ends, *shared]
        outs = [field, field]
        ext_h, ext_a = own + 2 * margin, half + 2 * margin
        if first:
            outs += [f32(ext_h, ext_a, radial), f32(2, angles, radial), f32(2, 2, own, radial)]
        if not last:
            outs += message(columns)
        else:
            outs.append(f32(n_ang * n_hgt, radial))
        block = vm(group, ext_h * (ext_a + 2 * PAD), radial)
        out = list(call(
            functools.partial(apply_step, dims, columns, group, first, last, 2 * step),
            outs, *args,
            scratch=[
                block, block, block, vm(group, (height + 2) * 3 * half, radial),
                vm(group, 2, angles, radial), vm(2 * columns * 8, radial), vm(group, own * half, radial),
            ],
        ))
        ws.append(out.pop(0))
        us.append(out.pop(0))
        if first:
            shared, out = out[:3], out[3:]
        if not last:
            sent, msg, side, out = out[0], out[1:3], out[3:5], out[5:]
        if last:
            dots = out.pop(0)
        else:
            dots, = call(
                functools.partial(two_sums, columns, 2 * step), [f32(n_ang * n_hgt, radial)],
                us[-2], ws[-1], us[-1], dots,
                scratch=[vm(2 * columns * 8, radial)],
                cost=None,
            )

    dots = lax.all_to_all(dots, ("ang", "hgt"), 0, 0, tiled=True)
    x, r, trouble = call(
        functools.partial(finish, columns, 2, dims), [field] * 2 + [f32(1, radial)], dots, *us, *ws, weight, winv,
        hbm_out=(0, 1),
        scratch=[
            vm(columns, cells, radial), vm(columns, cells, radial),
            vm(2 * ITERS + 1, -(-columns // 8) * 8, radial),
            pltpu.SemaphoreType.DMA((2,)),
        ],
    )
    x, r = x.reshape(loads.shape), r.reshape(loads.shape)

    def again(state):
        given = [jnp.where(state[0], v, jnp.zeros_like(v)) for v in (loads, material, support, modulus, positions)]
        return jnp.zeros_like(state[0]), *step_by_step(*given)

    return lax.while_loop(lambda state: state[0], again, (trouble[0, 0] > 0.0, x, r))[1:]


def solution(mesh):
    in_specs = (
        P(None, None, "ang", "hgt", None),
        P("ang", "hgt", None),
        P("ang", "hgt", None),
        P(),
        P(),
    )
    out_specs = (P(None, None, "ang", "hgt", None), P(None, None, "ang", "hgt", None))
    return jax.shard_map(body, mesh=mesh, in_specs=in_specs, out_specs=out_specs, check_vma=False)
```
